256 devices in a mesh: dp: 32 (over x, z_hi, core), space: 8 (over y, z_lo).
Axes of the slice: x: 4, y: 4, z: 8 (z_hi: 4, z_lo: 2; z = z_hi * 2 + z_lo), core: 2. Of those that a mesh axis runs over, the one named last changes fastest.
Arguments:
- block_input: bfloat16 [32, 56, 56, 768], P('dp', 'space'), may hold values from -8 to 8
- hidden_map: bfloat16 [32, 56, 56, 1536], P('dp', 'space'), may hold values from -6 to 6
- cotangent: bfloat16 [32, 56, 56, 768], P('dp', 'space'), may hold values from -16 to 16
- depth_weight: bfloat16 [9, 1536], replicated, may hold values from -2 to 2
- proj_weight: bfloat16 [1536, 768], replicated, may hold values from -0.15625 to 0.15625
- norm_gain: float32 [768], replicated, may hold values from 0.5 to 1.5
- qkv_weight: bfloat16 [768, 2304], replicated, may hold values from -10 to 10
- out_weight: bfloat16 [768, 768], replicated, may hold values from -0.21875 to 0.21875
Outputs:
- block_output: bfloat16 [32, 56, 56, 768], P('dp', 'space')
- input_grad: bfloat16 [32, 56, 56, 768], P('dp', 'space')
- hidden_grad: bfloat16 [32, 56, 56, 1536], P('dp', 'space')
- depth_grad: float32 [9, 1536], replicated
- gain_grad: float32 [768], replicated
- proj_grad: float32 [1536, 768], P('dp', 'space')
- qkv_grad: float32 [768, 2304], P('dp', 'space')
- out_grad: float32 [768, 768], P('dp', 'space')
The draws below stay inside these ranges and needn't reach their ends.
All inputs are finite; a program needn't handle non-finite values.
Results may differ from the reference program's by a relative error of at most 0.025.
Values may be sent and summed in bfloat16 or wider, within the bound.
A program may use at most 128 MiB of HBM per device.

```python
import jax
import jax.numpy as jnp
from jax import lax

C = 768
HEADS = 24
HD = 32
E = 1536
G = 7
W = 56
IMAGES = 32
H = 56


def draw_block_input(key, part):
    key = jax.random.fold_in(key, 11)
    noise_key = jax.random.fold_in(key, 0)
    noise_part = jax.random.normal(noise_key, (IMAGES, H, W, C), jnp.float32)
    return jnp.clip(noise_part, -8.0, 8.0).astype(jnp.bfloat16)


def draw_qkv_weight(key, part):
    key = jax.random.fold_in(key, 23)
    query_key, keys_key, value_key = jax.random.split(key, 3)
    weight_scale = C ** (-0.5)
    query_part = jax.random.normal(query_key, (C, C), jnp.float32) * weight_scale
    keys_part = jax.random.normal(keys_key, (C, C), jnp.float32) * weight_scale
    value_part = jax.random.normal(value_key, (C, C), jnp.float32) * weight_scale
    combined = jnp.concatenate([query_part, keys_part, value_part], axis=1)
    return jnp.clip(combined, -10.0, 10.0).astype(jnp.bfloat16)


def draw_cotangent(key, part):
    key = jax.random.fold_in(key, 37)
    noise_key = jax.random.fold_in(key, 0)
    noise_part = jax.random.normal(noise_key, (IMAGES, H, W, C), jnp.float32)
    return jnp.clip(noise_part, -16.0, 16.0).astype(jnp.bfloat16)


def shard_levels(own_key, shape, cuts, smallest, largest):
    gain = 1.0
    for position, parts in cuts:
        steps = jax.random.uniform(jax.random.fold_in(jax.random.fold_in(own_key, 6), position), (parts,), jnp.float32, smallest / len(cuts), largest / len(cuts))
        gain = gain * jnp.repeat(jnp.exp(steps), shape[position] // parts).reshape((-1,) + (1,) * (len(shape) - 1 - position))
    return gain


def noise(own_key, shape, spread, reach, cuts=(), held_as=jnp.bfloat16):
    level = shard_levels(own_key, shape, cuts, -0.22, 0.18) if cuts else 1.0
    array = jax.random.normal(own_key, shape, jnp.float32) * spread * level
    return jnp.minimum(jnp.maximum(array, -reach), reach).astype(held_as)


def setup_inputs(seed: int = 0) -> dict:
    key_list = jax.random.split(jax.random.key(seed), 9)
    block_input = draw_block_input(jax.random.fold_in(key_list[8], 71), 0)
    hidden_map = noise(key_list[1], (IMAGES, H, W, E), 1.0, 6.0, ((0, 32), (1, 8)))
    cotangent = draw_cotangent(jax.random.fold_in(key_list[8], 71), 0)
    depth_weight = noise(key_list[3], (9, E), 9 ** -0.5, 2.0)
    proj_weight = noise(key_list[4], (E, C), E ** -0.5, 0.15625)
    norm_gain = jnp.clip(1.0 + 0.1 * jax.random.normal(key_list[5], (C,), jnp.float32), 0.5, 1.5)
    qkv_weight = draw_qkv_weight(jax.random.fold_in(key_list[8], 71), 0)
    out_weight = noise(key_list[7], (C, C), C ** -0.5, 0.21875)
    return dict(block_input=block_input, hidden_map=hidden_map, cotangent=cotangent, depth_weight=depth_weight, proj_weight=proj_weight, norm_gain=norm_gain, qkv_weight=qkv_weight, out_weight=out_weight)


EPS = 1e-05

def rounded(value):
    return lax.optimization_barrier(value.astype(jnp.bfloat16))

def conv_forward(padded, depth_weight, map_rows, map_cols):
    summed = None
    for tap_index in range(9):
        tap_row, tap_col = (tap_index // 3, tap_index % 3)
        shifted_piece = padded[..., tap_row:tap_row + map_rows, tap_col:tap_col + map_cols, :].astype(jnp.float32)
        term = shifted_piece * depth_weight[tap_index].astype(jnp.float32)
        summed = term if summed is None else summed + term
    return summed

def conv_backward(padded, depth_weight, map_rows, map_cols):
    summed = None
    for tap_index in range(9):
        tap_row, tap_col = (2 - tap_index // 3, 2 - tap_index % 3)
        shifted_piece = padded[..., tap_row:tap_row + map_rows, tap_col:tap_col + map_cols, :].astype(jnp.float32)
        term = shifted_piece * depth_weight[tap_index].astype(jnp.float32)
        summed = term if summed is None else summed + term
    return summed

def depth_sum(padded, grad_conv, map_rows, map_cols):
    grad_wide = grad_conv.astype(jnp.float32)
    lead_axes = tuple(range(grad_conv.ndim - 1))
    tap_sums = []
    for tap_index in range(9):
        tap_row, tap_col = (tap_index // 3, tap_index % 3)
        shifted_piece = padded[..., tap_row:tap_row + map_rows, tap_col:tap_col + map_cols, :].astype(jnp.float32)
        tap_sums.append(lax.optimization_barrier(jnp.sum(shifted_piece * grad_wide, axis=lead_axes)))
    return jnp.stack(tap_sums)

def norm_forward(mid_stream, norm_gain):
    token_mean = lax.optimization_barrier(jnp.mean(mid_stream, axis=-1, keepdims=True))
    centred = mid_stream - token_mean
    variance = lax.optimization_barrier(jnp.mean(centred * centred, axis=-1, keepdims=True))
    inv_std = lax.rsqrt(variance + EPS)
    normal_hat = centred * inv_std
    normed = (normal_hat * norm_gain).astype(jnp.bfloat16)
    return (normal_hat, inv_std, normed)

def to_windows(grid_map):
    map_rows, map_cols, features = grid_map.shape
    pieces = grid_map.reshape(G, map_rows // G, G, map_cols // G, features)
    pieces = pieces.transpose(1, 3, 0, 2, 4)
    return pieces.reshape(-1, G * G, features)

def from_windows(windowed, map_rows, map_cols):
    features = windowed.shape[-1]
    pieces = windowed.reshape(map_rows // G, map_cols // G, G, G, features)
    pieces = pieces.transpose(2, 0, 3, 1, 4)
    return pieces.reshape(map_rows, map_cols, features)

def attend_forward(queries, key_rows, values):
    score_scale = HD ** (-0.5)
    scores = jnp.einsum('nqhd,nkhd->nhqk', queries.astype(jnp.float32), key_rows.astype(jnp.float32)) * score_scale
    shifted = scores - lax.optimization_barrier(jnp.max(scores, axis=-1, keepdims=True))
    exponent = jnp.exp(shifted)
    weights = exponent / lax.optimization_barrier(jnp.sum(exponent, axis=-1, keepdims=True))
    weights_low = rounded(weights)
    attended = jnp.einsum('nhqk,nkhd->nqhd', weights_low.astype(jnp.float32), values.astype(jnp.float32))
    return (attended.astype(jnp.bfloat16), weights, weights_low)

def attend_backward(queries, key_rows, values, weights, weights_low, grad_att):
    score_scale = HD ** (-0.5)
    grad_weights = jnp.einsum('nqhd,nkhd->nhqk', grad_att.astype(jnp.float32), values.astype(jnp.float32))
    grad_values = jnp.einsum('nhqk,nqhd->nkhd', weights_low.astype(jnp.float32), grad_att.astype(jnp.float32))
    centred = grad_weights - lax.optimization_barrier(jnp.sum(grad_weights * weights, axis=-1, keepdims=True))
    grad_low = rounded(weights * centred * score_scale)
    grad_queries = jnp.einsum('nhqk,nkhd->nqhd', grad_low.astype(jnp.float32), key_rows.astype(jnp.float32))
    grad_keys = jnp.einsum('nhqk,nqhd->nkhd', grad_low.astype(jnp.float32), queries.astype(jnp.float32))
    return (grad_queries.astype(jnp.bfloat16), grad_keys.astype(jnp.bfloat16), grad_values.astype(jnp.bfloat16))

def image_pass(slices, depth_weight, proj_weight, norm_gain, qkv_weight, out_weight):
    block_input, hidden_map, cotangent = slices
    map_rows, map_cols, hidden_units = hidden_map.shape
    channels = block_input.shape[-1]
    token_count = map_rows * map_cols
    hidden_pad = jnp.pad(hidden_map, ((1, 1), (1, 1), (0, 0)))
    conv_out = conv_forward(hidden_pad, depth_weight, map_rows, map_cols)
    act_low = rounded(jax.nn.gelu(conv_out)).reshape(token_count, hidden_units)
    mid_stream = block_input.reshape(token_count, channels).astype(jnp.float32) + jnp.dot(act_low, proj_weight, preferred_element_type=jnp.float32)
    normal_hat, inv_std, normed = norm_forward(mid_stream, norm_gain)
    qkv_low = rounded(jnp.dot(normed, qkv_weight, preferred_element_type=jnp.float32))
    qkv_win = to_windows(qkv_low.reshape(map_rows, map_cols, 3 * channels))
    window_count = qkv_win.shape[0]
    qkv_win = qkv_win.reshape(window_count, G * G, 3, HEADS, HD)
    queries, key_rows, values = (qkv_win[:, :, 0], qkv_win[:, :, 1], qkv_win[:, :, 2])
    attended, weights, weights_low = attend_forward(queries, key_rows, values)
    att_tok = from_windows(attended.reshape(window_count, G * G, channels), map_rows, map_cols).reshape(token_count, channels)
    output_full = mid_stream + jnp.dot(att_tok, out_weight, preferred_element_type=jnp.float32)
    block_output = output_full.astype(jnp.bfloat16).reshape(map_rows, map_cols, channels)
    cot_tok = cotangent.reshape(token_count, channels)
    out_part = jnp.dot(att_tok.T, cot_tok, preferred_element_type=jnp.float32)
    grad_att = rounded(jnp.dot(cot_tok, out_weight.T, preferred_element_type=jnp.float32))
    grad_win = to_windows(grad_att.reshape(map_rows, map_cols, channels)).reshape(window_count, G * G, HEADS, HD)
    grad_queries, grad_keys, grad_values = attend_backward(queries, key_rows, values, weights, weights_low, grad_win)
    grad_stack = jnp.stack([grad_queries, grad_keys, grad_values], axis=2).reshape(window_count, G * G, 3 * channels)
    grad_qkv = from_windows(grad_stack, map_rows, map_cols).reshape(token_count, 3 * channels)
    qkv_part = jnp.dot(normed.T, grad_qkv, preferred_element_type=jnp.float32)
    grad_wide = rounded(jnp.dot(grad_qkv, qkv_weight.T, preferred_element_type=jnp.float32)).astype(jnp.float32)
    grad_hat = grad_wide * norm_gain
    gain_part = lax.optimization_barrier(jnp.sum(grad_wide * normal_hat, axis=0))
    grad_mid = cot_tok.astype(jnp.float32) + inv_std * (grad_hat - lax.optimization_barrier(jnp.mean(grad_hat, axis=-1, keepdims=True)) - normal_hat * lax.optimization_barrier(jnp.mean(grad_hat * normal_hat, axis=-1, keepdims=True)))
    input_grad = grad_mid.astype(jnp.bfloat16)
    proj_part = jnp.dot(act_low.T, input_grad, preferred_element_type=jnp.float32)
    grad_act = jnp.dot(input_grad, proj_weight.T, preferred_element_type=jnp.float32).reshape(map_rows, map_cols, hidden_units)
    grad_conv = rounded(jax.vjp(jax.nn.gelu, conv_out)[1](grad_act)[0])
    grad_pad = jnp.pad(grad_conv, ((1, 1), (1, 1), (0, 0)))
    hidden_grad = conv_backward(grad_pad, depth_weight, map_rows, map_cols).astype(jnp.bfloat16)
    depth_part = depth_sum(hidden_pad, grad_conv, map_rows, map_cols)
    image_outs = (block_output, input_grad.reshape(map_rows, map_cols, channels), hidden_grad)
    return (image_outs, (depth_part, gain_part, proj_part, qkv_part, out_part))

def reference(block_input, hidden_map, cotangent, depth_weight, proj_weight, norm_gain, qkv_weight, out_weight):
    channels = block_input.shape[-1]
    hidden_units = hidden_map.shape[-1]
    start_sums = (jnp.zeros((9, hidden_units), jnp.float32), jnp.zeros((channels,), jnp.float32), jnp.zeros((hidden_units, channels), jnp.float32), jnp.zeros((channels, 3 * channels), jnp.float32), jnp.zeros((channels, channels), jnp.float32))

    def image_step(running, slices):
        image_outs, grad_parts = image_pass(slices, depth_weight, proj_weight, norm_gain, qkv_weight, out_weight)
        return (jax.tree.map(jnp.add, running, grad_parts), image_outs)
    totals, stacked = lax.scan(image_step, start_sums, (block_input, hidden_map, cotangent))
    block_output, input_grad, hidden_grad = stacked
    depth_grad, gain_grad, proj_grad, qkv_grad, out_grad = totals
    return (block_output, input_grad, hidden_grad, depth_grad, gain_grad, proj_grad, qkv_grad, out_grad)
```

```python
import jax
import jax.numpy as jnp
from jax import lax
from jax.experimental import pallas as pl
from jax.experimental.pallas import tpu as pltpu
from jax.sharding import PartitionSpec as P

HEADS = 24
HD = 32
G = 7


EPS = 1e-05


def extended(shard, sides, width):
    for axis, dim in sides:
        peers, length = (lax.axis_size(axis), shard.shape[dim])
        up = [(i, (i + 1) % peers) for i in range(peers - 1)]
        down = [(j, i) for i, j in up]
        last = lax.slice_in_dim(shard, length - width, length, axis=dim)
        initial = lax.slice_in_dim(shard, 0, width, axis=dim)
        before = lax.ppermute(last, axis, up)
        after = lax.ppermute(initial, axis, down)
        shard = jnp.concatenate([before, shard, after], axis=dim)
    return shard


def conv_forward(padded, depth_weight, map_rows, map_cols):
    summed = None
    for tap_index in range(9):
        tap_row, tap_col = (tap_index // 3, tap_index % 3)
        shifted_piece = padded[
            ..., tap_row : tap_row + map_rows, tap_col : tap_col + map_cols, :
        ].astype(jnp.float32)
        term = shifted_piece * depth_weight[tap_index].astype(jnp.float32)
        summed = term if summed is None else summed + term
    return summed


def conv_backward(padded, depth_weight, map_rows, map_cols):
    summed = None
    for tap_index in range(9):
        tap_row, tap_col = (2 - tap_index // 3, 2 - tap_index % 3)
        shifted_piece = padded[
            ..., tap_row : tap_row + map_rows, tap_col : tap_col + map_cols, :
        ].astype(jnp.float32)
        term = shifted_piece * depth_weight[tap_index].astype(jnp.float32)
        summed = term if summed is None else summed + term
    return summed


def depth_sum(padded, grad_conv, map_rows, map_cols):
    grad_wide = grad_conv.astype(jnp.float32)
    lead_axes = tuple(range(grad_conv.ndim - 1))
    tap_sums = []
    for tap_index in range(9):
        tap_row, tap_col = (tap_index // 3, tap_index % 3)
        shifted_piece = padded[
            ..., tap_row : tap_row + map_rows, tap_col : tap_col + map_cols, :
        ].astype(jnp.float32)
        tap_sums.append(jnp.sum(shifted_piece * grad_wide, axis=lead_axes))
    return jnp.stack(tap_sums)


def norm_forward(mid_stream, norm_gain):
    token_mean = jnp.mean(mid_stream, axis=-1, keepdims=True)
    centred = mid_stream - token_mean
    variance = jnp.mean(centred * centred, axis=-1, keepdims=True)
    inv_std = lax.rsqrt(variance + EPS)
    normal_hat = centred * inv_std
    normed = (normal_hat * norm_gain).astype(jnp.bfloat16)
    return (normal_hat, inv_std, normed)


def to_windows(grid_part, row_step):
    images, all_rows, columns, local_step, features = grid_part.shape
    pieces = grid_part.reshape(images, G, row_step, G, local_step, features)
    pieces = pieces.transpose(0, 2, 4, 1, 3, 5)
    return pieces.reshape(images * row_step * local_step, G * G, features)


def from_windows(windowed, images, row_step, local_step):
    features = windowed.shape[-1]
    pieces = windowed.reshape(images, row_step, local_step, G, G, features)
    pieces = pieces.transpose(0, 3, 1, 4, 2, 5)
    return pieces.reshape(images, G * row_step, G, local_step, features)


def attend_forward(queries, key_rows, values):
    score_scale = HD ** (-0.5)
    scores = (
        jnp.einsum("nqhd,nkhd->nhqk", queries, key_rows, preferred_element_type=jnp.float32)
        * score_scale
    )
    shifted = scores - jnp.max(scores, axis=-1, keepdims=True)
    exponent = jnp.exp(shifted)
    weights = exponent / jnp.sum(exponent, axis=-1, keepdims=True)
    weights_low = weights.astype(jnp.bfloat16)
    attended = jnp.einsum(
        "nhqk,nkhd->nqhd", weights_low, values, preferred_element_type=jnp.float32
    )
    return (attended.astype(jnp.bfloat16), weights, weights_low)


def attend_backward(queries, key_rows, values, weights, weights_low, grad_att):
    score_scale = HD ** (-0.5)
    grad_weights = jnp.einsum(
        "nqhd,nkhd->nhqk", grad_att, values, preferred_element_type=jnp.float32
    )
    grad_values = jnp.einsum(
        "nhqk,nqhd->nkhd", weights_low, grad_att, preferred_element_type=jnp.float32
    )
    centred = grad_weights - jnp.sum(grad_weights * weights, axis=-1, keepdims=True)
    grad_low = (weights * centred * score_scale).astype(jnp.bfloat16)
    grad_queries = jnp.einsum(
        "nhqk,nkhd->nqhd", grad_low, key_rows, preferred_element_type=jnp.float32
    )
    grad_keys = jnp.einsum("nhqk,nqhd->nkhd", grad_low, queries, preferred_element_type=jnp.float32)
    return (
        grad_queries.astype(jnp.bfloat16),
        grad_keys.astype(jnp.bfloat16),
        grad_values.astype(jnp.bfloat16),
    )


MESH = pl.DeviceIdType.MESH
F32, BF16 = jnp.float32, jnp.bfloat16


def place():
    dp, sp = lax.axis_index("dp"), lax.axis_index("space")
    return lax.div(dp, 8), lax.rem(lax.div(dp, 2), 4), lax.rem(dp, 2), sp


def dp_of(x, zh, core):
    return (x * 4 + zh) * 2 + core


def sum_partners(x, zh, core, sp):
    dp = dp_of(x, zh, core)
    ids = [(dp_of(x, zh, 1 - core), sp)]
    ids += [(dp_of(lax.rem(x + j, 4), zh, core), sp) for j in (1, 2, 3)]
    ids += [(dp_of(x, lax.rem(zh + j, 4), core), sp) for j in (1, 2, 3)]
    ids += [(dp, lax.rem(sp + j, 8)) for j in range(1, 8)]
    return ids


def greet(ids):
    barrier = pltpu.get_barrier_semaphore()
    for one in ids:
        pl.semaphore_signal(barrier, inc=1, device_id=one, device_id_type=MESH)
    pl.semaphore_wait(barrier, len(ids))


def remote(src, dst, send, recv, to):
    return pltpu.make_async_remote_copy(
        src_ref=src, dst_ref=dst, send_sem=send, recv_sem=recv, device_id=to, device_id_type=MESH
    )


def sum_kernel(
    grads, small, proj_o, qkv_o, out_o, small_o,
    r0, s0, r1, s1, r2, tiles, r3, sacc, sr,
    s0s, s0r, s1s, s1r, s2s, s2r, s3s, s3r, sms, smr,
):
    x, zh, core, sp = place()
    ids = sum_partners(x, zh, core, sp)
    greet(ids)
    pair, xs, zs, sps = ids[0], ids[1:4], ids[4:7], ids[7:14]
    order = (1, 3, 2, 0)
    first = []
    for j in order:
        xx = lax.rem(x + j, 4)
        cp = remote(grads.at[xx, :, 1 - core], r0.at[xx], s0s.at[j], s0r.at[j], pair)
        cp.start()
        first.append(cp)

    def small_stage(src, dst, base, peers):
        cps = []
        for n, peer in enumerate(peers):
            cp = remote(src, sr.at[base + n], sms.at[base + n], smr.at[base + n], peer)
            cp.start()
            cps.append(cp)
        return cps

    def small_sum(cps, src, dst, base):
        for cp in cps:
            cp.wait()
        total = src[...]
        for n in range(len(cps)):
            total = total + sr[base + n]
        dst[...] = total

    c0 = small_stage(small, sacc.at[0], 0, [pair])
    second = []
    for n, j in enumerate(order):
        xx = lax.rem(x + j, 4)
        first[n].wait_recv()

        def body(i, carry, xx=xx):
            s0[xx, i] = (grads[xx, i, core].astype(F32) + r0[xx, i].astype(F32)).astype(BF16)
            return carry

        lax.fori_loop(0, 4, body, 0)
        if j:
            cp = remote(s0.at[xx], r1.at[j - 1], s1s.at[j - 1], s1r.at[j - 1], xs[j - 1])
            cp.start()
            second.append(cp)
    small_sum(c0, small, sacc.at[0], 0)
    c1 = small_stage(sacc.at[0], None, 1, xs)
    for cp in second:
        cp.wait_recv()
    third = []
    for j in order:
        zz = lax.rem(zh + j, 4)
        total = s0[x, zz].astype(F32)
        for n in range(3):
            total = total + r1[n, zz].astype(F32)
        s1[zz] = total.astype(BF16)
        if j:
            cp = remote(s1.at[zz], r2.at[j - 1], s2s.at[j - 1], s2r.at[j - 1], zs[j - 1])
            cp.start()
            third.append(cp)
    small_sum(c1, sacc.at[0], sacc.at[1], 1)
    c2 = small_stage(sacc.at[1], None, 4, zs)
    for cp in third:
        cp.wait_recv()
    total = s1[zh].astype(F32)
    for n in range(3):
        total = total + r2[n].astype(F32)
    for j in range(8):
        half, col = j // 4, j % 4
        qkv = total[24 * half : 24 * half + 24, 768 + 288 * col : 768 + 288 * col + 288]
        out = total[24 * half : 24 * half + 24, 1920 + 96 * col : 1920 + 96 * col + 96]
        tiles[j, :, 0:96] = total[:, 96 * j : 96 * j + 96].astype(BF16)
        tiles[j, :, 128:272] = jnp.concatenate([qkv[:, :144], qkv[:, 144:]], axis=0).astype(BF16)
        tiles[j, :, 272:320] = jnp.concatenate([out[:, :48], out[:, 48:]], axis=0).astype(BF16)
    fourth = []
    for j in range(1, 8):
        to = lax.rem(sp + j, 8)
        cp = remote(tiles.at[to], r3.at[j - 1], s3s.at[j - 1], s3r.at[j - 1], sps[j - 1])
        cp.start()
        fourth.append(cp)
    small_sum(c2, sacc.at[1], sacc.at[2], 4)
    c3 = small_stage(sacc.at[2], None, 7, sps)
    for cp in fourth:
        cp.wait_recv()
    total = tiles[sp].astype(F32)
    for n in range(7):
        total = total + r3[n].astype(F32)
    proj_o[...] = total[:, 0:96]
    qkv_o[:, 0:144] = total[0:24, 128:272]
    qkv_o[:, 144:288] = total[24:48, 128:272]
    out_o[:, 0:48] = total[0:24, 272:320]
    out_o[:, 48:96] = total[24:48, 272:320]
    small_sum(c3, sacc.at[2], small_o, 7)
    for cp in first + second + third + fourth:
        cp.wait_send()


def sum_grads(proj_local, qkv_local, out_local, depth_local, gain_local):
    proj = proj_local.astype(BF16).reshape(32, 48, 768)
    qkv = qkv_local.astype(BF16).reshape(32, 24, 2, 1152).transpose(0, 2, 1, 3).reshape(32, 48, 1152)
    out = out_local.astype(BF16).reshape(32, 24, 2, 384).transpose(0, 2, 1, 3).reshape(32, 48, 384)
    grads = jnp.concatenate([proj, qkv, out], axis=2).reshape(4, 4, 2, 48, 2304)
    tail = jnp.concatenate([depth_local[8], gain_local, jnp.zeros((768,), F32)]).reshape(8, 384)
    small = jnp.concatenate([depth_local[:8], tail], axis=1)
    vm = pl.BlockSpec(memory_space=pltpu.VMEM)
    dma = pltpu.SemaphoreType.DMA
    proj_o, qkv_o, out_o, small_o = pl.pallas_call(
        sum_kernel,
        out_shape=(
            jax.ShapeDtypeStruct((48, 96), F32),
            jax.ShapeDtypeStruct((24, 288), F32),
            jax.ShapeDtypeStruct((24, 96), F32),
            jax.ShapeDtypeStruct((8, 1920), F32),
        ),
        in_specs=[vm, vm],
        out_specs=(vm, vm, vm, vm),
        scratch_shapes=[
            pltpu.VMEM((4, 4, 48, 2304), BF16),
            pltpu.VMEM((4, 4, 48, 2304), BF16),
            pltpu.VMEM((3, 4, 48, 2304), BF16),
            pltpu.VMEM((4, 48, 2304), BF16),
            pltpu.VMEM((3, 48, 2304), BF16),
            pltpu.VMEM((8, 48, 384), BF16),
            pltpu.VMEM((7, 48, 384), BF16),
            pltpu.VMEM((3, 8, 1920), F32),
            pltpu.VMEM((14, 8, 1920), F32),
            dma((4,)), dma((4,)), dma((3,)), dma((3,)), dma((3,)), dma((3,)),
            dma((7,)), dma((7,)), dma((14,)), dma((14,)),
        ],
        compiler_params=pltpu.CompilerParams(
            collective_id=0, has_side_effects=True, vmem_limit_bytes=48 * 1024 * 1024
        ),
        cost_estimate=pl.CostEstimate(flops=10**7, bytes_accessed=10**7, transcendentals=0),
        name="sum_grads",
    )(grads, small)
    tail = small_o[:, 1536:].reshape(-1)
    depth = jnp.concatenate([small_o[:, :1536], tail[None, :1536]], axis=0)
    return depth, tail[1536:2304], proj_o, qkv_o, out_o


def local(
    block_input, hidden_map, cotangent, depth_weight, proj_weight, norm_gain, qkv_weight, out_weight
):
    images, slab_rows, map_cols, hidden_units = hidden_map.shape
    channels = block_input.shape[-1]
    space_count = lax.axis_size("space")
    col_step = map_cols // G
    local_step = col_step // space_count
    row_step = slab_rows * space_count // G
    token_count = images * slab_rows * map_cols
    slab_shape = (images, slab_rows, G, col_step)
    hidden_rows = extended(hidden_map, (("space", 1),), 1)
    hidden_pad = jnp.pad(hidden_rows, ((0, 0), (0, 0), (1, 1), (0, 0)))
    conv_out = conv_forward(hidden_pad, depth_weight, slab_rows, map_cols)
    act_low = jax.nn.gelu(conv_out).astype(jnp.bfloat16).reshape(token_count, hidden_units)
    mid_stream = block_input.reshape(token_count, channels).astype(jnp.float32) + jnp.dot(
        act_low, proj_weight, preferred_element_type=jnp.float32
    )
    normal_hat, inv_std, normed = norm_forward(mid_stream, norm_gain)
    qkv_low = jnp.dot(normed, qkv_weight, preferred_element_type=jnp.float32).astype(jnp.bfloat16)
    qkv_grid = lax.all_to_all(
        qkv_low.reshape(slab_shape + (3 * channels,)),
        "space",
        split_axis=3,
        concat_axis=1,
        tiled=True,
    )
    qkv_win = to_windows(qkv_grid, row_step)
    window_count = qkv_win.shape[0]
    qkv_win = qkv_win.reshape(window_count, G * G, 3, HEADS, HD)
    queries, key_rows, values = (qkv_win[:, :, 0], qkv_win[:, :, 1], qkv_win[:, :, 2])
    attended, weights, weights_low = attend_forward(queries, key_rows, values)
    att_grid = from_windows(
        attended.reshape(window_count, G * G, channels), images, row_step, local_step
    )
    att_slab = lax.all_to_all(att_grid, "space", split_axis=1, concat_axis=3, tiled=True)
    att_tok = att_slab.reshape(token_count, channels)
    output_full = mid_stream + jnp.dot(att_tok, out_weight, preferred_element_type=jnp.float32)
    block_output = output_full.astype(jnp.bfloat16).reshape(images, slab_rows, map_cols, channels)
    cot_tok = cotangent.reshape(token_count, channels)
    out_local = jnp.einsum("tc,td->cd", att_tok, cot_tok, preferred_element_type=jnp.float32)
    grad_att = jnp.dot(cot_tok, out_weight.T, preferred_element_type=jnp.float32).astype(
        jnp.bfloat16
    )
    grad_att_grid = lax.all_to_all(
        grad_att.reshape(slab_shape + (channels,)), "space", split_axis=3, concat_axis=1, tiled=True
    )
    grad_win = to_windows(grad_att_grid, row_step).reshape(window_count, G * G, HEADS, HD)
    grad_queries, grad_keys, grad_values = attend_backward(
        queries, key_rows, values, weights, weights_low, grad_win
    )
    grad_stack = jnp.stack([grad_queries, grad_keys, grad_values], axis=2).reshape(
        window_count, G * G, 3 * channels
    )
    grad_qkv_grid = from_windows(grad_stack, images, row_step, local_step)
    grad_qkv = lax.all_to_all(
        grad_qkv_grid, "space", split_axis=1, concat_axis=3, tiled=True
    ).reshape(token_count, 3 * channels)
    qkv_local = jnp.einsum("tc,td->cd", normed, grad_qkv, preferred_element_type=jnp.float32)
    grad_normed = jnp.dot(grad_qkv, qkv_weight.T, preferred_element_type=jnp.float32).astype(
        jnp.bfloat16
    )
    grad_wide = grad_normed.astype(jnp.float32)
    grad_hat = grad_wide * norm_gain
    gain_local = jnp.sum(grad_wide * normal_hat, axis=0)
    grad_mid = cot_tok.astype(jnp.float32) + inv_std * (
        grad_hat
        - jnp.mean(grad_hat, axis=-1, keepdims=True)
        - normal_hat * jnp.mean(grad_hat * normal_hat, axis=-1, keepdims=True)
    )
    input_grad = grad_mid.astype(jnp.bfloat16)
    proj_local = jnp.einsum("te,tc->ec", act_low, input_grad, preferred_element_type=jnp.float32)
    grad_act = jnp.dot(input_grad, proj_weight.T, preferred_element_type=jnp.float32).reshape(
        images, slab_rows, map_cols, hidden_units
    )
    grad_conv = jax.vjp(jax.nn.gelu, conv_out)[1](grad_act)[0].astype(jnp.bfloat16)
    grad_rows = extended(grad_conv, (("space", 1),), 1)
    grad_pad = jnp.pad(grad_rows, ((0, 0), (0, 0), (1, 1), (0, 0)))
    hidden_grad = conv_backward(grad_pad, depth_weight, slab_rows, map_cols).astype(jnp.bfloat16)
    depth_local = depth_sum(hidden_pad, grad_conv, slab_rows, map_cols)
    depth_grad, gain_grad, proj_grad, qkv_grad, out_grad = sum_grads(
        proj_local, qkv_local, out_local, depth_local, gain_local
    )
    return (
        block_output,
        input_grad.reshape(images, slab_rows, map_cols, channels),
        hidden_grad,
        depth_grad,
        gain_grad,
        proj_grad,
        qkv_grad,
        out_grad,
    )


def solution(mesh):
    return jax.shard_map(
        local,
        mesh=mesh,
        in_specs=(
            P("dp", "space", None, None),
            P("dp", "space", None, None),
            P("dp", "space", None, None),
            P(),
            P(),
            P(),
            P(),
            P(),
        ),
        out_specs=(
            P("dp", "space", None, None),
            P("dp", "space", None, None),
            P("dp", "space", None, None),
            P(),
            P(),
            P("dp", "space"),
            P("dp", "space"),
            P("dp", "space"),
        ),
        check_vma=False,
    )
```

```python
import jax
import jax.numpy as jnp
from jax import lax
from jax.experimental import pallas as pl
from jax.experimental.pallas import tpu as pltpu
from jax.sharding import PartitionSpec as P

MESH = pl.DeviceIdType.MESH
F32, BF16 = jnp.float32, jnp.bfloat16
EPS = 1e-05
C, E, HEADS, HD = 768, 1536, 24, 32
ROWS, COLS, PLANE = 7, 56, 64
TOK = ROWS * PLANE
WIN = 512
SCALE = HD ** (-0.5)
ORDER = (1, 3, 2, 0)
NT = (((1,), (1,)), ((), ()))
TN = (((0,), (0,)), ((), ()))


def place():
    dp, sp = lax.axis_index("dp"), lax.axis_index("space")
    return dp, sp, lax.div(dp, 8), lax.rem(lax.div(dp, 2), 4), lax.rem(dp, 2)


def dp_of(x, zh, core):
    return (x * 4 + zh) * 2 + core


def greet(ids):
    barrier = pltpu.get_barrier_semaphore()
    for one in ids:
        pl.semaphore_signal(barrier, inc=1, device_id=one, device_id_type=MESH)
    pl.semaphore_wait(barrier, len(ids))


def remote(src, dst, send, recv, to):
    return pltpu.make_async_remote_copy(
        src_ref=src, dst_ref=dst, send_sem=send, recv_sem=recv, device_id=to, device_id_type=MESH
    )


def planes(ref, n):
    return ref.at[pl.ds(pl.multiple_of(n * PLANE, PLANE), PLANE)]


class Rows:
    def __init__(self, src, dst, ssem, rsem, dp, sp, out):
        self.src, self.dst, self.ssem, self.rsem = src, dst, ssem, rsem
        self.dp, self.sp, self.out = dp, sp, out

    def target(self, n):
        if self.out:
            row = self.sp * 7 + n
            return lax.rem(row, 8), lax.div(row, 8)
        row = n * 8 + self.sp
        return lax.div(row, 7), lax.rem(row, 7)

    def copies(self, n):
        to, slot = self.target(n)
        src, dst = planes(self.src, n), planes(self.dst, slot)
        far = remote(src, dst, self.ssem.at[n], self.rsem.at[slot], (self.dp, to))
        near = pltpu.make_async_copy(src, dst, self.rsem.at[slot])
        return to, far, near

    def start(self, n):
        to, far, near = self.copies(n)

        @pl.when(to != self.sp)
        def _():
            far.start()

        @pl.when(to == self.sp)
        def _():
            near.start()

    def wait_recv(self, n):
        one = planes(self.dst, n)
        pltpu.make_async_copy(one, one, self.rsem.at[n]).wait()

    def wait_send(self, n):
        to, far, _ = self.copies(n)

        @pl.when(to != self.sp)
        def _():
            far.wait_send()


class Halo:
    def __init__(self, top, bottom, halo, ssem, rsem, dp, sp):
        self.sp = sp
        self.up = remote(top, halo.at[1], ssem.at[0], rsem.at[1], (dp, jnp.maximum(sp - 1, 0)))
        self.down = remote(bottom, halo.at[0], ssem.at[1], rsem.at[0], (dp, jnp.minimum(sp + 1, 7)))
        self.halo = halo

    def start(self):
        @pl.when(self.sp > 0)
        def _():
            self.up.start()

        @pl.when(self.sp < 7)
        def _():
            self.down.start()

        zero = jnp.zeros(self.halo.shape[1:], self.halo.dtype)

        @pl.when(self.sp == 0)
        def _():
            self.halo[0] = zero

        @pl.when(self.sp == 7)
        def _():
            self.halo[1] = zero

    def wait_recv(self):
        @pl.when(self.sp > 0)
        def _():
            self.down.wait_recv()

        @pl.when(self.sp < 7)
        def _():
            self.up.wait_recv()

    def wait_send(self):
        @pl.when(self.sp > 0)
        def _():
            self.up.wait_send()

        @pl.when(self.sp < 7)
        def _():
            self.down.wait_send()


def col_masks(lanes):
    index = lax.broadcasted_iota(jnp.int32, (COLS, lanes), 0)
    return index == 0, index == COLS - 1


def later(value, first):
    return jnp.where(first, 0.0, pltpu.roll(value, 1, 0))


def earlier(value, last):
    return jnp.where(last, 0.0, pltpu.roll(value, COLS - 1, 0))


def padded(value):
    return jnp.concatenate([value, jnp.zeros((PLANE - COLS, value.shape[1]), F32)], axis=0)


def gelu_and_slope(value):
    k0, k1 = 0.7978845608028654, 0.044715
    square = value * value
    tanh = jnp.tanh(k0 * value * (1.0 + k1 * square))
    half = 0.5 * (1.0 + tanh)
    slope = half + 0.5 * value * (1.0 - tanh * tanh) * (k0 * (1.0 + 3.0 * k1 * square))
    return value * half, slope


def conv_forward(hidden, halo, taps, act, slope):
    def chunk(n, carry):
        lanes = pl.ds(pl.multiple_of(n * 128, 128), 128)
        first, last = col_masks(128)
        rows = [halo[0, :, lanes].astype(F32)]
        rows += [hidden[r, :, lanes].astype(F32) for r in range(ROWS)]
        rows += [halo[1, :, lanes].astype(F32)]
        tap = [taps[t : t + 1, lanes] for t in range(9)]
        for r in range(ROWS):
            part = [sum(tap[3 * a + b] * rows[r + a] for a in range(3)) for b in range(3)]
            conv = later(part[0], first) + part[1] + earlier(part[2], last)
            low, grad = gelu_and_slope(conv)
            act[PLANE * r : PLANE * (r + 1), lanes] = padded(low).astype(BF16)
            slope[PLANE * r : PLANE * (r + 1), lanes] = padded(grad)
        return carry

    lax.fori_loop(0, E // 128, chunk, 0)


def normal(mid):
    mean = jnp.mean(mid, axis=1, keepdims=True)
    centred = mid - mean
    inv = lax.rsqrt(jnp.mean(centred * centred, axis=1, keepdims=True) + EPS)
    return centred * inv, inv


def front_kernel(
    block, hidden, cot, depth_w, proj_w, gain,
    win_n, win_c, mid, act, slope,
    halo, taps, own_n, own_c, hs, hr, ns, nr, cs, cr,
):
    dp, sp, x, zh, core = place()
    greet([(dp, lax.rem(sp + j, 8)) for j in range(1, 8)])
    edge = Halo(hidden.at[0], hidden.at[ROWS - 1], halo, hs, hr, dp, sp)
    edge.start()
    cots = Rows(own_c, win_c, cs, cr, dp, sp, True)
    norms = Rows(own_n, win_n, ns, nr, dp, sp, True)
    for r in range(ROWS):
        own_c[PLANE * r : PLANE * (r + 1)] = padded(cot[r].astype(F32)).astype(BF16)
        cots.start(r)
    taps[0:9] = depth_w[...].astype(F32)
    edge.wait_recv()
    conv_forward(hidden, halo, taps, act, slope)

    def proj(n, carry):
        lanes = pl.ds(pl.multiple_of(n * 256, 256), 256)
        mid[:, lanes] = jnp.dot(act[...], proj_w[:, lanes], preferred_element_type=F32)
        return carry

    lax.fori_loop(0, C // 256, proj, 0)

    def norm(r, carry):
        here = pl.ds(pl.multiple_of(r * PLANE, PLANE), PLANE)
        total = mid[here, :] + padded(block[r].astype(F32))
        mid[here, :] = total
        own_n[here, :] = (normal(total)[0] * gain[...]).astype(BF16)
        norms.start(r)
        return carry

    lax.fori_loop(0, ROWS, norm, 0)
    for r in range(ROWS):
        cots.wait_recv(r)
        norms.wait_recv(r)
    for r in range(ROWS):
        cots.wait_send(r)
        norms.wait_send(r)
    edge.wait_send()


def window_place(index):
    win, n = index >> 6, index & 63
    g = (n * 37) >> 8
    return jnp.where(n < 49, g * PLANE + (n - 7 * g) * 8 + win, -1)


def attention(qkv, gatt, att, gqkv):
    lane = lax.broadcasted_iota(jnp.int32, (64, 128), 1) >> 5
    big = lax.broadcasted_iota(jnp.int32, (256, 128), 0) >> 6
    own = (big == (lax.broadcasted_iota(jnp.int32, (256, 128), 1) >> 5)).astype(F32).astype(BF16)
    valid = lax.broadcasted_iota(jnp.int32, (64, 256), 0) < 49

    def spread(value):
        return jnp.concatenate([value] * 4, axis=0) * own

    def gather(value):
        return jnp.where(
            lane < 2,
            jnp.where(lane == 0, value[0:64], value[64:128]),
            jnp.where(lane == 2, value[128:192], value[192:256]),
        )

    def window(w, carry):
        rows = pl.ds(pl.multiple_of(w * 64, 64), 64)
        for g in range(6):
            at = [slice(part * C + 128 * g, part * C + 128 * (g + 1)) for part in range(3)]
            query, key, value = (qkv[rows, at[part]] for part in range(3))
            query = spread(query)
            grad = spread(gatt[rows, at[0]])
            score = lax.dot_general(key, query, NT, preferred_element_type=F32) * SCALE
            score = jnp.where(valid, score, -1e30)
            power = jnp.exp(score - jnp.max(score, axis=0, keepdims=True))
            prob = power * (1.0 / jnp.sum(power, axis=0, keepdims=True))
            low = prob.astype(BF16)
            grad_prob = lax.dot_general(value, grad, NT, preferred_element_type=F32)
            inner = jnp.sum(grad_prob * prob, axis=0, keepdims=True)
            grad_low = (prob * (grad_prob - inner) * SCALE).astype(BF16)
            att[rows, at[0]] = gather(
                lax.dot_general(low, value, TN, preferred_element_type=F32)
            ).astype(BF16)
            gqkv[rows, at[0]] = gather(
                lax.dot_general(grad_low, key, TN, preferred_element_type=F32)
            ).astype(BF16)
            gqkv[rows, at[1]] = jnp.dot(grad_low, query, preferred_element_type=F32).astype(BF16)
            gqkv[rows, at[2]] = jnp.dot(low, grad, preferred_element_type=F32).astype(BF16)
        return carry

    lax.fori_loop(0, 8, window, 0)


def half_rows(value):
    left, right = (value[:, 128 * h : 128 * (h + 1)].reshape(32, 24, 128) for h in range(2))
    return jnp.concatenate([left, right], axis=1).reshape(4, 4, 2, 48, 128).astype(BF16)


def middle_kernel(
    win_n, win_c, qkv_w, out_w,
    att_t, gn_t, grads,
    norm_p, cot_p, qkv, gatt, att, gqkv, turned, gn_p,
):
    index = window_place(lax.broadcasted_iota(jnp.int32, (WIN, 1), 0))
    tokens = lax.broadcasted_iota(jnp.int32, (WIN, TOK), 1)
    perm = (index == tokens).astype(F32).astype(BF16)
    norm_p[...] = jnp.dot(perm, win_n[...], preferred_element_type=F32).astype(BF16)
    cot_p[...] = jnp.dot(perm, win_c[...], preferred_element_type=F32).astype(BF16)

    def tile(n):
        return pl.ds(pl.multiple_of(n * 256, 256), 256)

    def qkv_step(n, carry):
        qkv[:, tile(n)] = jnp.dot(
            norm_p[...], qkv_w[:, tile(n)], preferred_element_type=F32
        ).astype(BF16)
        return carry

    lax.fori_loop(0, 9, qkv_step, 0)

    def gatt_step(n, carry):
        gatt[:, tile(n)] = lax.dot_general(
            cot_p[...], out_w[tile(n), :], NT, preferred_element_type=F32
        ).astype(BF16)
        return carry

    lax.fori_loop(0, 3, gatt_step, 0)
    attention(qkv, gatt, att, gqkv)
    index = window_place(lax.broadcasted_iota(jnp.int32, (1, WIN), 1))
    tokens = lax.broadcasted_iota(jnp.int32, (TOK, WIN), 0)
    back = (index == tokens).astype(F32).astype(BF16)
    att_t[...] = jnp.dot(back, att[...], preferred_element_type=F32).astype(BF16)

    def gn_step(n, carry):
        gn_p[:, tile(n)] = lax.dot_general(
            gqkv[...], qkv_w[tile(n), :], NT, preferred_element_type=F32
        ).astype(BF16)
        return carry

    lax.fori_loop(0, 3, gn_step, 0)
    gn_t[...] = jnp.dot(back, gn_p[...], preferred_element_type=F32).astype(BF16)
    turned[...] = att[...].T

    def lanes(n):
        return pl.ds(pl.multiple_of(n * 128, 128), 128)

    def out_step(n, carry):
        right = jnp.concatenate([cot_p[:, lanes(n)], cot_p[:, lanes(n + 3)]], axis=1)
        grads[:, :, :, :, lanes(n + 9)] = half_rows(
            jnp.dot(turned[...], right, preferred_element_type=F32)
        )
        return carry

    lax.fori_loop(0, 3, out_step, 0)
    turned[...] = norm_p[...].T

    def grad_step(n, carry):
        right = jnp.concatenate([gqkv[:, lanes(n)], gqkv[:, lanes(n + 9)]], axis=1)
        grads[:, :, :, :, lanes(n)] = half_rows(
            jnp.dot(turned[...], right, preferred_element_type=F32)
        )
        return carry

    lax.fori_loop(0, 9, grad_step, 0)


class Sum:
    def __init__(self, grads, bufs, sems, spot, pair, xs, zs):
        self.g = grads
        self.r0, self.s0, self.r1, self.s1, self.r2 = bufs
        self.s0s, self.s0r, self.s1s, self.s1r, self.s2s, self.s2r = sems
        self.x, self.zh, self.core = spot
        self.pair, self.xs, self.zs = pair, xs, zs
        self.sent = []
        self.first, self.second, self.third = {}, [], []

    def start0(self, j):
        xx = lax.rem(self.x + j, 4)
        cp = remote(
            self.g.at[xx, :, 1 - self.core], self.r0.at[xx], self.s0s.at[j], self.s0r.at[j], self.pair
        )
        cp.start()
        self.first[j] = cp
        self.sent.append(cp)

    def step1(self, j):
        xx = lax.rem(self.x + j, 4)
        self.first[j].wait_recv()

        def body(i, carry):
            mine = self.g[xx, i, self.core].astype(F32)
            self.s0[xx, i] = (mine + self.r0[xx, i].astype(F32)).astype(BF16)
            return carry

        lax.fori_loop(0, 4, body, 0)
        if j:
            cp = remote(
                self.s0.at[xx], self.r1.at[j - 1], self.s1s.at[j - 1], self.s1r.at[j - 1], self.xs[j - 1]
            )
            cp.start()
            self.second.append(cp)
            self.sent.append(cp)

    def step2(self):
        for cp in self.second:
            cp.wait_recv()
        for j in ORDER:
            zz = lax.rem(self.zh + j, 4)
            total = self.s0[self.x, zz].astype(F32)
            for n in range(3):
                total = total + self.r1[n, zz].astype(F32)
            self.s1[zz] = total.astype(BF16)
            if j:
                cp = remote(
                    self.s1.at[zz], self.r2.at[j - 1], self.s2s.at[j - 1], self.s2r.at[j - 1], self.zs[j - 1]
                )
                cp.start()
                self.third.append(cp)
                self.sent.append(cp)

    def step3(self):
        for cp in self.third:
            cp.wait_recv()
        total = self.s1[self.zh].astype(F32)
        for n in range(3):
            total = total + self.r2[n].astype(F32)
        return total


class Last:
    def __init__(self, tiles, recv, ssem, rsem, sp, sps):
        self.tiles, self.recv, self.sp = tiles, recv, sp
        self.cps = [
            remote(tiles.at[lax.rem(sp + j, 8)], recv.at[j - 1], ssem.at[j - 1], rsem.at[j - 1], sps[j - 1])
            for j in range(1, 8)
        ]

    def start(self):
        for cp in self.cps:
            cp.start()

    def total(self):
        for cp in self.cps:
            cp.wait_recv()
        total = self.tiles[self.sp].astype(F32)
        for n in range(7):
            total = total + self.recv[n].astype(F32)
        return total

    def wait_send(self):
        for cp in self.cps:
            cp.wait_send()


class Small:
    def __init__(self, acc, recv, ssem, rsem, stages):
        self.acc, self.recv, self.ssem, self.rsem, self.stages = acc, recv, ssem, rsem, stages
        self.cps, base = [], 0
        for n, peers in enumerate(stages):
            self.cps.append([
                remote(acc.at[n], recv.at[base + i], ssem.at[base + i], rsem.at[base + i], peer)
                for i, peer in enumerate(peers)
            ])
            base += len(peers)

    def start(self, n):
        for cp in self.cps[n]:
            cp.start()

    def total(self, n):
        base = sum(len(peers) for peers in self.stages[:n])
        total = self.acc[n]
        for i, cp in enumerate(self.cps[n]):
            cp.wait_recv()
            total = total + self.recv[base + i]
        return total

    def step(self, n):
        self.acc[n + 1] = self.total(n)
        self.start(n + 1)

    def wait_send(self):
        for stage in self.cps:
            for cp in stage:
                cp.wait_send()


def conv_backward(grad, halo, hidden, taps, hidden_grad, depth):
    def chunk(n, carry):
        lanes = pl.ds(pl.multiple_of(n * 128, 128), 128)
        first, last = col_masks(128)
        rows = [halo[0, 0:COLS, lanes].astype(F32)]
        rows += [grad[PLANE * r : PLANE * r + COLS, lanes].astype(F32) for r in range(ROWS)]
        rows += [halo[1, 0:COLS, lanes].astype(F32)]
        tap = [taps[t : t + 1, lanes] for t in range(9)]
        sums = [jnp.zeros((8, 128), F32) for _ in range(9)]
        for r in range(ROWS):
            near = [rows[r + 2 - a] for a in range(3)]
            part = [sum(tap[3 * a + b] * near[a] for a in range(3)) for b in range(3)]
            total = earlier(part[0], last) + part[1] + later(part[2], first)
            hidden_grad[r, :, lanes] = total.astype(BF16)
            own = hidden[r, :, lanes].astype(F32)
            moved = [later(own, first), own, earlier(own, last)]
            for a in range(3):
                for b in range(3):
                    product = moved[b] * near[a]
                    for i in range(7):
                        sums[3 * a + b] = sums[3 * a + b] + product[8 * i : 8 * i + 8]
        for t in range(9):
            depth[t : t + 1, lanes] = jnp.sum(sums[t], axis=0, keepdims=True)
        return carry

    lax.fori_loop(0, E // 128, chunk, 0)


def back_kernel(
    att_w, gn_w, mid, act, slope, hidden, cot, depth_w, proj_w, gain, out_w, grads,
    block_o, input_o, hidden_o, depth_o, gain_o, proj_o, qkv_o, out_o,
    att, gn, ig, gc, halo, taps, depth, pgrads,
    ar0, as0, ar1, as1, ar2, pr0, ps0, pr1, ps1, pr2,
    atile, arecv, ptile, precv, sacc, srecv,
    ts, tr, us, ur, hs, hr,
    a0s, a0r, a1s, a1r, a2s, a2r, p0s, p0r, p1s, p1r, p2s, p2r,
    las, lar, lps, lpr, sms, smr,
):
    dp, sp, x, zh, core = place()
    pair = (dp_of(x, zh, 1 - core), sp)
    xs = [(dp_of(lax.rem(x + j, 4), zh, core), sp) for j in (1, 2, 3)]
    zs = [(dp_of(x, lax.rem(zh + j, 4), core), sp) for j in (1, 2, 3)]
    sps = [(dp, lax.rem(sp + j, 8)) for j in range(1, 8)]
    greet([pair] + xs + zs + sps)
    spot = (x, zh, core)
    asum = Sum(grads, (ar0, as0, ar1, as1, ar2), (a0s, a0r, a1s, a1r, a2s, a2r), spot, pair, xs, zs)
    psum = Sum(pgrads, (pr0, ps0, pr1, ps1, pr2), (p0s, p0r, p1s, p1r, p2s, p2r), spot, pair, xs, zs)
    alast = Last(atile, arecv, las, lar, sp, sps)
    plast = Last(ptile, precv, lps, lpr, sp, sps)
    small = Small(sacc, srecv, sms, smr, ([pair], xs, zs, sps))
    gns = Rows(gn_w, gn, us, ur, dp, sp, False)
    atts = Rows(att_w, att, ts, tr, dp, sp, False)
    for g in range(ROWS):
        gns.start(g)
    for g in range(ROWS):
        atts.start(g)
    for j in ORDER:
        asum.start0(j)
    taps[0:9] = depth_w[...].astype(F32)

    for r in range(ROWS):
        gns.wait_recv(r)

    def norm_step(r, carry):
        here = pl.ds(pl.multiple_of(r * PLANE, PLANE), PLANE)
        hat, inv = normal(mid[here, :])
        wide = gn[here, :].astype(F32)
        grad_hat = wide * gain[...]
        carry = carry + (wide * hat).reshape(8, 8, C).sum(axis=0)
        inner = jnp.mean(grad_hat * hat, axis=1, keepdims=True)
        mean = jnp.mean(grad_hat, axis=1, keepdims=True)
        cots = padded(cot[r].astype(F32))
        low = (cots + inv * (grad_hat - mean - hat * inner)).astype(BF16)
        ig[here, :] = low
        input_o[r] = low[0:COLS]
        return carry

    gain_part = lax.fori_loop(0, ROWS, norm_step, jnp.zeros((8, C), F32))
    gain_part = jnp.sum(gain_part, axis=0, keepdims=True)
    for j in ORDER:
        asum.step1(j)
    for j in ORDER:
        xx = lax.rem(x + j, 4)
        left = act[:, pl.ds(pl.multiple_of(xx * 384, 128), 384)].T
        for n in range(3):
            tile = slice(256 * n, 256 * (n + 1))
            part = jnp.dot(left, ig[:, tile], preferred_element_type=F32)
            pgrads[xx, :, :, :, tile] = part.reshape(4, 2, 48, 256).astype(BF16)
        psum.start0(j)

    def act_step(n, carry):
        here = pl.ds(pl.multiple_of(n * 256, 256), 256)
        part = lax.dot_general(ig[...], proj_w[here, :], NT, preferred_element_type=F32)
        gc[:, here] = (part * slope[:, here]).astype(BF16)
        return carry

    lax.fori_loop(0, E // 256, act_step, 0)
    edge = Halo(gc.at[0:PLANE], gc.at[TOK - PLANE : TOK], halo, hs, hr, dp, sp)
    edge.start()
    for j in ORDER:
        psum.step1(j)
    for r in range(ROWS):
        atts.wait_recv(r)

    def out_step(n, carry):
        here = pl.ds(pl.multiple_of(n * 256, 256), 256)
        part = jnp.dot(att[...], out_w[:, here], preferred_element_type=F32)
        part = (part + mid[:, here]).astype(BF16)
        for r in range(ROWS):
            block_o[r, :, here] = part[PLANE * r : PLANE * r + COLS]
        return carry

    lax.fori_loop(0, C // 256, out_step, 0)
    asum.step2()
    edge.wait_recv()
    conv_backward(gc, halo, hidden, taps, hidden_o, depth)
    sacc[0, 0:8, 0:E] = depth[0:8]
    for i in range(4):
        sacc[0, i : i + 1, E : E + 384] = depth[8:9, 384 * i : 384 * (i + 1)]
    for i in range(2):
        sacc[0, 4 + i : 5 + i, E : E + 384] = gain_part[:, 384 * i : 384 * (i + 1)]
    sacc[0, 6:8, E : E + 384] = jnp.zeros((2, 384), F32)
    small.start(0)
    psum.step2()
    total = asum.step3()
    for j in range(8):
        half, col = j // 4, j % 4
        qkv = total[24 * half : 24 * half + 24, 288 * col : 288 * col + 288]
        out = total[24 * half : 24 * half + 24, 1152 + 96 * col : 1152 + 96 * col + 96]
        atile[j, :, 0:144] = jnp.concatenate([qkv[:, :144], qkv[:, 144:]], axis=0).astype(BF16)
        atile[j, :, 144:192] = jnp.concatenate([out[:, :48], out[:, 48:]], axis=0).astype(BF16)
    alast.start()
    small.step(0)
    total = psum.step3()
    for j in range(8):
        ptile[j, :, 0:96] = total[:, 96 * j : 96 * j + 96].astype(BF16)
    plast.start()
    small.step(1)
    total = alast.total()
    qkv_o[:, 0:144] = total[0:24, 0:144]
    qkv_o[:, 144:288] = total[24:48, 0:144]
    out_o[:, 0:48] = total[0:24, 144:192]
    out_o[:, 48:96] = total[24:48, 144:192]
    small.step(2)
    proj_o[...] = plast.total()[:, 0:96]
    total = small.total(3)
    depth_o[0:8] = total[:, 0:E]
    for i in range(4):
        depth_o[8:9, 384 * i : 384 * (i + 1)] = total[i : i + 1, E : E + 384]
    for i in range(2):
        gain_o[:, 384 * i : 384 * (i + 1)] = total[4 + i : 5 + i, E : E + 384]
    for g in range(ROWS):
        gns.wait_send(g)
        atts.wait_send(g)
    edge.wait_send()
    for cp in asum.sent + psum.sent:
        cp.wait_send()
    alast.wait_send()
    plast.wait_send()
    small.wait_send()


VM = pl.BlockSpec(memory_space=pltpu.VMEM)
DMA = pltpu.SemaphoreType.DMA
MIB = 1024 * 1024


def shape(dims, dtype=BF16):
    return jax.ShapeDtypeStruct(dims, dtype)


def sum_bufs(width):
    return [
        pltpu.VMEM((4, 4, 48, width), BF16),
        pltpu.VMEM((4, 4, 48, width), BF16),
        pltpu.VMEM((3, 4, 48, width), BF16),
        pltpu.VMEM((4, 48, width), BF16),
        pltpu.VMEM((3, 48, width), BF16),
    ]


def sum_sems():
    return [DMA((4,)), DMA((4,)), DMA((3,)), DMA((3,)), DMA((3,)), DMA((3,))]


def local(block, hidden, cot, depth_w, proj_w, gain, qkv_w, out_w):
    gain = gain.reshape(1, C)
    block, hidden, cot = block[0], hidden[0], cot[0]
    win_n, win_c, mid, act, slope = pl.pallas_call(
        front_kernel,
        out_shape=(shape((TOK, C)), shape((TOK, C)), shape((TOK, C), F32), shape((TOK, E)), shape((TOK, E), F32)),
        in_specs=[VM] * 6,
        out_specs=(VM,) * 5,
        scratch_shapes=[
            pltpu.VMEM((2, COLS, E), BF16),
            pltpu.VMEM((16, E), F32),
            pltpu.VMEM((TOK, C), BF16),
            pltpu.VMEM((TOK, C), BF16),
            DMA((2,)), DMA((2,)), DMA((7,)), DMA((7,)), DMA((7,)), DMA((7,)),
        ],
        compiler_params=pltpu.CompilerParams(
            collective_id=1, has_side_effects=True, vmem_limit_bytes=48 * MIB
        ),
        name="front",
    )(block, hidden, cot, depth_w, proj_w, gain)
    att_w, gn_w, grads = pl.pallas_call(
        middle_kernel,
        out_shape=(shape((TOK, C)), shape((TOK, C)), shape((4, 4, 2, 48, E))),
        in_specs=[VM] * 4,
        out_specs=(VM,) * 3,
        scratch_shapes=[
            pltpu.VMEM((WIN, C), BF16),
            pltpu.VMEM((WIN, C), BF16),
            pltpu.VMEM((WIN, 3 * C), BF16),
            pltpu.VMEM((WIN, C), BF16),
            pltpu.VMEM((WIN, C), BF16),
            pltpu.VMEM((WIN, 3 * C), BF16),
            pltpu.VMEM((C, WIN), BF16),
            pltpu.VMEM((WIN, C), BF16),
        ],
        compiler_params=pltpu.CompilerParams(vmem_limit_bytes=48 * MIB),
        name="middle",
    )(win_n, win_c, qkv_w, out_w)
    block_o, input_o, hidden_o, depth_o, gain_o, proj_o, qkv_o, out_o = pl.pallas_call(
        back_kernel,
        out_shape=(
            shape((ROWS, COLS, C)), shape((ROWS, COLS, C)), shape((ROWS, COLS, E)),
            shape((9, E), F32), shape((1, C), F32),
            shape((48, 96), F32), shape((24, 288), F32), shape((24, 96), F32),
        ),
        in_specs=[VM] * 12,
        out_specs=(VM,) * 8,
        scratch_shapes=[
            pltpu.VMEM((TOK, C), BF16),
            pltpu.VMEM((TOK, C), BF16),
            pltpu.VMEM((TOK, C), BF16),
            pltpu.VMEM((TOK, E), BF16),
            pltpu.VMEM((2, PLANE, E), BF16),
            pltpu.VMEM((16, E), F32),
            pltpu.VMEM((16, E), F32),
            pltpu.VMEM((4, 4, 2, 48, C), BF16),
        ]
        + sum_bufs(E)
        + sum_bufs(C)
        + [
            pltpu.VMEM((8, 48, 256), BF16),
            pltpu.VMEM((7, 48, 256), BF16),
            pltpu.VMEM((8, 48, 128), BF16),
            pltpu.VMEM((7, 48, 128), BF16),
            pltpu.VMEM((4, 8, 1920), F32),
            pltpu.VMEM((14, 8, 1920), F32),
        ]
        + [DMA((7,)), DMA((7,)), DMA((7,)), DMA((7,)), DMA((2,)), DMA((2,))]
        + sum_sems()
        + sum_sems()
        + [DMA((7,)), DMA((7,)), DMA((7,)), DMA((7,)), DMA((14,)), DMA((14,))],
        compiler_params=pltpu.CompilerParams(
            collective_id=2, has_side_effects=True, vmem_limit_bytes=58 * MIB
        ),
        name="back",
    )(att_w, gn_w, mid, act, slope, hidden, cot, depth_w, proj_w, gain, out_w, grads)
    return (
        block_o[None], input_o[None], hidden_o[None], depth_o, gain_o.reshape(C), proj_o, qkv_o, out_o,
    )


def solution(mesh):
    slab = P("dp", "space", None, None)
    part = P("dp", "space")
    return jax.shard_map(
        local,
        mesh=mesh,
        in_specs=(slab, slab, slab, P(), P(), P(), P(), P()),
        out_specs=(slab, slab, slab, P(), P(), part, part, part),
        check_vma=False,
    )
```

```python
import jax
import jax.numpy as jnp
from jax import lax
from jax.experimental import pallas as pl
from jax.experimental.pallas import tpu as pltpu
from jax.sharding import PartitionSpec as P

MESH = pl.DeviceIdType.MESH
F32, BF16 = jnp.float32, jnp.bfloat16
EPS = 1e-05
C, E, HEADS, HD = 768, 1536, 24, 32
ROWS, COLS, PLANE = 7, 56, 64
TOK = ROWS * PLANE
WIN = 512
SCALE = HD ** (-0.5)
XORS = (2, 1, 3, 0)
NT = (((1,), (1,)), ((), ()))
TN = (((0,), (0,)), ((), ()))


def place():
    dp, sp = lax.axis_index("dp"), lax.axis_index("space")
    return dp, sp, lax.div(dp, 8), lax.rem(lax.div(dp, 2), 4), lax.rem(dp, 2)


def dp_of(x, zh, core):
    return (x * 4 + zh) * 2 + core


def greet(ids):
    barrier = pltpu.get_barrier_semaphore()
    for one in ids:
        pl.semaphore_signal(barrier, inc=1, device_id=one, device_id_type=MESH)
    pl.semaphore_wait(barrier, len(ids))


def remote(src, dst, send, recv, to):
    return pltpu.make_async_remote_copy(
        src_ref=src, dst_ref=dst, send_sem=send, recv_sem=recv, device_id=to, device_id_type=MESH
    )


def planes(ref, n):
    return ref.at[pl.ds(pl.multiple_of(n * PLANE, PLANE), PLANE)]


class Rows:
    def __init__(self, src, dst, ssem, rsem, dp, sp, out):
        self.src, self.dst, self.ssem, self.rsem = src, dst, ssem, rsem
        self.dp, self.sp, self.out = dp, sp, out

    def target(self, n):
        if self.out:
            row = self.sp * 7 + n
            return lax.rem(row, 8), lax.div(row, 8)
        row = n * 8 + self.sp
        return lax.div(row, 7), lax.rem(row, 7)

    def copies(self, n):
        to, slot = self.target(n)
        src, dst = planes(self.src, n), planes(self.dst, slot)
        far = remote(src, dst, self.ssem.at[n], self.rsem.at[slot], (self.dp, to))
        near = pltpu.make_async_copy(src, dst, self.rsem.at[slot])
        return to, far, near

    def start(self, n):
        to, far, near = self.copies(n)

        @pl.when(to != self.sp)
        def _():
            far.start()

        @pl.when(to == self.sp)
        def _():
            near.start()

    def wait_recv(self, n):
        one = planes(self.dst, n)
        pltpu.make_async_copy(one, one, self.rsem.at[n]).wait()

    def wait_send(self, n):
        to, far, _ = self.copies(n)

        @pl.when(to != self.sp)
        def _():
            far.wait_send()


class Halo:
    def __init__(self, top, bottom, halo, ssem, rsem, dp, sp):
        self.sp = sp
        self.up = remote(top, halo.at[1], ssem.at[0], rsem.at[1], (dp, jnp.maximum(sp - 1, 0)))
        self.down = remote(bottom, halo.at[0], ssem.at[1], rsem.at[0], (dp, jnp.minimum(sp + 1, 7)))
        self.halo = halo

    def start(self):
        @pl.when(self.sp > 0)
        def _():
            self.up.start()

        @pl.when(self.sp < 7)
        def _():
            self.down.start()

        zero = jnp.zeros(self.halo.shape[1:], self.halo.dtype)

        @pl.when(self.sp == 0)
        def _():
            self.halo[0] = zero

        @pl.when(self.sp == 7)
        def _():
            self.halo[1] = zero

    def wait_recv(self):
        @pl.when(self.sp > 0)
        def _():
            self.down.wait_recv()

        @pl.when(self.sp < 7)
        def _():
            self.up.wait_recv()

    def wait_send(self):
        @pl.when(self.sp > 0)
        def _():
            self.up.wait_send()

        @pl.when(self.sp < 7)
        def _():
            self.down.wait_send()


def col_masks(lanes):
    index = lax.broadcasted_iota(jnp.int32, (COLS, lanes), 0)
    return index == 0, index == COLS - 1


def later(value, first):
    return jnp.where(first, 0.0, pltpu.roll(value, 1, 0))


def earlier(value, last):
    return jnp.where(last, 0.0, pltpu.roll(value, COLS - 1, 0))


def padded(value):
    return jnp.concatenate([value, jnp.zeros((PLANE - COLS, value.shape[1]), F32)], axis=0)


def gelu_and_slope(value):
    k0, k1 = 0.7978845608028654, 0.044715
    square = value * value
    tanh = jnp.tanh(k0 * value * (1.0 + k1 * square))
    half = 0.5 * (1.0 + tanh)
    slope = half + 0.5 * value * (1.0 - tanh * tanh) * (k0 * (1.0 + 3.0 * k1 * square))
    return value * half, slope


def conv_forward(hidden, halo, taps, act, slope, begin, end):
    def chunk(n, carry):
        lanes = pl.ds(pl.multiple_of(n * 128, 128), 128)
        first, last = col_masks(128)
        rows = {}
        for r in range(begin - 1, end + 1):
            if r < 0:
                rows[r] = halo[0, :, lanes].astype(F32)
            elif r == ROWS:
                rows[r] = halo[1, :, lanes].astype(F32)
            else:
                rows[r] = hidden[r, :, lanes].astype(F32)
        tap = [taps[t : t + 1, lanes] for t in range(9)]
        for r in range(begin, end):
            part = [sum(tap[3 * a + b] * rows[r + a - 1] for a in range(3)) for b in range(3)]
            conv = later(part[0], first) + part[1] + earlier(part[2], last)
            low, grad = gelu_and_slope(conv)
            act[PLANE * r : PLANE * (r + 1), lanes] = padded(low).astype(BF16)
            slope[PLANE * r : PLANE * (r + 1), lanes] = padded(grad)
        return carry

    lax.fori_loop(0, E // 128, chunk, 0)


def normal(mid):
    mean = jnp.mean(mid, axis=1, keepdims=True)
    centred = mid - mean
    inv = lax.rsqrt(jnp.mean(centred * centred, axis=1, keepdims=True) + EPS)
    return centred * inv, inv


def window_place(index):
    win, n = index >> 6, index & 63
    g = (n * 37) >> 8
    return jnp.where(n < 49, g * PLANE + (n - 7 * g) * 8 + win, -1)


def attention(qkv, gatt, att, gqkv):
    lane = lax.broadcasted_iota(jnp.int32, (64, 128), 1) >> 5
    big = lax.broadcasted_iota(jnp.int32, (256, 128), 0) >> 6
    own = (big == (lax.broadcasted_iota(jnp.int32, (256, 128), 1) >> 5)).astype(F32).astype(BF16)
    valid = lax.broadcasted_iota(jnp.int32, (64, 256), 0) < 49

    def spread(value):
        return jnp.concatenate([value] * 4, axis=0) * own

    def gather(value):
        return jnp.where(
            lane < 2,
            jnp.where(lane == 0, value[0:64], value[64:128]),
            jnp.where(lane == 2, value[128:192], value[192:256]),
        )

    def window(w, carry):
        rows = pl.ds(pl.multiple_of(w * 64, 64), 64)
        for g in range(6):
            at = [slice(part * C + 128 * g, part * C + 128 * (g + 1)) for part in range(3)]
            query, key, value = (qkv[rows, at[part]] for part in range(3))
            query = spread(query)
            grad = spread(gatt[rows, at[0]])
            score = lax.dot_general(key, query, NT, preferred_element_type=F32) * SCALE
            score = jnp.where(valid, score, -1e30)
            power = jnp.exp(score - jnp.max(score, axis=0, keepdims=True))
            prob = power * (1.0 / jnp.sum(power, axis=0, keepdims=True))
            low = prob.astype(BF16)
            grad_prob = lax.dot_general(value, grad, NT, preferred_element_type=F32)
            inner = jnp.sum(grad_prob * prob, axis=0, keepdims=True)
            grad_low = (prob * (grad_prob - inner) * SCALE).astype(BF16)
            att[rows, at[0]] = gather(
                lax.dot_general(low, value, TN, preferred_element_type=F32)
            ).astype(BF16)
            gqkv[rows, at[0]] = gather(
                lax.dot_general(grad_low, key, TN, preferred_element_type=F32)
            ).astype(BF16)
            gqkv[rows, at[1]] = jnp.dot(grad_low, query, preferred_element_type=F32).astype(BF16)
            gqkv[rows, at[2]] = jnp.dot(low, grad, preferred_element_type=F32).astype(BF16)
        return carry

    lax.fori_loop(0, 8, window, 0)


def flip(q, mask):
    if mask == 0:
        return q
    if mask == 1:
        return q + 1 - 2 * lax.rem(q, 2)
    if mask == 3:
        return 3 - q
    return lax.rem(q + 2, 4)


class Pair:
    def __init__(self, grads, recv, total, ssem, rsem, core, peer, depth):
        self.grads, self.recv, self.dst, self.core, self.depth = grads, recv, total, core, depth
        self.ssem, self.rsem, self.peer = ssem, rsem, peer

    def copy(self, q):
        index = (q,) + (slice(None),) * self.depth + (1 - self.core,)
        return remote(
            self.grads.at[index], self.recv.at[q], self.ssem.at[q], self.rsem.at[q], self.peer
        )

    def start(self, q):
        self.copy(q).start()

    def add(self, q):
        self.copy(q).wait_recv()

        def body(i, carry):
            index = (q, lax.div(i, 4), lax.rem(i, 4)) if self.depth == 2 else (q, i)
            mine = self.grads[index + (self.core,)].astype(F32)
            self.dst[index] = (mine + self.recv[index].astype(F32)).astype(BF16)
            return carry

        lax.fori_loop(0, 4**self.depth, body, 0)

    def wait_send(self):
        for q in range(4):
            self.copy(q).wait_send()


class Halve:
    def __init__(self, src, recv, ssem, rsem, q, peers, view, piece, count):
        self.src, self.recv, self.q, self.view, self.piece, self.count = src, recv, q, view, piece, count
        self.cps = {}
        for h in range(2):
            near, far = (1, 3) if h == 0 else (3, 1)
            for slot, (block, to) in enumerate(((near, near), (2, near), (far, far))):
                n = 3 * h + slot
                self.cps[h, slot] = remote(
                    src.at[view(flip(q, block), h)], recv.at[view(slot, h)], ssem.at[n], rsem.at[n], peers[to]
                )

    def start(self):
        for slot in (1, 0):
            for h in range(2):
                self.cps[h, slot].start()

    def forward(self):
        for h in range(2):
            self.cps[h, 1].wait_recv()
            block = flip(self.q, 3 if h == 0 else 1)

            def body(i, carry, h=h, block=block):
                mine = self.src[self.piece(block, h, i)].astype(F32)
                mine = mine + self.recv[self.piece(1, h, i)].astype(F32)
                self.src[self.piece(block, h, i)] = mine.astype(BF16)
                return carry

            lax.fori_loop(0, self.count, body, 0)
            self.cps[h, 2].start()

    def finish(self, put):
        for h in range(2):
            self.cps[h, 0].wait_recv()
            self.cps[h, 2].wait_recv()

            def body(i, carry, h=h):
                mine = self.src[self.piece(self.q, h, i)].astype(F32)
                mine = mine + self.recv[self.piece(0, h, i)].astype(F32)
                put(h, i, mine + self.recv[self.piece(2, h, i)].astype(F32))
                return carry

            lax.fori_loop(0, self.count, body, 0)

    def wait_send(self):
        for cp in self.cps.values():
            cp.wait_send()


class Fan:
    def __init__(self, pieces, recvs, ssem, rsem, peers):
        self.cps = [
            remote(pieces(n), recvs(n), ssem.at[n], rsem.at[n], peer) for n, peer in enumerate(peers)
        ]

    def start(self):
        for cp in self.cps:
            cp.start()

    def wait_recv(self):
        for cp in self.cps:
            cp.wait_recv()

    def wait_send(self):
        for cp in self.cps:
            cp.wait_send()


def conv_backward(grad, halo, hidden, taps, hidden_grad, depth, begin, end):
    def chunk(n, carry):
        lanes = pl.ds(pl.multiple_of(n * 128, 128), 128)
        first, last = col_masks(128)
        rows = [halo[0, 0:COLS, lanes].astype(F32)]
        rows += [grad[PLANE * r : PLANE * r + COLS, lanes].astype(F32) for r in range(ROWS)]
        rows += [halo[1, 0:COLS, lanes].astype(F32)]
        tap = [taps[t : t + 1, lanes] for t in range(9)]
        sums = [jnp.zeros((8, 128), F32) for _ in range(9)]
        for r in range(ROWS):
            near = [rows[r + 2 - a] for a in range(3)]
            part = [sum(tap[3 * a + b] * near[a] for a in range(3)) for b in range(3)]
            total = earlier(part[0], last) + part[1] + later(part[2], first)
            hidden_grad[r, :, lanes] = total.astype(BF16)
            own = hidden[r, :, lanes].astype(F32)
            moved = [later(own, first), own, earlier(own, last)]
            for a in range(3):
                for b in range(3):
                    product = moved[b] * near[a]
                    for i in range(7):
                        sums[3 * a + b] = sums[3 * a + b] + product[8 * i : 8 * i + 8]
        for t in range(9):
            depth[t : t + 1, lanes] = jnp.sum(sums[t], axis=0, keepdims=True)
        return carry

    lax.fori_loop(begin, end, chunk, 0)


def tile(n, width=256):
    return pl.ds(pl.multiple_of(n * width, width), width)


def section_kernel(
    block_h, hidden_h, cot_h, proj_h, qkv_h, out_h, depth_w, gain,
    block_o, input_o, hidden_o, depth_o, gain_o, proj_o, qkv_o, out_o,
    block, hidden, cot, proj_w, qkv_w, out_w, loads,
    halo, taps, own_n, own_c, win_n, win_c, mid, act, slope,
    norm_p, cot_p, qkv, gatt, att_p, gqkv, turned, gn_p, wide,
    att_w, gn_w, att, gn, ig, gc, edges, depth,
    agrads, ar0, as0, ary, as1, arx, as2, arz, alast, alrecv,
    pgrads, pr0, ps0, prx, ps1, prz, ptile, precv,
    small, srecv, ssum, sall, sfinal,
    hs, hr, ns, nr, cs, cr, ts, tr, us, ur, es, er,
    a0s, a0r, ays, ayr, axs, axr, azs, azr, als, alr,
    p0s, p0r, pxs, pxr, pzs, pzr, pls, plr,
    d0s, d0r, d1s, d1r, d2s, d2r,
):
    dp, sp, x, zh, core = place()
    y, zl = lax.div(sp, 2), lax.rem(sp, 2)
    pulls = {}
    pairs = ((hidden_h, hidden), (cot_h, cot), (proj_h, proj_w), (block_h, block), (out_h, out_w), (qkv_h, qkv_w))
    for n, (src, dst) in enumerate(pairs):
        pulls[n] = pltpu.make_async_copy(src, dst, loads.at[n])
        pulls[n].start()
    pair = (dp_of(x, zh, 1 - core), sp)
    plane16 = [(dp_of(lax.rem(x + i, 4), lax.rem(zh + j, 4), core), sp) for i in range(4) for j in range(4)][1:]
    sps = [(dp, lax.rem(sp + j, 8)) for j in range(1, 8)]
    others = sps + [(dp_of(x, zh, 1 - core), lax.rem(sp + j, 8)) for j in range(8)]
    greet(plane16 + others)
    xp = {m: (dp_of(flip(x, m), zh, core), sp) for m in (1, 3)}
    zp = {m: (dp_of(x, flip(zh, m), core), sp) for m in (1, 3)}
    yp = {m: (dp, flip(y, m) * 2 + zl) for m in (1, 3)}

    edge = Halo(hidden_h.at[0], hidden_h.at[ROWS - 1], halo, hs, hr, dp, sp)
    edge.start()
    cots = Rows(own_c, win_c, cs, cr, dp, sp, True)
    norms = Rows(own_n, win_n, ns, nr, dp, sp, True)
    pulls[1].wait()
    for r in range(ROWS):
        own_c[PLANE * r : PLANE * (r + 1)] = padded(cot[r].astype(F32)).astype(BF16)
        cots.start(r)
    taps[0:9] = depth_w[...].astype(F32)
    scale = gain[...].reshape(1, C)
    pulls[0].wait()
    edge.wait_recv()
    for begin, end in ((0, 4), (4, 7)):
        conv_forward(hidden, halo, taps, act, slope, begin, end)
        if begin == 0:
            pulls[2].wait()
            pulls[3].wait()
        span = slice(PLANE * begin, PLANE * end)

        def proj(n, carry, span=span):
            mid[span, tile(n)] = jnp.dot(act[span, :], proj_w[:, tile(n)], preferred_element_type=F32)
            return carry

        lax.fori_loop(0, C // 256, proj, 0)

        def norm(r, carry):
            here = tile(r, PLANE)
            total = mid[here, :] + padded(block[r].astype(F32))
            mid[here, :] = total
            own_n[here, :] = (normal(total)[0] * scale).astype(BF16)
            norms.start(r)
            return carry

        lax.fori_loop(begin, end, norm, 0)

    index = window_place(lax.broadcasted_iota(jnp.int32, (WIN, 1), 0))
    tokens = lax.broadcasted_iota(jnp.int32, (WIN, TOK), 1)
    perm = (index == tokens).astype(F32).astype(BF16)
    for r in range(ROWS):
        cots.wait_recv(r)
    cot_p[...] = jnp.dot(perm, win_c[...], preferred_element_type=F32).astype(BF16)
    pulls[4].wait()

    def gatt_step(n, carry):
        gatt[:, tile(n)] = lax.dot_general(
            cot_p[...], out_w[tile(n), :], NT, preferred_element_type=F32
        ).astype(BF16)
        return carry

    lax.fori_loop(0, 3, gatt_step, 0)
    for r in range(ROWS):
        norms.wait_recv(r)
    norm_p[...] = jnp.dot(perm, win_n[...], preferred_element_type=F32).astype(BF16)
    pulls[5].wait()

    def qkv_step(n, carry):
        qkv[:, tile(n)] = jnp.dot(
            norm_p[...], qkv_w[:, tile(n)], preferred_element_type=F32
        ).astype(BF16)
        return carry

    lax.fori_loop(0, 9, qkv_step, 0)
    attention(qkv, gatt, att_p, gqkv)
    index = window_place(lax.broadcasted_iota(jnp.int32, (1, WIN), 1))
    tokens = lax.broadcasted_iota(jnp.int32, (TOK, WIN), 0)
    back = (index == tokens).astype(F32).astype(BF16)

    def gn_step(n, carry):
        gn_p[:, tile(n)] = lax.dot_general(
            gqkv[...], qkv_w[tile(n), :], NT, preferred_element_type=F32
        ).astype(BF16)
        return carry

    lax.fori_loop(0, 3, gn_step, 0)
    gns = Rows(gn_w, gn, us, ur, dp, sp, False)
    atts = Rows(att_w, att, ts, tr, dp, sp, False)
    gn_w[...] = jnp.dot(back, gn_p[...], preferred_element_type=F32).astype(BF16)
    for g in range(ROWS):
        gns.start(g)
    att_w[...] = jnp.dot(back, att_p[...], preferred_element_type=F32).astype(BF16)
    for g in range(ROWS):
        atts.start(g)

    apair = Pair(agrads, ar0, as0, a0s, a0r, core, pair, 2)
    ahalf = [
        Halve(as0, ary, ays, ayr, y, yp, lambda q, h: (q, slice(None), pl.ds(2 * h, 2)),
              lambda q, h, i: (q, i, pl.ds(2 * h, 2)), 4),
        Halve(as1, arx, axs, axr, x, xp, lambda q, h: (q, pl.ds(2 * h, 2)),
              lambda q, h, i: (q, 2 * h + i), 2),
        Halve(as2, arz, azs, azr, zh, zp, lambda q, h: (q, slice(None), slice(256 * h, 256 + 128 * h)),
              lambda q, h, i: (q, slice(None), slice(256 * h, 256 + 128 * h)), 1),
    ]
    for half in range(2):
        turned[...] = norm_p[...].T

        def grad_step(n, carry, half=half):
            right = gqkv[:, pl.ds(pl.multiple_of(1152 * half + 384 * n, 128), 384)]
            wide[:, tile(n, 384)] = jnp.dot(turned[...], right, preferred_element_type=F32)
            return carry

        lax.fori_loop(0, 3, grad_step, 0)
        turned[...] = att_p[...].T

        def out_grad_step(n, carry, half=half):
            right = cot_p[:, pl.ds(pl.multiple_of(384 * half + 128 * n, 128), 128)]
            wide[:, pl.ds(pl.multiple_of(1152 + 128 * n, 128), 128)] = jnp.dot(
                turned[...], right, preferred_element_type=F32
            )
            return carry

        lax.fori_loop(0, 3, out_grad_step, 0)

        def pack(xx, carry, half=half):
            rows = pl.ds(pl.multiple_of(192 * xx, 8), 192)
            for yy in range(2):
                both = []
                for low in range(2):
                    i = 2 * yy + low
                    left = wide[rows, 288 * i : 288 * (i + 1)]
                    right = wide[rows, 1152 + 96 * i : 1152 + 96 * (i + 1)]
                    both.append(jnp.concatenate([left, right], axis=1).reshape(8, 24, 384))
                value = jnp.concatenate(both, axis=1).astype(BF16)
                agrads[2 * half + yy, xx] = value.reshape(4, 2, 48, 384)
            return carry

        lax.fori_loop(0, 4, pack, 0)
        apair.start(2 * half)
        apair.start(2 * half + 1)

    for r in range(ROWS):
        gns.wait_recv(r)

    def norm_step(r, carry):
        here = tile(r, PLANE)
        hat, inv = normal(mid[here, :])
        grad = gn[here, :].astype(F32)
        grad_hat = grad * scale
        carry = carry + (grad * hat).reshape(8, 8, C).sum(axis=0)
        inner = jnp.mean(grad_hat * hat, axis=1, keepdims=True)
        mean = jnp.mean(grad_hat, axis=1, keepdims=True)
        cotangent = padded(cot[r].astype(F32))
        low = (cotangent + inv * (grad_hat - mean - hat * inner)).astype(BF16)
        ig[here, :] = low
        input_o[r] = low[0:COLS]
        return carry

    gain_part = lax.fori_loop(0, ROWS, norm_step, jnp.zeros((8, C), F32))
    gain_part = jnp.sum(gain_part, axis=0, keepdims=True)
    for m in XORS:
        apair.add(flip(y, m))
    ahalf[0].start()

    ppair = Pair(pgrads, pr0, ps0, p0s, p0r, core, pair, 1)
    phalf = [
        Halve(ps0, prx, pxs, pxr, x, xp, lambda q, h: (q, pl.ds(2 * h, 2)),
              lambda q, h, i: (q, 2 * h + i), 2),
        Halve(ps1, prz, pzs, pzr, zh, zp, lambda q, h: (q, slice(None), slice(384 * h, 384 * (h + 1))),
              lambda q, h, i: (q, slice(None), slice(384 * h, 384 * (h + 1))), 1),
    ]
    for m in XORS:
        xx = flip(x, m)
        turned[0:384, 0:TOK] = act[:, pl.ds(pl.multiple_of(xx * 384, 128), 384)].T

        def proj_step(n, carry, xx=xx):
            part = jnp.dot(turned[0:384, 0:TOK], ig[:, tile(n)], preferred_element_type=F32)
            pgrads[xx, :, :, :, tile(n)] = part.reshape(4, 2, 48, 256).astype(BF16)
            return carry

        lax.fori_loop(0, 3, proj_step, 0)
        ppair.start(xx)

    def act_step(n, carry):
        part = lax.dot_general(ig[...], proj_w[tile(n), :], NT, preferred_element_type=F32)
        gc[:, tile(n)] = (part * slope[:, tile(n)]).astype(BF16)
        return carry

    lax.fori_loop(0, E // 256, act_step, 0)
    edge2 = Halo(gc.at[0:PLANE], gc.at[TOK - PLANE : TOK], edges, es, er, dp, sp)
    edge2.start()
    for m in XORS:
        ppair.add(flip(x, m))
    phalf[0].start()
    ahalf[0].forward()
    for r in range(ROWS):
        atts.wait_recv(r)

    def out_step(n, carry):
        part = jnp.dot(att[...], out_w[:, tile(n)], preferred_element_type=F32)
        part = (part + mid[:, tile(n)]).astype(BF16)
        for r in range(ROWS):
            block_o[r, :, tile(n)] = part[PLANE * r : PLANE * r + COLS]
        return carry

    lax.fori_loop(0, C // 256, out_step, 0)
    edge2.wait_recv()
    conv_backward(gc, edges, hidden, taps, hidden_o, depth, 0, 6)
    phalf[0].forward()

    def put_as1(h, i, value):
        as1[i, pl.ds(2 * h, 2)] = value.astype(BF16)

    ahalf[0].finish(put_as1)
    ahalf[1].start()
    conv_backward(gc, edges, hidden, taps, hidden_o, depth, 6, 12)

    for n in range(12):
        small[n] = depth[0:8, 128 * n : 128 * (n + 1)]
        small[12 + n // 8, n % 8 : n % 8 + 1, :] = depth[8:9, 128 * n : 128 * (n + 1)]
    for n in range(6):
        small[13 + (4 + n) // 8, (4 + n) % 8 : (4 + n) % 8 + 1, :] = gain_part[:, 128 * n : 128 * (n + 1)]
    small[14, 2:8, :] = jnp.zeros((6, 128), F32)
    small[15] = jnp.zeros((8, 128), F32)
    shifts = [(i, j) for i in range(4) for j in range(4)][1:]

    def spot(i, j):
        return lax.rem(x + i, 4) * 4 + lax.rem(zh + j, 4)

    mine = x * 4 + zh
    scatter = Fan(lambda n: small.at[spot(*shifts[n])], lambda n: srecv.at[n], d0s, d0r, plane16)
    spread = Fan(lambda n: ssum, lambda n: sall.at[n], d1s, d1r, others)
    collect = Fan(lambda n: sfinal.at[mine], lambda n: sfinal.at[mine], d2s, d2r, plane16)
    scatter.start()

    def put_ps1(h, i, value):
        ps1[2 * h + i] = value.astype(BF16)

    phalf[0].finish(put_ps1)
    phalf[1].start()
    ahalf[1].forward()
    scatter.wait_recv()
    total = small[mine]
    for n in range(15):
        total = total + srecv[n]
    ssum[...] = total
    spread.start()
    phalf[1].forward()

    def put_as2(h, i, value):
        as2[2 * h + i] = value.astype(BF16)

    ahalf[1].finish(put_as2)
    ahalf[2].start()
    spread.wait_recv()
    total = ssum[...]
    for n in range(15):
        total = total + sall[n]
    sfinal[mine] = total
    collect.start()

    def put_tiles(h, i, value):
        for j in range(4):
            ptile[4 * h + j, :, 0:96] = value[:, 96 * j : 96 * (j + 1)].astype(BF16)

    phalf[1].finish(put_tiles)
    plast = Fan(lambda n: ptile.at[lax.rem(sp + n + 1, 8)], lambda n: precv.at[n], pls, plr, sps)
    plast.start()
    ahalf[2].forward()

    def put_last(h, i, value):
        for low in range(2):
            alast[low, :, 256 * h : 256 + 128 * h] = value[24 * low : 24 * (low + 1)]

    ahalf[2].finish(put_last)
    final = Fan(lambda n: alast.at[1 - zl], lambda n: alrecv, als, alr, [(dp, 2 * y + 1 - zl)])
    final.start()
    plast.wait_recv()
    total = ptile[sp].astype(F32)
    for n in range(7):
        total = total + precv[n].astype(F32)
    proj_o[...] = total[:, 0:96]
    final.wait_recv()
    total = alast[zl] + alrecv[...]
    qkv_o[...] = total[:, 0:288]
    out_o[...] = total[:, 288:384]
    collect.wait_recv()
    for n in range(12):
        depth_o[0:8, 128 * n : 128 * (n + 1)] = sfinal[n]
        depth_o[8:9, 128 * n : 128 * (n + 1)] = sfinal[12 + n // 8, n % 8 : n % 8 + 1, :]
    gains = [sfinal[13 + (4 + n) // 8, (4 + n) % 8 : (4 + n) % 8 + 1, :] for n in range(6)]
    gain_o[...] = jnp.concatenate(gains, axis=1).reshape(C)
    for g in range(ROWS):
        for rows in (cots, norms, gns, atts):
            rows.wait_send(g)
    for one in [edge, edge2, apair, ppair, scatter, spread, collect, plast, final] + ahalf + phalf:
        one.wait_send()


VM = pl.BlockSpec(memory_space=pltpu.VMEM)
ANY = pl.BlockSpec(memory_space=pl.ANY)
DMA = pltpu.SemaphoreType.DMA
MIB = 1024 * 1024


def shape(dims, dtype=BF16):
    return jax.ShapeDtypeStruct(dims, dtype)


def low(*dims):
    return pltpu.VMEM(dims, BF16)


def full(*dims):
    return pltpu.VMEM(dims, F32)


def local(block, hidden, cot, depth_w, proj_w, gain, qkv_w, out_w):
    scratch = [low(ROWS, COLS, C), low(ROWS, COLS, E), low(ROWS, COLS, C), low(E, C), low(C, 3 * C), low(C, C), DMA((6,))]
    scratch += [low(2, COLS, E), full(16, E)] + [low(TOK, C)] * 4 + [full(TOK, C), low(TOK, E), full(TOK, E)]
    scratch += [low(WIN, C), low(WIN, C), low(WIN, 3 * C), low(WIN, C), low(WIN, C), low(WIN, 3 * C), low(C, WIN), low(WIN, C)]
    scratch += [full(C, E)]
    scratch += [low(TOK, C)] * 5 + [low(TOK, E), low(2, PLANE, E), full(16, E)]
    scratch += [
        low(4, 4, 4, 2, 48, 384), low(4, 4, 4, 48, 384), low(4, 4, 4, 48, 384), low(3, 4, 4, 48, 384),
        low(4, 4, 48, 384), low(3, 4, 48, 384), low(4, 48, 384), low(3, 48, 384), full(2, 24, 384), full(24, 384),
    ]
    scratch += [
        low(4, 4, 2, 48, C), low(4, 4, 48, C), low(4, 4, 48, C), low(3, 4, 48, C),
        low(4, 48, C), low(3, 48, C), low(8, 48, 128), low(7, 48, 128),
    ]
    scratch += [full(16, 8, 128), full(15, 8, 128), full(8, 128), full(15, 8, 128), full(16, 8, 128)]
    counts = [2, 2, 7, 7, 7, 7, 7, 7, 7, 7, 2, 2]
    counts += [4, 4, 6, 6, 6, 6, 6, 6, 1, 1]
    counts += [4, 4, 6, 6, 6, 6, 7, 7]
    counts += [15] * 6
    scratch += [DMA((n,)) for n in counts]
    block_o, input_o, hidden_o, depth_o, gain_o, proj_o, qkv_o, out_o = pl.pallas_call(
        section_kernel,
        out_shape=(
            shape((ROWS, COLS, C)), shape((ROWS, COLS, C)), shape((ROWS, COLS, E)),
            shape((9, E), F32), shape((C,), F32),
            shape((48, 96), F32), shape((24, 288), F32), shape((24, 96), F32),
        ),
        in_specs=[ANY] * 6 + [VM] * 2,
        out_specs=(VM,) * 8,
        scratch_shapes=scratch,
        compiler_params=pltpu.CompilerParams(
            collective_id=1, has_side_effects=True, vmem_limit_bytes=63 * MIB
        ),
        name="section",
    )(block[0], hidden[0], cot[0], proj_w, qkv_w, out_w, depth_w, gain)
    return (block_o[None], input_o[None], hidden_o[None], depth_o, gain_o, proj_o, qkv_o, out_o)


def solution(mesh):
    slab = P("dp", "space", None, None)
    part = P("dp", "space")
    return jax.shard_map(
        local,
        mesh=mesh,
        in_specs=(slab, slab, slab, P(), P(), P(), P(), P()),
        out_specs=(slab, slab, slab, P(), P(), part, part, part),
        check_vma=False,
    )
```

```python
import jax
import jax.numpy as jnp
from jax import lax
from jax.experimental import pallas as pl
from jax.experimental.pallas import tpu as pltpu
from jax.sharding import PartitionSpec as P

MESH = pl.DeviceIdType.MESH
F32, BF16 = jnp.float32, jnp.bfloat16
EPS = 1e-05
C, E, HEADS, HD = 768, 1536, 24, 32
ROWS, COLS, PLANE = 7, 56, 64
TOK = ROWS * PLANE
WIN = 512
SCALE = HD ** (-0.5)
XORS = (2, 1, 3, 0)
NT = (((1,), (1,)), ((), ()))
TN = (((0,), (0,)), ((), ()))


def place():
    dp, sp = lax.axis_index("dp"), lax.axis_index("space")
    return dp, sp, lax.div(dp, 8), lax.rem(lax.div(dp, 2), 4), lax.rem(dp, 2)


def dp_of(x, zh, core):
    return (x * 4 + zh) * 2 + core


def greet(ids):
    barrier = pltpu.get_barrier_semaphore()
    for one in ids:
        pl.semaphore_signal(barrier, inc=1, device_id=one, device_id_type=MESH)
    pl.semaphore_wait(barrier, len(ids))


def remote(src, dst, send, recv, to):
    return pltpu.make_async_remote_copy(
        src_ref=src, dst_ref=dst, send_sem=send, recv_sem=recv, device_id=to, device_id_type=MESH
    )


def planes(ref, n):
    return ref.at[pl.ds(pl.multiple_of(n * PLANE, PLANE), PLANE)]


class Rows:
    def __init__(self, src, dst, ssem, rsem, dp, sp, out):
        self.src, self.dst, self.ssem, self.rsem = src, dst, ssem, rsem
        self.dp, self.sp, self.out = dp, sp, out

    def target(self, n):
        if self.out:
            row = self.sp * 7 + n
            return lax.rem(row, 8), lax.div(row, 8)
        row = n * 8 + self.sp
        return lax.div(row, 7), lax.rem(row, 7)

    def copies(self, n):
        to, slot = self.target(n)
        src, dst = planes(self.src, n), planes(self.dst, slot)
        far = remote(src, dst, self.ssem.at[n], self.rsem.at[slot], (self.dp, to))
        near = pltpu.make_async_copy(src, dst, self.rsem.at[slot])
        return to, far, near

    def start(self, n):
        to, far, near = self.copies(n)

        @pl.when(to != self.sp)
        def _():
            far.start()

        @pl.when(to == self.sp)
        def _():
            near.start()

    def wait_recv(self, n):
        one = planes(self.dst, n)
        pltpu.make_async_copy(one, one, self.rsem.at[n]).wait()

    def wait_send(self, n):
        to, far, _ = self.copies(n)

        @pl.when(to != self.sp)
        def _():
            far.wait_send()


class Halo:
    def __init__(self, top, bottom, halo, ssem, rsem, dp, sp):
        self.sp = sp
        self.up = remote(top, halo.at[1], ssem.at[0], rsem.at[1], (dp, jnp.maximum(sp - 1, 0)))
        self.down = remote(bottom, halo.at[0], ssem.at[1], rsem.at[0], (dp, jnp.minimum(sp + 1, 7)))
        self.halo = halo

    def start(self):
        @pl.when(self.sp > 0)
        def _():
            self.up.start()

        @pl.when(self.sp < 7)
        def _():
            self.down.start()

        zero = jnp.zeros(self.halo.shape[1:], self.halo.dtype)

        @pl.when(self.sp == 0)
        def _():
            self.halo[0] = zero

        @pl.when(self.sp == 7)
        def _():
            self.halo[1] = zero

    def wait_recv(self):
        @pl.when(self.sp > 0)
        def _():
            self.down.wait_recv()

        @pl.when(self.sp < 7)
        def _():
            self.up.wait_recv()

    def wait_send(self):
        @pl.when(self.sp > 0)
        def _():
            self.up.wait_send()

        @pl.when(self.sp < 7)
        def _():
            self.down.wait_send()


def col_masks(lanes):
    index = lax.broadcasted_iota(jnp.int32, (COLS, lanes), 0)
    return index == 0, index == COLS - 1


def later(value, first):
    return jnp.where(first, 0.0, pltpu.roll(value, 1, 0))


def earlier(value, last):
    return jnp.where(last, 0.0, pltpu.roll(value, COLS - 1, 0))


def padded(value):
    return jnp.concatenate([value, jnp.zeros((PLANE - COLS, value.shape[1]), F32)], axis=0)


def gelu_and_slope(value):
    k0, k1 = 0.7978845608028654, 0.044715
    square = value * value
    tanh = jnp.tanh(k0 * value * (1.0 + k1 * square))
    half = 0.5 * (1.0 + tanh)
    slope = half + 0.5 * value * (1.0 - tanh * tanh) * (k0 * (1.0 + 3.0 * k1 * square))
    return value * half, slope


def conv_forward(hidden, halo, taps, act, slope, begin, end):
    def chunk(n, carry):
        lanes = pl.ds(pl.multiple_of(n * 128, 128), 128)
        first, last = col_masks(128)
        rows = {}
        for r in range(begin - 1, end + 1):
            if r < 0:
                rows[r] = halo[0, :, lanes].astype(F32)
            elif r == ROWS:
                rows[r] = halo[1, :, lanes].astype(F32)
            else:
                rows[r] = hidden[r, :, lanes].astype(F32)
        tap = [taps[t : t + 1, lanes] for t in range(9)]
        for r in range(begin, end):
            part = [sum(tap[3 * a + b] * rows[r + a - 1] for a in range(3)) for b in range(3)]
            conv = later(part[0], first) + part[1] + earlier(part[2], last)
            low, grad = gelu_and_slope(conv)
            act[PLANE * r : PLANE * (r + 1), lanes] = padded(low).astype(BF16)
            slope[PLANE * r : PLANE * (r + 1), lanes] = padded(grad)
        return carry

    lax.fori_loop(0, E // 128, chunk, 0)


def normal(mid):
    mean = jnp.mean(mid, axis=1, keepdims=True)
    centred = mid - mean
    inv = lax.rsqrt(jnp.mean(centred * centred, axis=1, keepdims=True) + EPS)
    return centred * inv, inv


def window_place(index):
    win, n = index >> 6, index & 63
    g = (n * 37) >> 8
    return jnp.where(n < 49, g * PLANE + (n - 7 * g) * 8 + win, -1)


def head_tools():
    lane = lax.broadcasted_iota(jnp.int32, (64, 128), 1) >> 5
    big = lax.broadcasted_iota(jnp.int32, (256, 128), 0) >> 6
    own = (big == (lax.broadcasted_iota(jnp.int32, (256, 128), 1) >> 5)).astype(F32).astype(BF16)

    def spread(value):
        return jnp.concatenate([value] * 4, axis=0) * own

    def gather(value):
        return jnp.where(
            lane < 2,
            jnp.where(lane == 0, value[0:64], value[64:128]),
            jnp.where(lane == 2, value[128:192], value[192:256]),
        )

    return spread, gather


def heads(part, g):
    return slice(part * C + 128 * g, part * C + 128 * (g + 1))


def attend(qkv, probs, att):
    spread, gather = head_tools()
    valid = lax.broadcasted_iota(jnp.int32, (64, 256), 0) < 49

    def window(w, carry):
        rows = pl.ds(pl.multiple_of(w * 64, 64), 64)
        for g in range(6):
            query, key, value = (qkv[rows, heads(part, g)] for part in range(3))
            score = lax.dot_general(key, spread(query), NT, preferred_element_type=F32) * SCALE
            score = jnp.where(valid, score, -1e30)
            power = jnp.exp(score - jnp.max(score, axis=0, keepdims=True))
            prob = power * (1.0 / jnp.sum(power, axis=0, keepdims=True))
            probs[g, rows] = prob
            att[rows, heads(0, g)] = gather(
                lax.dot_general(prob.astype(BF16), value, TN, preferred_element_type=F32)
            ).astype(BF16)
        return carry

    lax.fori_loop(0, 8, window, 0)


def attend_back(qkv, gatt, probs, gqkv, groups):
    spread, gather = head_tools()

    def window(pair, carry):
        for w in range(2):
            rows = pl.ds(pl.multiple_of(pair * 128 + 64 * w, 64), 64)
            for g in groups:
                query, key, value = (qkv[rows, heads(part, g)] for part in range(3))
                query = spread(query)
                grad = spread(gatt[rows, heads(0, g)])
                prob = probs[g, rows]
                low = prob.astype(BF16)
                grad_prob = lax.dot_general(value, grad, NT, preferred_element_type=F32)
                inner = jnp.sum(grad_prob * prob, axis=0, keepdims=True)
                grad_low = (prob * (grad_prob - inner) * SCALE).astype(BF16)
                gqkv[rows, heads(0, g)] = gather(
                    lax.dot_general(grad_low, key, TN, preferred_element_type=F32)
                ).astype(BF16)
                gqkv[rows, heads(1, g)] = jnp.dot(
                    grad_low, query, preferred_element_type=F32
                ).astype(BF16)
                gqkv[rows, heads(2, g)] = jnp.dot(low, grad, preferred_element_type=F32).astype(BF16)
        return carry

    lax.fori_loop(0, 4, window, 0)


def half_rows(value):
    left, right = (value[:, 128 * h : 128 * (h + 1)].reshape(32, 24, 128) for h in range(2))
    return jnp.concatenate([left, right], axis=1).reshape(4, 4, 2, 48, 128).astype(BF16)


def flip(q, mask):
    if mask == 0:
        return q
    if mask == 1:
        return q + 1 - 2 * lax.rem(q, 2)
    if mask == 3:
        return 3 - q
    return lax.rem(q + 2, 4)


class Pair:
    def __init__(self, grads, recv, ssem, rsem, core, peer):
        self.grads, self.recv, self.core = grads, recv, core
        self.ssem, self.rsem, self.peer = ssem, rsem, peer
        self.begun = []

    def copy(self, q):
        return remote(
            self.grads.at[q, :, 1 - self.core], self.recv.at[q], self.ssem.at[q], self.rsem.at[q], self.peer
        )

    def start(self, q):
        self.copy(q).start()

    def add(self, q, put):
        self.copy(q).wait_recv()

        def body(i, carry):
            mine = self.grads[q, i, self.core].astype(F32)
            put(q, i, (mine + self.recv[q, i].astype(F32)).astype(BF16))
            return carry

        lax.fori_loop(0, 4, body, 0)

    def wait_send(self):
        for q in range(4):
            self.copy(q).wait_send()


class Whole(Pair):
    def copy(self, q=0):
        return remote(self.grads.at[:, :, 1 - self.core], self.recv, self.ssem, self.rsem, self.peer)

    def add(self, put):
        self.copy().wait_recv()

        def body(i, carry):
            q, j = lax.div(i, 4), lax.rem(i, 4)
            mine = self.grads[q, j, self.core].astype(F32)
            put(q, j, (mine + self.recv[q, j].astype(F32)).astype(BF16))
            return carry

        lax.fori_loop(0, 16, body, 0)

    def wait_send(self):
        self.copy().wait_send()


class Halve:
    def __init__(self, src, recv, ssem, rsem, q, peers, view, piece, count):
        self.src, self.recv, self.q, self.view, self.piece, self.count = src, recv, q, view, piece, count
        self.cps = {}
        for h in range(2):
            near, far = (1, 3) if h == 0 else (3, 1)
            for slot, (block, to) in enumerate(((near, near), (2, near), (far, far))):
                n = 3 * h + slot
                self.cps[h, slot] = remote(
                    src.at[view(flip(q, block), h)], recv.at[view(slot, h)], ssem.at[n], rsem.at[n], peers[to]
                )

    def start(self):
        for slot in (1, 0):
            for h in range(2):
                self.cps[h, slot].start()

    def forward(self):
        for h in range(2):
            self.cps[h, 1].wait_recv()
            block = flip(self.q, 3 if h == 0 else 1)

            def body(i, carry, h=h, block=block):
                mine = self.src[self.piece(block, h, i)].astype(F32)
                mine = mine + self.recv[self.piece(1, h, i)].astype(F32)
                self.src[self.piece(block, h, i)] = mine.astype(BF16)
                return carry

            lax.fori_loop(0, self.count, body, 0)
            self.cps[h, 2].start()

    def finish(self, put):
        for h in range(2):
            self.cps[h, 0].wait_recv()
            self.cps[h, 2].wait_recv()

            def body(i, carry, h=h):
                mine = self.src[self.piece(self.q, h, i)].astype(F32)
                mine = mine + self.recv[self.piece(0, h, i)].astype(F32)
                put(h, i, mine + self.recv[self.piece(2, h, i)].astype(F32))
                return carry

            lax.fori_loop(0, self.count, body, 0)

    def wait_send(self):
        for cp in self.cps.values():
            cp.wait_send()


class Fan:
    def __init__(self, pieces, recvs, ssem, rsem, peers):
        self.cps = [
            remote(pieces(n), recvs(n), ssem.at[n], rsem.at[n], peer) for n, peer in enumerate(peers)
        ]

    def start(self):
        for cp in self.cps:
            cp.start()

    def wait_recv(self):
        for cp in self.cps:
            cp.wait_recv()

    def wait_send(self):
        for cp in self.cps:
            cp.wait_send()


def conv_backward(grad, halo, hidden, taps, hidden_grad, depth, begin, end):
    def chunk(n, carry):
        lanes = pl.ds(pl.multiple_of(n * 128, 128), 128)
        first, last = col_masks(128)
        rows = [halo[0, 0:COLS, lanes].astype(F32)]
        rows += [grad[PLANE * r : PLANE * r + COLS, lanes].astype(F32) for r in range(ROWS)]
        rows += [halo[1, 0:COLS, lanes].astype(F32)]
        tap = [taps[t : t + 1, lanes] for t in range(9)]
        sums = [jnp.zeros((8, 128), F32) for _ in range(9)]
        for r in range(ROWS):
            near = [rows[r + 2 - a] for a in range(3)]
            part = [sum(tap[3 * a + b] * near[a] for a in range(3)) for b in range(3)]
            total = earlier(part[0], last) + part[1] + later(part[2], first)
            hidden_grad[r, :, lanes] = total.astype(BF16)
            own = hidden[r, :, lanes].astype(F32)
            moved = [later(own, first), own, earlier(own, last)]
            for a in range(3):
                for b in range(3):
                    product = moved[b] * near[a]
                    for i in range(7):
                        sums[3 * a + b] = sums[3 * a + b] + product[8 * i : 8 * i + 8]
        for t in range(9):
            depth[t : t + 1, lanes] = jnp.sum(sums[t], axis=0, keepdims=True)
        return carry

    lax.fori_loop(begin, end, chunk, 0)


def tile(n, width=256):
    return pl.ds(pl.multiple_of(n * width, width), width)


def section_kernel(
    block_h, hidden_h, cot_h, proj_h, qkv_h, out_h, depth_w, gain,
    block_o, input_o, hidden_o, depth_o, gain_o, proj_o, qkv_o, out_o,
    block, hidden, cot, proj_w, qkv_w, out_w, loads,
    halo, taps, own_n, own_c, win_n, win_c, mid, act, slope,
    norm_p, cot_p, qkv, gatt, att_p, gqkv, turned, turned2, gn_p, probs,
    att_w, gn_w, att, gn, ig, gc, edges, depth,
    agrads, ar0, as0, arx, as1, arz, atot, arow, atile, arecv,
    pgrads, pr0, ps0, prx, ps1, prz, qs0, qrz, qs1, qrx, ptot, ptile, precv,
    small, srecv, ssum, sall, sfinal,
    hs, hr, ns, nr, cs, cr, ts, tr, us, ur, es, er,
    a0s, a0r, axs, axr, azs, azr, als, alr,
    p0s, p0r, pxs, pxr, pzs, pzr, qzs, qzr, qxs, qxr, pls, plr,
    d0s, d0r, d1s, d1r, d2s, d2r,
):
    dp, sp, x, zh, core = place()
    pulls = {}
    pairs = ((hidden_h, hidden), (cot_h, cot), (proj_h, proj_w), (block_h, block), (out_h, out_w), (qkv_h, qkv_w))
    for n, (src, dst) in enumerate(pairs):
        pulls[n] = pltpu.make_async_copy(src, dst, loads.at[n])
        pulls[n].start()
    pair = (dp_of(x, zh, 1 - core), sp)
    plane16 = [(dp_of(lax.rem(x + i, 4), lax.rem(zh + j, 4), core), sp) for i in range(4) for j in range(4)][1:]
    sps = [(dp, lax.rem(sp + j, 8)) for j in range(1, 8)]
    others = sps + [(dp_of(x, zh, 1 - core), lax.rem(sp + j, 8)) for j in range(8)]
    greet(plane16 + others)
    xp = {m: (dp_of(flip(x, m), zh, core), sp) for m in (1, 3)}
    zp = {m: (dp_of(x, flip(zh, m), core), sp) for m in (1, 3)}

    edge = Halo(hidden_h.at[0], hidden_h.at[ROWS - 1], halo, hs, hr, dp, sp)
    edge.start()
    cots = Rows(own_c, win_c, cs, cr, dp, sp, True)
    norms = Rows(own_n, win_n, ns, nr, dp, sp, True)
    pulls[1].wait()
    for r in range(ROWS):
        own_c[PLANE * r : PLANE * (r + 1)] = padded(cot[r].astype(F32)).astype(BF16)
        cots.start(r)
    taps[0:9] = depth_w[...].astype(F32)
    scale = gain[...].reshape(1, C)
    pulls[0].wait()
    edge.wait_recv()
    for begin, end in ((0, 4), (4, 7)):
        conv_forward(hidden, halo, taps, act, slope, begin, end)
        if begin == 0:
            pulls[2].wait()
            pulls[3].wait()
        span = slice(PLANE * begin, PLANE * end)

        def proj(n, carry, span=span):
            mid[span, tile(n)] = jnp.dot(act[span, :], proj_w[:, tile(n)], preferred_element_type=F32)
            return carry

        lax.fori_loop(0, C // 256, proj, 0)

        def norm(r, carry):
            here = tile(r, PLANE)
            total = mid[here, :] + padded(block[r].astype(F32))
            mid[here, :] = total
            own_n[here, :] = (normal(total)[0] * scale).astype(BF16)
            norms.start(r)
            return carry

        lax.fori_loop(begin, end, norm, 0)

    index = window_place(lax.broadcasted_iota(jnp.int32, (WIN, 1), 0))
    tokens = lax.broadcasted_iota(jnp.int32, (WIN, TOK), 1)
    perm = (index == tokens).astype(F32).astype(BF16)
    for r in range(ROWS):
        cots.wait_recv(r)
    cot_p[...] = jnp.dot(perm, win_c[...], preferred_element_type=F32).astype(BF16)
    pulls[4].wait()

    def gatt_step(n, carry):
        gatt[:, tile(n)] = lax.dot_general(
            cot_p[...], out_w[tile(n), :], NT, preferred_element_type=F32
        ).astype(BF16)
        return carry

    lax.fori_loop(0, 3, gatt_step, 0)
    for r in range(ROWS):
        norms.wait_recv(r)
    norm_p[...] = jnp.dot(perm, win_n[...], preferred_element_type=F32).astype(BF16)
    pulls[5].wait()

    def qkv_step(n, carry):
        qkv[:, tile(n)] = jnp.dot(
            norm_p[...], qkv_w[:, tile(n)], preferred_element_type=F32
        ).astype(BF16)
        return carry

    lax.fori_loop(0, 9, qkv_step, 0)
    turned[...] = norm_p[...].T
    attend(qkv, probs, att_p)

    ring = lambda q, h: (q, pl.ds(2 * h, 2))
    ring_piece = lambda q, h, i: (q, 2 * h + i)
    line = lambda q, h: (q, slice(None), slice(256 * h, 256 + 128 * h))
    line_piece = lambda q, h, i: line(q, h)

    class Chunk:
        def __init__(self, c):
            self.c = c
            self.pair = Whole(agrads.at[c], ar0.at[c], a0s.at[c], a0r.at[c], core, pair)
            six = pl.ds(6 * c, 6)
            self.first = Halve(
                as0.at[c], arx.at[c], axs.at[six], axr.at[six], x, xp, ring, ring_piece, 2
            )
            self.second = Halve(
                as1.at[c], arz.at[c], azs.at[six], azr.at[six], zh, zp, line, line_piece, 1
            )

        def put0(self, q, i, value):
            as0[self.c, q, i] = value

        def put1(self, h, i, value):
            as1[self.c, 2 * h + i] = value.astype(BF16)

        def put2(self, h, i, value):
            atot[self.c, :, 256 * h : 256 + 128 * h] = value

        def step(self, n):
            if n == 0:
                self.pair.start(0)
            elif n == 1:
                self.pair.add(self.put0)
                self.first.start()
            elif n == 2:
                self.first.forward()
            elif n == 3:
                self.first.finish(self.put1)
                self.second.start()
            elif n == 4:
                self.second.forward()
            elif n == 5:
                self.second.finish(self.put2)

        def wait_send(self):
            for one in (self.pair, self.first, self.second):
                one.wait_send()

    chunks = [Chunk(c) for c in range(4)]

    def advance(slot):
        for c in range(4):
            if 0 <= slot - c <= 5:
                chunks[c].step(slot - c)

    turned2[...] = att_p[...].T

    def out_grad_step(n, carry):
        right = jnp.concatenate([cot_p[:, tile(n, 128)], cot_p[:, tile(n + 3, 128)]], axis=1)
        agrads[0, :, :, :, :, tile(n, 128)] = half_rows(
            jnp.dot(turned2[...], right, preferred_element_type=F32)
        )
        return carry

    lax.fori_loop(0, 3, out_grad_step, 0)
    advance(0)
    index = window_place(lax.broadcasted_iota(jnp.int32, (1, WIN), 1))
    tokens = lax.broadcasted_iota(jnp.int32, (TOK, WIN), 0)
    back = (index == tokens).astype(F32).astype(BF16)
    gns = Rows(gn_w, gn, us, ur, dp, sp, False)
    atts = Rows(att_w, att, ts, tr, dp, sp, False)
    att_w[...] = jnp.dot(back, att_p[...], preferred_element_type=F32).astype(BF16)
    for g in range(ROWS):
        atts.start(g)
    for c in range(1, 4):
        attend_back(qkv, gatt, probs, gqkv, (2 * c - 2, 2 * c - 1))
        if c == 3:

            def gn_step(n, carry):
                gn_p[:, tile(n)] = lax.dot_general(
                    gqkv[...], qkv_w[tile(n), :], NT, preferred_element_type=F32
                ).astype(BF16)
                return carry

            lax.fori_loop(0, 3, gn_step, 0)
            gn_w[...] = jnp.dot(back, gn_p[...], preferred_element_type=F32).astype(BF16)
            for g in range(ROWS):
                gns.start(g)

        def grad_step(n, carry, c=c):
            right = gqkv[:, pl.ds(pl.multiple_of(768 * n + 256 * (c - 1), 256), 256)]
            agrads[c, :, :, :, :, tile(n, 128)] = half_rows(
                jnp.dot(turned[...], right, preferred_element_type=F32)
            )
            return carry

        lax.fori_loop(0, 3, grad_step, 0)
        advance(c)
    for r in range(ROWS):
        atts.wait_recv(r)

    def out_step(n, carry):
        part = jnp.dot(att[...], out_w[:, tile(n)], preferred_element_type=F32)
        part = (part + mid[:, tile(n)]).astype(BF16)
        for r in range(ROWS):
            block_o[r, :, tile(n)] = part[PLANE * r : PLANE * r + COLS]
        return carry

    lax.fori_loop(0, C // 256, out_step, 0)

    for r in range(ROWS):
        gns.wait_recv(r)

    def norm_step(r, carry):
        here = tile(r, PLANE)
        hat, inv = normal(mid[here, :])
        grad = gn[here, :].astype(F32)
        grad_hat = grad * scale
        carry = carry + (grad * hat).reshape(8, 8, C).sum(axis=0)
        inner = jnp.mean(grad_hat * hat, axis=1, keepdims=True)
        mean = jnp.mean(grad_hat, axis=1, keepdims=True)
        cotangent = padded(cot[r].astype(F32))
        low = (cotangent + inv * (grad_hat - mean - hat * inner)).astype(BF16)
        ig[here, :] = low
        input_o[r] = low[0:COLS]
        return carry

    gain_part = lax.fori_loop(0, ROWS, norm_step, jnp.zeros((8, C), F32))
    gain_part = jnp.sum(gain_part, axis=0, keepdims=True)
    advance(4)

    ppair = Pair(pgrads, pr0, p0s, p0r, core, pair)
    ends = lambda width: (
        lambda q, h: (q, slice(None), slice(width * h, width * (h + 1))),
        lambda q, h, i: (q, slice(None), slice(width * h, width * (h + 1))),
    )
    px = Halve(ps0, prx, pxs, pxr, x, xp, ring, ring_piece, 2)
    pz = Halve(ps1, prz, pzs, pzr, zh, zp, *ends(256), 1)
    qz = Halve(qs0, qrz, qzs, qzr, zh, zp, ring, ring_piece, 2)
    qx = Halve(qs1, qrx, qxs, qxr, x, xp, *ends(128), 1)

    def put_p0(q, i, value):
        ps0[q, i] = value[:, 0:512]
        qs0[i, q] = value[:, 512:768]

    def put_ps1(h, i, value):
        ps1[2 * h + i] = value.astype(BF16)

    def put_qs1(h, i, value):
        qs1[2 * h + i] = value.astype(BF16)

    def put_p2(h, i, value):
        ptot[:, 256 * h : 256 * (h + 1)] = value

    def put_q2(h, i, value):
        ptot[:, 512 + 128 * h : 512 + 128 * (h + 1)] = value

    for m in XORS:
        xx = flip(x, m)
        turned2[0:384, 0:TOK] = act[:, pl.ds(pl.multiple_of(xx * 384, 128), 384)].T

        def proj_step(n, carry, xx=xx):
            part = jnp.dot(turned2[0:384, 0:TOK], ig[:, tile(n)], preferred_element_type=F32)
            pgrads[xx, :, :, :, tile(n)] = part.reshape(4, 2, 48, 256).astype(BF16)
            return carry

        lax.fori_loop(0, 3, proj_step, 0)
        ppair.start(xx)

    advance(5)

    def act_step(n, carry):
        part = lax.dot_general(ig[...], proj_w[tile(n), :], NT, preferred_element_type=F32)
        gc[:, tile(n)] = (part * slope[:, tile(n)]).astype(BF16)
        return carry

    lax.fori_loop(0, E // 256, act_step, 0)
    edge2 = Halo(gc.at[0:PLANE], gc.at[TOK - PLANE : TOK], edges, es, er, dp, sp)
    edge2.start()
    for m in XORS:
        ppair.add(flip(x, m), put_p0)
    px.start()
    qz.start()
    advance(6)
    edge2.wait_recv()
    conv_backward(gc, edges, hidden, taps, hidden_o, depth, 0, 6)
    px.forward()
    qz.forward()
    advance(7)
    conv_backward(gc, edges, hidden, taps, hidden_o, depth, 6, 12)

    for n in range(12):
        small[n] = depth[0:8, 128 * n : 128 * (n + 1)]
        small[12 + n // 8, n % 8 : n % 8 + 1, :] = depth[8:9, 128 * n : 128 * (n + 1)]
    for n in range(6):
        small[13 + (4 + n) // 8, (4 + n) % 8 : (4 + n) % 8 + 1, :] = gain_part[:, 128 * n : 128 * (n + 1)]
    small[14, 2:8, :] = jnp.zeros((6, 128), F32)
    small[15] = jnp.zeros((8, 128), F32)
    shifts = [(i, j) for i in range(4) for j in range(4)][1:]

    def spot(i, j):
        return lax.rem(x + i, 4) * 4 + lax.rem(zh + j, 4)

    mine = x * 4 + zh
    scatter = Fan(lambda n: small.at[spot(*shifts[n])], lambda n: srecv.at[n], d0s, d0r, plane16)
    spread = Fan(lambda n: ssum, lambda n: sall.at[n], d1s, d1r, others)
    collect = Fan(lambda n: sfinal.at[mine], lambda n: sfinal.at[mine], d2s, d2r, plane16)
    scatter.start()
    px.finish(put_ps1)
    pz.start()
    qz.finish(put_qs1)
    qx.start()
    advance(8)
    for hh in range(2):
        rows = slice(24 * hh, 24 * (hh + 1))
        arow[:, 2304 + 384 * hh : 2304 + 384 * (hh + 1)] = atot[0, rows, :]
        for c in range(1, 4):
            for part in range(3):
                begin = C * part + 256 * (c - 1) + 128 * hh
                arow[:, begin : begin + 128] = atot[c, rows, 128 * part : 128 * (part + 1)]
    blank = jnp.zeros((8, 384), F32)
    for j in range(8):
        left = arow[:, 288 * j : 288 * (j + 1)]
        right = arow[:, 2304 + 96 * j : 2304 + 96 * (j + 1)]
        value = jnp.concatenate([jnp.concatenate([left, right], axis=1), blank], axis=0)
        atile[j] = value.astype(BF16)
    alast = Fan(lambda n: atile.at[lax.rem(sp + n + 1, 8)], lambda n: arecv.at[n], als, alr, sps)
    alast.start()
    scatter.wait_recv()
    total = small[mine]
    for n in range(15):
        total = total + srecv[n]
    ssum[...] = total
    spread.start()
    pz.forward()
    qx.forward()
    spread.wait_recv()
    total = ssum[...]
    for n in range(15):
        total = total + sall[n]
    sfinal[mine] = total
    collect.start()
    qx.finish(put_q2)
    pz.finish(put_p2)
    for j in range(8):
        ptile[j, :, 0:96] = ptot[:, 96 * j : 96 * (j + 1)].astype(BF16)
    plast = Fan(lambda n: ptile.at[lax.rem(sp + n + 1, 8)], lambda n: precv.at[n], pls, plr, sps)
    plast.start()
    alast.wait_recv()
    total = atile[sp].astype(F32)
    for n in range(7):
        total = total + arecv[n].astype(F32)
    qkv_o[...] = total[0:24, 0:288]
    out_o[...] = total[0:24, 288:384]
    collect.wait_recv()
    for n in range(12):
        depth_o[0:8, 128 * n : 128 * (n + 1)] = sfinal[n]
        depth_o[8:9, 128 * n : 128 * (n + 1)] = sfinal[12 + n // 8, n % 8 : n % 8 + 1, :]
    gains = [sfinal[13 + (4 + n) // 8, (4 + n) % 8 : (4 + n) % 8 + 1, :] for n in range(6)]
    gain_o[...] = jnp.concatenate(gains, axis=1).reshape(C)
    plast.wait_recv()
    total = ptile[sp].astype(F32)
    for n in range(7):
        total = total + precv[n].astype(F32)
    proj_o[...] = total[:, 0:96]
    for g in range(ROWS):
        for rows in (cots, norms, gns, atts):
            rows.wait_send(g)
    for one in [edge, edge2, ppair, px, pz, qx, qz, scatter, spread, collect, plast, alast] + chunks:
        one.wait_send()


VM = pl.BlockSpec(memory_space=pltpu.VMEM)
ANY = pl.BlockSpec(memory_space=pl.ANY)
DMA = pltpu.SemaphoreType.DMA
MIB = 1024 * 1024


def shape(dims, dtype=BF16):
    return jax.ShapeDtypeStruct(dims, dtype)


def low(*dims):
    return pltpu.VMEM(dims, BF16)


def full(*dims):
    return pltpu.VMEM(dims, F32)


def local(block, hidden, cot, depth_w, proj_w, gain, qkv_w, out_w):
    scratch = [low(ROWS, COLS, C), low(ROWS, COLS, E), low(ROWS, COLS, C), low(E, C), low(C, 3 * C), low(C, C), DMA((6,))]
    scratch += [low(2, COLS, E), full(16, E)] + [low(TOK, C)] * 4 + [full(TOK, C), low(TOK, E), full(TOK, E)]
    scratch += [low(WIN, C), low(WIN, C), low(WIN, 3 * C), low(WIN, C), low(WIN, C), low(WIN, 3 * C), low(C, WIN), low(C, WIN), low(WIN, C)]
    scratch += [full(6, WIN, 256)]
    scratch += [low(TOK, C)] * 5 + [low(TOK, E), low(2, PLANE, E), full(16, E)]
    scratch += [
        low(4, 4, 4, 2, 48, 384), low(4, 4, 4, 48, 384), low(4, 4, 4, 48, 384), low(4, 3, 4, 48, 384),
        low(4, 4, 48, 384), low(4, 3, 48, 384), full(4, 48, 384), full(24, 4 * C), low(8, 32, 384), low(7, 32, 384),
    ]
    scratch += [
        low(4, 4, 2, 48, C), low(4, 4, 48, C), low(4, 4, 48, 512), low(3, 4, 48, 512), low(4, 48, 512), low(3, 48, 512),
        low(4, 4, 48, 256), low(3, 4, 48, 256), low(4, 48, 256), low(3, 48, 256),
        full(48, C), low(8, 48, 128), low(7, 48, 128),
    ]
    scratch += [full(16, 8, 128), full(15, 8, 128), full(8, 128), full(15, 8, 128), full(16, 8, 128)]
    counts = [2, 2, 7, 7, 7, 7, 7, 7, 7, 7, 2, 2]
    counts += [4, 4, 24, 24, 24, 24, 7, 7]
    counts += [4, 4, 6, 6, 6, 6, 6, 6, 6, 6, 7, 7]
    counts += [15] * 6
    scratch += [DMA((n,)) for n in counts]
    block_o, input_o, hidden_o, depth_o, gain_o, proj_o, qkv_o, out_o = pl.pallas_call(
        section_kernel,
        out_shape=(
            shape((ROWS, COLS, C)), shape((ROWS, COLS, C)), shape((ROWS, COLS, E)),
            shape((9, E), F32), shape((C,), F32),
            shape((48, 96), F32), shape((24, 288), F32), shape((24, 96), F32),
        ),
        in_specs=[ANY] * 6 + [VM] * 2,
        out_specs=(VM,) * 8,
        scratch_shapes=scratch,
        compiler_params=pltpu.CompilerParams(
            collective_id=1, has_side_effects=True, vmem_limit_bytes=63 * MIB
        ),
        name="section",
    )(block[0], hidden[0], cot[0], proj_w, qkv_w, out_w, depth_w, gain)
    return (block_o[None], input_o[None], hidden_o[None], depth_o, gain_o, proj_o, qkv_o, out_o)


def solution(mesh):
    slab = P("dp", "space", None, None)
    part = P("dp", "space")
    return jax.shard_map(
        local,
        mesh=mesh,
        in_specs=(slab, slab, slab, P(), P(), P(), P(), P()),
        out_specs=(slab, slab, slab, P(), P(), part, part, part),
        check_vma=False,
    )
```

```python
import jax
import jax.numpy as jnp
from jax import lax
from jax.experimental import pallas as pl
from jax.experimental.pallas import tpu as pltpu
from jax.sharding import PartitionSpec as P

MESH = pl.DeviceIdType.MESH
F32, BF16 = jnp.float32, jnp.bfloat16
EPS = 1e-05
C, E, HEADS, HD = 768, 1536, 24, 32
ROWS, COLS, PLANE = 7, 56, 64
TOK = ROWS * PLANE
WIN = 512
SCALE = HD ** (-0.5)
XORS = (2, 1, 3, 0)
NT = (((1,), (1,)), ((), ()))
TN = (((0,), (0,)), ((), ()))


def place():
    dp, sp = lax.axis_index("dp"), lax.axis_index("space")
    return dp, sp, lax.div(dp, 8), lax.rem(lax.div(dp, 2), 4), lax.rem(dp, 2)


def dp_of(x, zh, core):
    return (x * 4 + zh) * 2 + core


def greet(ids):
    barrier = pltpu.get_barrier_semaphore()
    for one in ids:
        pl.semaphore_signal(barrier, inc=1, device_id=one, device_id_type=MESH)
    pl.semaphore_wait(barrier, len(ids))


def remote(src, dst, send, recv, to):
    return pltpu.make_async_remote_copy(
        src_ref=src, dst_ref=dst, send_sem=send, recv_sem=recv, device_id=to, device_id_type=MESH
    )


def planes(ref, n):
    return ref.at[pl.ds(pl.multiple_of(n * PLANE, PLANE), PLANE)]


class Rows:
    def __init__(self, src, dst, ssem, rsem, dp, sp, out):
        self.src, self.dst, self.ssem, self.rsem = src, dst, ssem, rsem
        self.dp, self.sp, self.out = dp, sp, out

    def target(self, n):
        if self.out:
            row = self.sp * 7 + n
            return lax.rem(row, 8), lax.div(row, 8)
        row = n * 8 + self.sp
        return lax.div(row, 7), lax.rem(row, 7)

    def copies(self, n):
        to, slot = self.target(n)
        src, dst = planes(self.src, n), planes(self.dst, slot)
        far = remote(src, dst, self.ssem.at[n], self.rsem.at[slot], (self.dp, to))
        near = pltpu.make_async_copy(src, dst, self.rsem.at[slot])
        return to, far, near

    def start(self, n):
        to, far, near = self.copies(n)

        @pl.when(to != self.sp)
        def _():
            far.start()

        @pl.when(to == self.sp)
        def _():
            near.start()

    def wait_recv(self, n):
        one = planes(self.dst, n)
        pltpu.make_async_copy(one, one, self.rsem.at[n]).wait()

    def wait_send(self, n):
        to, far, _ = self.copies(n)

        @pl.when(to != self.sp)
        def _():
            far.wait_send()


class Halo:
    def __init__(self, top, bottom, halo, ssem, rsem, dp, sp):
        self.sp = sp
        self.up = remote(top, halo.at[1], ssem.at[0], rsem.at[1], (dp, jnp.maximum(sp - 1, 0)))
        self.down = remote(bottom, halo.at[0], ssem.at[1], rsem.at[0], (dp, jnp.minimum(sp + 1, 7)))
        self.halo = halo

    def start(self):
        @pl.when(self.sp > 0)
        def _():
            self.up.start()

        @pl.when(self.sp < 7)
        def _():
            self.down.start()

        zero = jnp.zeros(self.halo.shape[1:], self.halo.dtype)

        @pl.when(self.sp == 0)
        def _():
            self.halo[0] = zero

        @pl.when(self.sp == 7)
        def _():
            self.halo[1] = zero

    def wait_recv(self):
        @pl.when(self.sp > 0)
        def _():
            self.down.wait_recv()

        @pl.when(self.sp < 7)
        def _():
            self.up.wait_recv()

    def wait_send(self):
        @pl.when(self.sp > 0)
        def _():
            self.up.wait_send()

        @pl.when(self.sp < 7)
        def _():
            self.down.wait_send()


def col_masks(lanes):
    index = lax.broadcasted_iota(jnp.int32, (COLS, lanes), 0)
    return index == 0, index == COLS - 1


def later(value, first):
    return jnp.where(first, 0.0, pltpu.roll(value, 1, 0))


def earlier(value, last):
    return jnp.where(last, 0.0, pltpu.roll(value, COLS - 1, 0))


def padded(value):
    return jnp.concatenate([value, jnp.zeros((PLANE - COLS, value.shape[1]), F32)], axis=0)


def gelu_and_slope(value):
    k0, k1 = 0.7978845608028654, 0.044715
    square = value * value
    tanh = jnp.tanh(k0 * value * (1.0 + k1 * square))
    half = 0.5 * (1.0 + tanh)
    slope = half + 0.5 * value * (1.0 - tanh * tanh) * (k0 * (1.0 + 3.0 * k1 * square))
    return value * half, slope


def conv_forward(hidden, halo, taps, act, slope, begin, end):
    def chunk(n, carry):
        lanes = pl.ds(pl.multiple_of(n * 128, 128), 128)
        first, last = col_masks(128)
        rows = {}
        for r in range(begin - 1, end + 1):
            if r < 0:
                rows[r] = halo[0, :, lanes].astype(F32)
            elif r == ROWS:
                rows[r] = halo[1, :, lanes].astype(F32)
            else:
                rows[r] = hidden[r, :, lanes].astype(F32)
        tap = [taps[t : t + 1, lanes] for t in range(9)]
        for r in range(begin, end):
            part = [sum(tap[3 * a + b] * rows[r + a - 1] for a in range(3)) for b in range(3)]
            conv = later(part[0], first) + part[1] + earlier(part[2], last)
            low, grad = gelu_and_slope(conv)
            act[PLANE * r : PLANE * (r + 1), lanes] = padded(low).astype(BF16)
            slope[PLANE * r : PLANE * (r + 1), lanes] = padded(grad)
        return carry

    lax.fori_loop(0, E // 128, chunk, 0)


def normal(mid):
    mean = jnp.mean(mid, axis=1, keepdims=True)
    centred = mid - mean
    inv = lax.rsqrt(jnp.mean(centred * centred, axis=1, keepdims=True) + EPS)
    return centred * inv, inv


def window_place(index):
    win, n = index >> 6, index & 63
    g = (n * 37) >> 8
    return jnp.where(n < 49, g * PLANE + (n - 7 * g) * 8 + win, -1)


def head_tools():
    lane = lax.broadcasted_iota(jnp.int32, (64, 128), 1) >> 5
    big = lax.broadcasted_iota(jnp.int32, (256, 128), 0) >> 6
    own = (big == (lax.broadcasted_iota(jnp.int32, (256, 128), 1) >> 5)).astype(F32).astype(BF16)

    def spread(value):
        return jnp.concatenate([value] * 4, axis=0) * own

    def gather(value):
        return jnp.where(
            lane < 2,
            jnp.where(lane == 0, value[0:64], value[64:128]),
            jnp.where(lane == 2, value[128:192], value[192:256]),
        )

    return spread, gather


def heads(part, g):
    return slice(part * C + 128 * g, part * C + 128 * (g + 1))


def attend(qkv, probs, att):
    spread, gather = head_tools()
    valid = lax.broadcasted_iota(jnp.int32, (64, 256), 0) < 49

    def window(w, carry):
        rows = pl.ds(pl.multiple_of(w * 64, 64), 64)
        for g in range(6):
            query, key, value = (qkv[rows, heads(part, g)] for part in range(3))
            score = lax.dot_general(key, spread(query), NT, preferred_element_type=F32) * SCALE
            score = jnp.where(valid, score, -1e30)
            power = jnp.exp(score - jnp.max(score, axis=0, keepdims=True))
            prob = power * (1.0 / jnp.sum(power, axis=0, keepdims=True))
            probs[g, rows] = prob
            att[rows, heads(0, g)] = gather(
                lax.dot_general(prob.astype(BF16), value, TN, preferred_element_type=F32)
            ).astype(BF16)
        return carry

    lax.fori_loop(0, 8, window, 0)


def attend_back(qkv, gatt, probs, gqkv, groups):
    spread, gather = head_tools()

    def window(pair, carry):
        for w in range(2):
            rows = pl.ds(pl.multiple_of(pair * 128 + 64 * w, 64), 64)
            for g in groups:
                query, key, value = (qkv[rows, heads(part, g)] for part in range(3))
                query = spread(query)
                grad = spread(gatt[rows, heads(0, g)])
                prob = probs[g, rows]
                low = prob.astype(BF16)
                grad_prob = lax.dot_general(value, grad, NT, preferred_element_type=F32)
                inner = jnp.sum(grad_prob * prob, axis=0, keepdims=True)
                grad_low = (prob * (grad_prob - inner) * SCALE).astype(BF16)
                gqkv[rows, heads(0, g)] = gather(
                    lax.dot_general(grad_low, key, TN, preferred_element_type=F32)
                ).astype(BF16)
                gqkv[rows, heads(1, g)] = jnp.dot(
                    grad_low, query, preferred_element_type=F32
                ).astype(BF16)
                gqkv[rows, heads(2, g)] = jnp.dot(low, grad, preferred_element_type=F32).astype(BF16)
        return carry

    lax.fori_loop(0, 4, window, 0)


def half_rows(value):
    left, right = (value[:, 128 * h : 128 * (h + 1)].reshape(32, 24, 128) for h in range(2))
    return jnp.concatenate([left, right], axis=1).reshape(4, 4, 2, 48, 128).astype(BF16)


def flip(q, mask):
    if mask == 0:
        return q
    if mask == 1:
        return q + 1 - 2 * lax.rem(q, 2)
    if mask == 3:
        return 3 - q
    return lax.rem(q + 2, 4)


class Pair:
    def __init__(self, grads, recv, ssem, rsem, core, peer):
        self.grads, self.recv, self.core = grads, recv, core
        self.ssem, self.rsem, self.peer = ssem, rsem, peer
        self.begun = []

    def copy(self, q):
        return remote(
            self.grads.at[q, :, 1 - self.core], self.recv.at[q], self.ssem.at[q], self.rsem.at[q], self.peer
        )

    def start(self, q):
        self.copy(q).start()

    def add(self, q, put):
        self.copy(q).wait_recv()

        def body(i, carry):
            mine = self.grads[q, i, self.core].astype(F32)
            put(q, i, (mine + self.recv[q, i].astype(F32)).astype(BF16))
            return carry

        lax.fori_loop(0, 4, body, 0)

    def wait_send(self):
        for q in range(4):
            self.copy(q).wait_send()


class Whole(Pair):
    def copy(self, q=0):
        return remote(self.grads.at[:, :, 1 - self.core], self.recv, self.ssem, self.rsem, self.peer)

    def add(self, put):
        self.copy().wait_recv()

        def body(i, carry):
            q, j = lax.div(i, 4), lax.rem(i, 4)
            mine = self.grads[q, j, self.core].astype(F32)
            put(q, j, (mine + self.recv[q, j].astype(F32)).astype(BF16))
            return carry

        lax.fori_loop(0, 16, body, 0)

    def wait_send(self):
        self.copy().wait_send()


class Halve:
    def __init__(self, src, recv, ssem, rsem, q, peers, view, piece, count):
        self.src, self.recv, self.q, self.view, self.piece, self.count = src, recv, q, view, piece, count
        self.cps = {}
        for h in range(2):
            near, far = (1, 3) if h == 0 else (3, 1)
            for slot, (block, to) in enumerate(((near, near), (2, near), (far, far))):
                n = 3 * h + slot
                self.cps[h, slot] = remote(
                    src.at[view(flip(q, block), h)], recv.at[view(slot, h)], ssem.at[n], rsem.at[n], peers[to]
                )

    def start(self):
        for slot in (1, 0):
            for h in range(2):
                self.cps[h, slot].start()

    def forward(self):
        for h in range(2):
            self.cps[h, 1].wait_recv()
            block = flip(self.q, 3 if h == 0 else 1)

            def body(i, carry, h=h, block=block):
                mine = self.src[self.piece(block, h, i)].astype(F32)
                mine = mine + self.recv[self.piece(1, h, i)].astype(F32)
                self.src[self.piece(block, h, i)] = mine.astype(BF16)
                return carry

            lax.fori_loop(0, self.count, body, 0)
            self.cps[h, 2].start()

    def finish(self, put):
        for h in range(2):
            self.cps[h, 0].wait_recv()
            self.cps[h, 2].wait_recv()

            def body(i, carry, h=h):
                mine = self.src[self.piece(self.q, h, i)].astype(F32)
                mine = mine + self.recv[self.piece(0, h, i)].astype(F32)
                put(h, i, mine + self.recv[self.piece(2, h, i)].astype(F32))
                return carry

            lax.fori_loop(0, self.count, body, 0)

    def wait_send(self):
        for cp in self.cps.values():
            cp.wait_send()


class Fan:
    def __init__(self, pieces, recvs, ssem, rsem, peers):
        self.cps = [
            remote(pieces(n), recvs(n), ssem.at[n], rsem.at[n], peer) for n, peer in enumerate(peers)
        ]

    def start(self):
        for cp in self.cps:
            cp.start()

    def wait_recv(self):
        for cp in self.cps:
            cp.wait_recv()

    def wait_send(self):
        for cp in self.cps:
            cp.wait_send()


def depth_sums(grad, halo, hidden, depth):
    def chunk(n, carry):
        lanes = pl.ds(pl.multiple_of(n * 128, 128), 128)
        first, last = col_masks(128)
        rows = [grad[PLANE * r : PLANE * r + COLS, lanes].astype(F32) for r in range(ROWS)]
        sums = [jnp.zeros((8, 128), F32) for _ in range(9)]
        for r in range(-1, ROWS + 1):
            if r < 0:
                own = halo[0, :, lanes].astype(F32)
            elif r == ROWS:
                own = halo[1, :, lanes].astype(F32)
            else:
                own = hidden[r, :, lanes].astype(F32)
            moved = [later(own, first), own, earlier(own, last)]
            for a in range(3):
                if 0 <= r + 1 - a < ROWS:
                    for b in range(3):
                        product = moved[b] * rows[r + 1 - a]
                        for i in range(7):
                            sums[3 * a + b] = sums[3 * a + b] + product[8 * i : 8 * i + 8]
        for t in range(9):
            depth[t : t + 1, lanes] = jnp.sum(sums[t], axis=0, keepdims=True)
        return carry

    lax.fori_loop(0, E // 128, chunk, 0)


def conv_backward(grad, halo, taps, hidden_grad, begin, end):
    def chunk(n, carry):
        lanes = pl.ds(pl.multiple_of(n * 128, 128), 128)
        first, last = col_masks(128)
        rows = [halo[0, 0:COLS, lanes].astype(F32)]
        rows += [grad[PLANE * r : PLANE * r + COLS, lanes].astype(F32) for r in range(ROWS)]
        rows += [halo[1, 0:COLS, lanes].astype(F32)]
        tap = [taps[t : t + 1, lanes] for t in range(9)]
        for r in range(ROWS):
            part = [sum(tap[3 * a + b] * rows[r + 2 - a] for a in range(3)) for b in range(3)]
            total = earlier(part[0], last) + part[1] + later(part[2], first)
            hidden_grad[r, :, lanes] = total.astype(BF16)
        return carry

    lax.fori_loop(begin, end, chunk, 0)


def settle_kernel(*refs):
    count = len(refs) // 2
    copies = [
        pltpu.make_async_copy(refs[n], refs[count + n], refs[2 * count].at[n]) for n in range(count)
    ]
    for cp in copies:
        cp.start()
    for cp in copies:
        cp.wait()


def tile(n, width=256):
    return pl.ds(pl.multiple_of(n * width, width), width)


def section_kernel(
    block_h, hidden_h, cot_h, proj_h, qkv_h, out_h, depth_w, gain,
    block_o, input_o, hidden_o, depth_o, gain_o, proj_o, qkv_o, out_o,
    block, hidden, cot, proj_w, qkv_w, out_w, loads,
    halo, taps, own_n, own_c, win_n, win_c, mid, act, slope,
    norm_p, cot_p, qkv, gatt, att_p, gqkv, turned, turned2, gn_p, probs,
    att_w, gn_w, att, gn, ig, gc, edges, depth,
    agrads, ar0, as0, arx, as1, arz, atot, arow, atile, arecv,
    pgrads, pr0, ps0, prx, ps1, prz, qs0, qrz, qs1, qrx, ptot, ptile, precv,
    small, srecv, ssum, sall, sfinal,
    hs, hr, ns, nr, cs, cr, ts, tr, us, ur, es, er,
    a0s, a0r, axs, axr, azs, azr, als, alr,
    p0s, p0r, pxs, pxr, pzs, pzr, qzs, qzr, qxs, qxr, pls, plr,
    d0s, d0r, d1s, d1r, d2s, d2r,
):
    dp, sp, x, zh, core = place()
    pulls = {}
    pairs = ((hidden_h, hidden), (proj_h, proj_w), (block_h, block), (cot_h, cot), (qkv_h, qkv_w), (out_h, out_w))
    for n, (src, dst) in enumerate(pairs):
        pulls[n] = pltpu.make_async_copy(src, dst, loads.at[n])
        pulls[n].start()
    pair = (dp_of(x, zh, 1 - core), sp)
    plane16 = [(dp_of(lax.rem(x + i, 4), lax.rem(zh + j, 4), core), sp) for i in range(4) for j in range(4)][1:]
    sps = [(dp, lax.rem(sp + j, 8)) for j in range(1, 8)]
    others = sps + [(dp_of(x, zh, 1 - core), lax.rem(sp + j, 8)) for j in range(8)]
    greet(plane16 + others)
    xp = {m: (dp_of(flip(x, m), zh, core), sp) for m in (1, 3)}
    zp = {m: (dp_of(x, flip(zh, m), core), sp) for m in (1, 3)}

    edge = Halo(hidden_h.at[0], hidden_h.at[ROWS - 1], halo, hs, hr, dp, sp)
    edge.start()
    cots = Rows(own_c, win_c, cs, cr, dp, sp, True)
    norms = Rows(own_n, win_n, ns, nr, dp, sp, True)
    taps[0:9] = depth_w[...].astype(F32)
    scale = gain[...].reshape(1, C)

    def norm(r):
        here = tile(r, PLANE)
        total = mid[here, :] + padded(block[r].astype(F32))
        mid[here, :] = total
        own_n[here, :] = (normal(total)[0] * scale).astype(BF16)
        norms.start(r)

    def norm_inner(r, carry):
        norm(r)
        return carry

    def norm_outer(i, carry):
        norm(lax.rem(i + 5, 7))
        return carry

    def proj_inner(n, carry):
        mid[64:320, tile(n)] = jnp.dot(act[64:320, :], proj_w[:, tile(n)], preferred_element_type=F32)
        return carry

    def proj_outer(n, carry):
        left = jnp.concatenate([act[0:64, :], act[320:448, :]], axis=0)
        part = jnp.dot(left, proj_w[:, tile(n)], preferred_element_type=F32)
        mid[0:64, tile(n)] = part[0:64]
        mid[320:448, tile(n)] = part[64:192]
        return carry

    pulls[0].wait()
    conv_forward(hidden, halo, taps, act, slope, 1, 5)
    pulls[1].wait()
    lax.fori_loop(0, C // 256, proj_inner, 0)
    pulls[2].wait()
    lax.fori_loop(1, 5, norm_inner, 0)
    edge.wait_recv()
    conv_forward(hidden, halo, taps, act, slope, 5, 7)
    conv_forward(hidden, halo, taps, act, slope, 0, 1)
    lax.fori_loop(0, C // 256, proj_outer, 0)
    lax.fori_loop(0, 3, norm_outer, 0)
    pulls[3].wait()
    for r in range(ROWS):
        own_c[PLANE * r : PLANE * (r + 1)] = padded(cot[r].astype(F32)).astype(BF16)
        cots.start(r)

    index = window_place(lax.broadcasted_iota(jnp.int32, (WIN, 1), 0))
    tokens = lax.broadcasted_iota(jnp.int32, (WIN, TOK), 1)
    perm = (index == tokens).astype(F32).astype(BF16)
    for r in range(ROWS):
        norms.wait_recv(r)
    norm_p[...] = jnp.dot(perm, win_n[...], preferred_element_type=F32).astype(BF16)
    pulls[4].wait()

    def qkv_step(n, carry):
        qkv[:, tile(n)] = jnp.dot(
            norm_p[...], qkv_w[:, tile(n)], preferred_element_type=F32
        ).astype(BF16)
        return carry

    lax.fori_loop(0, 9, qkv_step, 0)
    turned[...] = norm_p[...].T
    attend(qkv, probs, att_p)
    for r in range(ROWS):
        cots.wait_recv(r)
    cot_p[...] = jnp.dot(perm, win_c[...], preferred_element_type=F32).astype(BF16)
    pulls[5].wait()

    def gatt_step(n, carry):
        gatt[:, tile(n)] = lax.dot_general(
            cot_p[...], out_w[tile(n), :], NT, preferred_element_type=F32
        ).astype(BF16)
        return carry

    lax.fori_loop(0, 3, gatt_step, 0)

    ring = lambda q, h: (q, pl.ds(2 * h, 2))
    ring_piece = lambda q, h, i: (q, 2 * h + i)
    line = lambda q, h: (q, slice(None), slice(256 * h, 256 + 128 * h))
    line_piece = lambda q, h, i: line(q, h)

    class Chunk:
        def __init__(self, c):
            self.c = c
            self.pair = Whole(agrads.at[c], ar0.at[c], a0s.at[c], a0r.at[c], core, pair)
            six = pl.ds(6 * c, 6)
            self.first = Halve(
                as0.at[c], arx.at[c], axs.at[six], axr.at[six], x, xp, ring, ring_piece, 2
            )
            self.second = Halve(
                as1.at[c], arz.at[c], azs.at[six], azr.at[six], zh, zp, line, line_piece, 1
            )

        def put0(self, q, i, value):
            as0[self.c, q, i] = value

        def put1(self, h, i, value):
            as1[self.c, 2 * h + i] = value.astype(BF16)

        def put2(self, h, i, value):
            atot[self.c, :, 256 * h : 256 + 128 * h] = value

        def step(self, n):
            if n == 0:
                self.pair.start(0)
            elif n == 1:
                self.pair.add(self.put0)
                self.first.start()
            elif n == 2:
                self.first.forward()
            elif n == 3:
                self.first.finish(self.put1)
                self.second.start()
            elif n == 4:
                self.second.forward()
            elif n == 5:
                self.second.finish(self.put2)

        def wait_send(self):
            for one in (self.pair, self.first, self.second):
                one.wait_send()

    chunks = [Chunk(c) for c in range(4)]

    def advance(slot):
        for c in range(4):
            if 0 <= slot - c <= 5:
                chunks[c].step(slot - c)

    turned2[...] = att_p[...].T

    def out_grad_step(n, carry):
        right = jnp.concatenate([cot_p[:, tile(n, 128)], cot_p[:, tile(n + 3, 128)]], axis=1)
        agrads[0, :, :, :, :, tile(n, 128)] = half_rows(
            jnp.dot(turned2[...], right, preferred_element_type=F32)
        )
        return carry

    lax.fori_loop(0, 3, out_grad_step, 0)
    advance(0)
    index = window_place(lax.broadcasted_iota(jnp.int32, (1, WIN), 1))
    tokens = lax.broadcasted_iota(jnp.int32, (TOK, WIN), 0)
    back = (index == tokens).astype(F32).astype(BF16)
    gns = Rows(gn_w, gn, us, ur, dp, sp, False)
    atts = Rows(att_w, att, ts, tr, dp, sp, False)
    att_w[...] = jnp.dot(back, att_p[...], preferred_element_type=F32).astype(BF16)
    for g in range(ROWS):
        atts.start(g)

    def qkv_grad(c):
        def grad_step(n, carry):
            right = gqkv[:, pl.ds(pl.multiple_of(768 * n + 256 * (c - 1), 256), 256)]
            agrads[c, :, :, :, :, tile(n, 128)] = half_rows(
                jnp.dot(turned[...], right, preferred_element_type=F32)
            )
            return carry

        lax.fori_loop(0, 3, grad_step, 0)
        advance(c)

    attend_back(qkv, gatt, probs, gqkv, (0, 1))
    qkv_grad(1)
    attend_back(qkv, gatt, probs, gqkv, (2, 3))
    attend_back(qkv, gatt, probs, gqkv, (4, 5))

    def gn_step(n, carry):
        gn_p[:, tile(n)] = lax.dot_general(
            gqkv[...], qkv_w[tile(n), :], NT, preferred_element_type=F32
        ).astype(BF16)
        return carry

    lax.fori_loop(0, 3, gn_step, 0)
    gn_w[...] = jnp.dot(back, gn_p[...], preferred_element_type=F32).astype(BF16)
    for g in range(ROWS):
        gns.start(g)
    qkv_grad(2)
    qkv_grad(3)
    for r in range(ROWS):
        atts.wait_recv(r)

    def out_step(n, carry):
        part = jnp.dot(att[...], out_w[:, tile(n)], preferred_element_type=F32)
        part = (part + mid[:, tile(n)]).astype(BF16)
        for r in range(ROWS):
            block_o[r, :, tile(n)] = part[PLANE * r : PLANE * r + COLS]
        return carry

    lax.fori_loop(0, C // 256, out_step, 0)

    for r in range(ROWS):
        gns.wait_recv(r)

    def norm_step(r, carry):
        here = tile(r, PLANE)
        hat, inv = normal(mid[here, :])
        grad = gn[here, :].astype(F32)
        grad_hat = grad * scale
        carry = carry + (grad * hat).reshape(8, 8, C).sum(axis=0)
        inner = jnp.mean(grad_hat * hat, axis=1, keepdims=True)
        mean = jnp.mean(grad_hat, axis=1, keepdims=True)
        cotangent = padded(cot[r].astype(F32))
        low = (cotangent + inv * (grad_hat - mean - hat * inner)).astype(BF16)
        ig[here, :] = low
        input_o[r] = low[0:COLS]
        return carry

    gain_part = lax.fori_loop(0, ROWS, norm_step, jnp.zeros((8, C), F32))
    gain_part = jnp.sum(gain_part, axis=0, keepdims=True)
    advance(4)

    ppair = Pair(pgrads, pr0, p0s, p0r, core, pair)
    ends = lambda width: (
        lambda q, h: (q, slice(None), slice(width * h, width * (h + 1))),
        lambda q, h, i: (q, slice(None), slice(width * h, width * (h + 1))),
    )
    px = Halve(ps0, prx, pxs, pxr, x, xp, ring, ring_piece, 2)
    pz = Halve(ps1, prz, pzs, pzr, zh, zp, *ends(256), 1)
    qz = Halve(qs0, qrz, qzs, qzr, zh, zp, ring, ring_piece, 2)
    qx = Halve(qs1, qrx, qxs, qxr, x, xp, *ends(128), 1)

    def put_p0(q, i, value):
        ps0[q, i] = value[:, 0:512]
        qs0[i, q] = value[:, 512:768]

    def put_ps1(h, i, value):
        ps1[2 * h + i] = value.astype(BF16)

    def put_qs1(h, i, value):
        qs1[2 * h + i] = value.astype(BF16)

    def put_p2(h, i, value):
        ptot[:, 256 * h : 256 * (h + 1)] = value

    def put_q2(h, i, value):
        ptot[:, 512 + 128 * h : 512 + 128 * (h + 1)] = value

    for m in XORS:
        xx = flip(x, m)
        turned2[0:384, 0:TOK] = act[:, pl.ds(pl.multiple_of(xx * 384, 128), 384)].T

        def proj_step(n, carry, xx=xx):
            part = jnp.dot(turned2[0:384, 0:TOK], ig[:, tile(n)], preferred_element_type=F32)
            pgrads[xx, :, :, :, tile(n)] = part.reshape(4, 2, 48, 256).astype(BF16)
            return carry

        lax.fori_loop(0, 3, proj_step, 0)
        ppair.start(xx)

    for m in XORS:
        ppair.add(flip(x, m), put_p0)
    px.start()
    qz.start()
    advance(5)

    def act_step(n, carry):
        part = lax.dot_general(ig[...], proj_w[tile(n), :], NT, preferred_element_type=F32)
        gc[:, tile(n)] = (part * slope[:, tile(n)]).astype(BF16)
        return carry

    lax.fori_loop(0, E // 256, act_step, 0)
    edge2 = Halo(gc.at[0:PLANE], gc.at[TOK - PLANE : TOK], edges, es, er, dp, sp)
    edge2.start()
    depth_sums(gc, halo, hidden, depth)

    for n in range(12):
        small[n] = depth[0:8, 128 * n : 128 * (n + 1)]
        small[12 + n // 8, n % 8 : n % 8 + 1, :] = depth[8:9, 128 * n : 128 * (n + 1)]
    for n in range(6):
        small[13 + (4 + n) // 8, (4 + n) % 8 : (4 + n) % 8 + 1, :] = gain_part[:, 128 * n : 128 * (n + 1)]
    small[14, 2:8, :] = jnp.zeros((6, 128), F32)
    small[15] = jnp.zeros((8, 128), F32)
    shifts = [(i, j) for i in range(4) for j in range(4)][1:]

    def spot(i, j):
        return lax.rem(x + i, 4) * 4 + lax.rem(zh + j, 4)

    mine = x * 4 + zh
    scatter = Fan(lambda n: small.at[spot(*shifts[n])], lambda n: srecv.at[n], d0s, d0r, plane16)
    spread = Fan(lambda n: ssum, lambda n: sall.at[n], d1s, d1r, others)
    collect = Fan(lambda n: sfinal.at[mine], lambda n: sfinal.at[mine], d2s, d2r, plane16)
    scatter.start()
    px.forward()
    qz.forward()
    advance(6)
    edge2.wait_recv()
    conv_backward(gc, edges, taps, hidden_o, 0, 6)
    scatter.wait_recv()
    total = small[mine]
    for n in range(15):
        total = total + srecv[n]
    ssum[...] = total
    spread.start()
    px.finish(put_ps1)
    pz.start()
    qz.finish(put_qs1)
    qx.start()
    advance(7)
    conv_backward(gc, edges, taps, hidden_o, 6, 12)
    spread.wait_recv()
    total = ssum[...]
    for n in range(15):
        total = total + sall[n]
    sfinal[mine] = total
    collect.start()
    pz.forward()
    qx.forward()
    advance(8)
    for hh in range(2):
        rows = slice(24 * hh, 24 * (hh + 1))
        arow[:, 2304 + 384 * hh : 2304 + 384 * (hh + 1)] = atot[0, rows, :]
        for c in range(1, 4):
            for part in range(3):
                begin = C * part + 256 * (c - 1) + 128 * hh
                arow[:, begin : begin + 128] = atot[c, rows, 128 * part : 128 * (part + 1)]
    blank = jnp.zeros((8, 384), F32)
    for j in range(8):
        left = arow[:, 288 * j : 288 * (j + 1)]
        right = arow[:, 2304 + 96 * j : 2304 + 96 * (j + 1)]
        value = jnp.concatenate([jnp.concatenate([left, right], axis=1), blank], axis=0)
        atile[j] = value.astype(BF16)
    alast = Fan(lambda n: atile.at[lax.rem(sp + n + 1, 8)], lambda n: arecv.at[n], als, alr, sps)
    alast.start()
    qx.finish(put_q2)
    pz.finish(put_p2)
    for j in range(8):
        ptile[j, :, 0:96] = ptot[:, 96 * j : 96 * (j + 1)].astype(BF16)
    plast = Fan(lambda n: ptile.at[lax.rem(sp + n + 1, 8)], lambda n: precv.at[n], pls, plr, sps)
    plast.start()
    alast.wait_recv()
    total = atile[sp].astype(F32)
    for n in range(7):
        total = total + arecv[n].astype(F32)
    qkv_o[...] = total[0:24, 0:288]
    out_o[...] = total[0:24, 288:384]
    collect.wait_recv()
    for n in range(12):
        depth_o[0:8, 128 * n : 128 * (n + 1)] = sfinal[n]
        depth_o[8:9, 128 * n : 128 * (n + 1)] = sfinal[12 + n // 8, n % 8 : n % 8 + 1, :]
    gains = [sfinal[13 + (4 + n) // 8, (4 + n) % 8 : (4 + n) % 8 + 1, :] for n in range(6)]
    gain_o[...] = jnp.concatenate(gains, axis=1).reshape(C)
    plast.wait_recv()
    total = ptile[sp].astype(F32)
    for n in range(7):
        total = total + precv[n].astype(F32)
    proj_o[...] = total[:, 0:96]
    for g in range(ROWS):
        for rows in (cots, norms, gns, atts):
            rows.wait_send(g)
    for one in [edge, edge2, ppair, px, pz, qx, qz, scatter, spread, collect, plast, alast] + chunks:
        one.wait_send()


VM = pl.BlockSpec(memory_space=pltpu.VMEM)
ANY = pl.BlockSpec(memory_space=pl.ANY)
DMA = pltpu.SemaphoreType.DMA
MIB = 1024 * 1024


def shape(dims, dtype=BF16):
    return jax.ShapeDtypeStruct(dims, dtype)


def low(*dims):
    return pltpu.VMEM(dims, BF16)


def full(*dims):
    return pltpu.VMEM(dims, F32)


def local(block, hidden, cot, depth_w, proj_w, gain, qkv_w, out_w):
    scratch = [low(ROWS, COLS, C), low(ROWS, COLS, E), low(ROWS, COLS, C), low(E, C), low(C, 3 * C), low(C, C), DMA((6,))]
    scratch += [low(2, COLS, E), full(16, E)] + [low(TOK, C)] * 4 + [full(TOK, C), low(TOK, E), full(TOK, E)]
    scratch += [low(WIN, C), low(WIN, C), low(WIN, 3 * C), low(WIN, C), low(WIN, C), low(WIN, 3 * C), low(C, WIN), low(C, WIN), low(WIN, C)]
    scratch += [full(6, WIN, 256)]
    scratch += [low(TOK, C)] * 5 + [low(TOK, E), low(2, PLANE, E), full(16, E)]
    scratch += [
        low(4, 4, 4, 2, 48, 384), low(4, 4, 4, 48, 384), low(4, 4, 4, 48, 384), low(4, 3, 4, 48, 384),
        low(4, 4, 48, 384), low(4, 3, 48, 384), full(4, 48, 384), full(24, 4 * C), low(8, 32, 384), low(7, 32, 384),
    ]
    scratch += [
        low(4, 4, 2, 48, C), low(4, 4, 48, C), low(4, 4, 48, 512), low(3, 4, 48, 512), low(4, 48, 512), low(3, 48, 512),
        low(4, 4, 48, 256), low(3, 4, 48, 256), low(4, 48, 256), low(3, 48, 256),
        full(48, C), low(8, 48, 128), low(7, 48, 128),
    ]
    scratch += [full(16, 8, 128), full(15, 8, 128), full(8, 128), full(15, 8, 128), full(16, 8, 128)]
    counts = [2, 2, 7, 7, 7, 7, 7, 7, 7, 7, 2, 2]
    counts += [4, 4, 24, 24, 24, 24, 7, 7]
    counts += [4, 4, 6, 6, 6, 6, 6, 6, 6, 6, 7, 7]
    counts += [15] * 6
    scratch += [DMA((n,)) for n in counts]
    shapes = (
        shape((ROWS, COLS, C)), shape((ROWS, COLS, C)), shape((ROWS, COLS, E)),
        shape((9, E), F32), shape((C,), F32),
        shape((48, 96), F32), shape((24, 288), F32), shape((24, 96), F32),
    )
    outs = pl.pallas_call(
        section_kernel,
        out_shape=shapes,
        in_specs=[ANY] * 6 + [VM] * 2,
        out_specs=(VM,) * 8,
        scratch_shapes=scratch,
        compiler_params=pltpu.CompilerParams(
            collective_id=1, has_side_effects=True, vmem_limit_bytes=63 * MIB
        ),
        name="section",
    )(block[0], hidden[0], cot[0], proj_w, qkv_w, out_w, depth_w, gain)
    outs = pl.pallas_call(
        settle_kernel,
        out_shape=shapes,
        in_specs=[ANY] * 8,
        out_specs=(ANY,) * 8,
        scratch_shapes=[DMA((8,))],
        name="settle",
    )(*outs)
    return tuple(one[None] for one in outs[:3]) + tuple(outs[3:])


def solution(mesh):
    slab = P("dp", "space", None, None)
    part = P("dp", "space")
    return jax.shard_map(
        local,
        mesh=mesh,
        in_specs=(slab, slab, slab, P(), P(), P(), P(), P()),
        out_specs=(slab, slab, slab, P(), P(), part, part, part),
        check_vma=False,
    )
```

```python
import jax
import jax.numpy as jnp
from jax import lax
from jax.experimental import pallas as pl
from jax.experimental.pallas import tpu as pltpu
from jax.sharding import PartitionSpec as P

MESH = pl.DeviceIdType.MESH
F32, BF16 = jnp.float32, jnp.bfloat16
EPS = 1e-05
C, E, HEADS, HD = 768, 1536, 24, 32
ROWS, COLS, PLANE = 7, 56, 64
TOK = ROWS * PLANE
WIN = 512
SCALE = HD ** (-0.5)
XORS = (2, 1, 3, 0)
NT = (((1,), (1,)), ((), ()))
TN = (((0,), (0,)), ((), ()))


def place():
    dp, sp = lax.axis_index("dp"), lax.axis_index("space")
    return dp, sp, lax.div(dp, 8), lax.rem(lax.div(dp, 2), 4), lax.rem(dp, 2)


def dp_of(x, zh, core):
    return (x * 4 + zh) * 2 + core


def greet(ids):
    barrier = pltpu.get_barrier_semaphore()
    for one in ids:
        pl.semaphore_signal(barrier, inc=1, device_id=one, device_id_type=MESH)
    pl.semaphore_wait(barrier, len(ids))


def remote(src, dst, send, recv, to):
    return pltpu.make_async_remote_copy(
        src_ref=src, dst_ref=dst, send_sem=send, recv_sem=recv, device_id=to, device_id_type=MESH
    )


def planes(ref, n):
    return ref.at[pl.ds(pl.multiple_of(n * PLANE, PLANE), PLANE)]


class Rows:
    def __init__(self, src, dst, ssem, rsem, dp, sp, out):
        self.src, self.dst, self.ssem, self.rsem = src, dst, ssem, rsem
        self.dp, self.sp, self.out = dp, sp, out

    def target(self, n):
        if self.out:
            row = self.sp * 7 + n
            return lax.rem(row, 8), lax.div(row, 8)
        row = n * 8 + self.sp
        return lax.div(row, 7), lax.rem(row, 7)

    def copies(self, n):
        to, slot = self.target(n)
        src, dst = planes(self.src, n), planes(self.dst, slot)
        far = remote(src, dst, self.ssem.at[n], self.rsem.at[slot], (self.dp, to))
        near = pltpu.make_async_copy(src, dst, self.rsem.at[slot])
        return to, far, near

    def start(self, n):
        to, far, near = self.copies(n)

        @pl.when(to != self.sp)
        def _():
            far.start()

        @pl.when(to == self.sp)
        def _():
            near.start()

    def wait_recv(self, n):
        one = planes(self.dst, n)
        pltpu.make_async_copy(one, one, self.rsem.at[n]).wait()

    def wait_send(self, n):
        to, far, _ = self.copies(n)

        @pl.when(to != self.sp)
        def _():
            far.wait_send()


class Halo:
    def __init__(self, top, bottom, halo, ssem, rsem, dp, sp):
        self.sp = sp
        self.up = remote(top, halo.at[1], ssem.at[0], rsem.at[1], (dp, jnp.maximum(sp - 1, 0)))
        self.down = remote(bottom, halo.at[0], ssem.at[1], rsem.at[0], (dp, jnp.minimum(sp + 1, 7)))
        self.halo = halo

    def start(self):
        @pl.when(self.sp > 0)
        def _():
            self.up.start()

        @pl.when(self.sp < 7)
        def _():
            self.down.start()

        zero = jnp.zeros(self.halo.shape[1:], self.halo.dtype)

        @pl.when(self.sp == 0)
        def _():
            self.halo[0] = zero

        @pl.when(self.sp == 7)
        def _():
            self.halo[1] = zero

    def wait_recv(self):
        @pl.when(self.sp > 0)
        def _():
            self.down.wait_recv()

        @pl.when(self.sp < 7)
        def _():
            self.up.wait_recv()

    def wait_send(self):
        @pl.when(self.sp > 0)
        def _():
            self.up.wait_send()

        @pl.when(self.sp < 7)
        def _():
            self.down.wait_send()


def col_masks(lanes):
    index = lax.broadcasted_iota(jnp.int32, (COLS, lanes), 0)
    return index == 0, index == COLS - 1


def later(value, first):
    return jnp.where(first, 0.0, pltpu.roll(value, 1, 0))


def earlier(value, last):
    return jnp.where(last, 0.0, pltpu.roll(value, COLS - 1, 0))


def padded(value):
    return jnp.concatenate([value, jnp.zeros((PLANE - COLS, value.shape[1]), F32)], axis=0)


def gelu_and_slope(value):
    k0, k1 = 0.7978845608028654, 0.044715
    square = value * value
    tanh = jnp.tanh(k0 * value * (1.0 + k1 * square))
    half = 0.5 * (1.0 + tanh)
    slope = half + 0.5 * value * (1.0 - tanh * tanh) * (k0 * (1.0 + 3.0 * k1 * square))
    return value * half, slope


def conv_forward(hidden, halo, taps, act, slope, begin, end):
    def chunk(n, carry):
        lanes = pl.ds(pl.multiple_of(n * 128, 128), 128)
        first, last = col_masks(128)
        rows = {}
        for r in range(begin - 1, end + 1):
            if r < 0:
                rows[r] = halo[0, :, lanes].astype(F32)
            elif r == ROWS:
                rows[r] = halo[1, :, lanes].astype(F32)
            else:
                rows[r] = hidden[r, :, lanes].astype(F32)
        tap = [taps[t : t + 1, lanes] for t in range(9)]
        for r in range(begin, end):
            part = [sum(tap[3 * a + b] * rows[r + a - 1] for a in range(3)) for b in range(3)]
            conv = later(part[0], first) + part[1] + earlier(part[2], last)
            low, grad = gelu_and_slope(conv)
            act[PLANE * r : PLANE * (r + 1), lanes] = padded(low).astype(BF16)
            slope[PLANE * r : PLANE * (r + 1), lanes] = padded(grad)
        return carry

    lax.fori_loop(0, E // 128, chunk, 0)


def normal(mid):
    mean = jnp.mean(mid, axis=1, keepdims=True)
    centred = mid - mean
    inv = lax.rsqrt(jnp.mean(centred * centred, axis=1, keepdims=True) + EPS)
    return centred * inv, inv


def window_place(index):
    win, n = index >> 6, index & 63
    g = (n * 37) >> 8
    return jnp.where(n < 49, g * PLANE + (n - 7 * g) * 8 + win, -1)


def head_tools():
    lane = lax.broadcasted_iota(jnp.int32, (64, 128), 1) >> 5
    big = lax.broadcasted_iota(jnp.int32, (256, 128), 0) >> 6
    own = (big == (lax.broadcasted_iota(jnp.int32, (256, 128), 1) >> 5)).astype(F32).astype(BF16)

    def spread(value):
        return jnp.concatenate([value] * 4, axis=0) * own

    def gather(value):
        return jnp.where(
            lane < 2,
            jnp.where(lane == 0, value[0:64], value[64:128]),
            jnp.where(lane == 2, value[128:192], value[192:256]),
        )

    return spread, gather


def heads(part, g):
    return slice(part * C + 128 * g, part * C + 128 * (g + 1))


def attend(qkv, probs, att):
    spread, gather = head_tools()
    valid = lax.broadcasted_iota(jnp.int32, (64, 256), 0) < 49

    def window(w, carry):
        rows = pl.ds(pl.multiple_of(w * 64, 64), 64)
        for g in range(6):
            query, key, value = (qkv[rows, heads(part, g)] for part in range(3))
            score = lax.dot_general(key, spread(query), NT, preferred_element_type=F32) * SCALE
            score = jnp.where(valid, score, -1e30)
            power = jnp.exp(score - jnp.max(score, axis=0, keepdims=True))
            prob = power * (1.0 / jnp.sum(power, axis=0, keepdims=True))
            probs[g, rows] = prob
            att[rows, heads(0, g)] = gather(
                lax.dot_general(prob.astype(BF16), value, TN, preferred_element_type=F32)
            ).astype(BF16)
        return carry

    lax.fori_loop(0, 8, window, 0)


def attend_back(qkv, gatt, probs, gqkv, groups):
    spread, gather = head_tools()

    def window(pair, carry):
        for w in range(2):
            rows = pl.ds(pl.multiple_of(pair * 128 + 64 * w, 64), 64)
            for g in groups:
                query, key, value = (qkv[rows, heads(part, g)] for part in range(3))
                query = spread(query)
                grad = spread(gatt[rows, heads(0, g)])
                prob = probs[g, rows]
                low = prob.astype(BF16)
                grad_prob = lax.dot_general(value, grad, NT, preferred_element_type=F32)
                inner = jnp.sum(grad_prob * prob, axis=0, keepdims=True)
                grad_low = (prob * (grad_prob - inner) * SCALE).astype(BF16)
                gqkv[rows, heads(0, g)] = gather(
                    lax.dot_general(grad_low, key, TN, preferred_element_type=F32)
                ).astype(BF16)
                gqkv[rows, heads(1, g)] = jnp.dot(
                    grad_low, query, preferred_element_type=F32
                ).astype(BF16)
                gqkv[rows, heads(2, g)] = jnp.dot(low, grad, preferred_element_type=F32).astype(BF16)
        return carry

    lax.fori_loop(0, 4, window, 0)


def half_rows(value):
    left, right = (value[:, 128 * h : 128 * (h + 1)].reshape(32, 24, 128) for h in range(2))
    return jnp.concatenate([left, right], axis=1).reshape(4, 4, 2, 48, 128).astype(BF16)


def flip(q, mask):
    if mask == 0:
        return q
    if mask == 1:
        return q + 1 - 2 * lax.rem(q, 2)
    if mask == 3:
        return 3 - q
    return lax.rem(q + 2, 4)


class Pair:
    def __init__(self, grads, recv, ssem, rsem, core, peer):
        self.grads, self.recv, self.core = grads, recv, core
        self.ssem, self.rsem, self.peer = ssem, rsem, peer
        self.begun = []

    def copy(self, q):
        return remote(
            self.grads.at[q, :, 1 - self.core], self.recv.at[q], self.ssem.at[q], self.rsem.at[q], self.peer
        )

    def start(self, q):
        self.copy(q).start()

    def add(self, q, put):
        self.copy(q).wait_recv()

        def body(i, carry):
            mine = self.grads[q, i, self.core].astype(F32)
            put(q, i, (mine + self.recv[q, i].astype(F32)).astype(BF16))
            return carry

        lax.fori_loop(0, 4, body, 0)

    def wait_send(self):
        for q in range(4):
            self.copy(q).wait_send()


class Whole(Pair):
    def copy(self, q=0):
        return remote(self.grads.at[:, :, 1 - self.core], self.recv, self.ssem, self.rsem, self.peer)

    def add(self, put):
        self.copy().wait_recv()

        def body(i, carry):
            q, j = lax.div(i, 4), lax.rem(i, 4)
            mine = self.grads[q, j, self.core].astype(F32)
            put(q, j, (mine + self.recv[q, j].astype(F32)).astype(BF16))
            return carry

        lax.fori_loop(0, 16, body, 0)

    def wait_send(self):
        self.copy().wait_send()


class Halve:
    def __init__(self, src, recv, ssem, rsem, q, peers, view, piece, count):
        self.src, self.recv, self.q, self.view, self.piece, self.count = src, recv, q, view, piece, count
        self.cps = {}
        for h in range(2):
            near, far = (1, 3) if h == 0 else (3, 1)
            for slot, (block, to) in enumerate(((near, near), (2, near), (far, far))):
                n = 3 * h + slot
                self.cps[h, slot] = remote(
                    src.at[view(flip(q, block), h)], recv.at[view(slot, h)], ssem.at[n], rsem.at[n], peers[to]
                )

    def start(self):
        for slot in (1, 0):
            for h in range(2):
                self.cps[h, slot].start()

    def forward(self):
        for h in range(2):
            self.cps[h, 1].wait_recv()
            block = flip(self.q, 3 if h == 0 else 1)

            def body(i, carry, h=h, block=block):
                mine = self.src[self.piece(block, h, i)].astype(F32)
                mine = mine + self.recv[self.piece(1, h, i)].astype(F32)
                self.src[self.piece(block, h, i)] = mine.astype(BF16)
                return carry

            lax.fori_loop(0, self.count, body, 0)
            self.cps[h, 2].start()

    def finish(self, put):
        for h in range(2):
            self.cps[h, 0].wait_recv()
            self.cps[h, 2].wait_recv()

            def body(i, carry, h=h):
                mine = self.src[self.piece(self.q, h, i)].astype(F32)
                mine = mine + self.recv[self.piece(0, h, i)].astype(F32)
                put(h, i, mine + self.recv[self.piece(2, h, i)].astype(F32))
                return carry

            lax.fori_loop(0, self.count, body, 0)

    def wait_send(self):
        for cp in self.cps.values():
            cp.wait_send()


class Fan:
    def __init__(self, pieces, recvs, ssem, rsem, peers):
        self.cps = [
            remote(pieces(n), recvs(n), ssem.at[n], rsem.at[n], peer) for n, peer in enumerate(peers)
        ]

    def start(self):
        for cp in self.cps:
            cp.start()

    def wait_recv(self):
        for cp in self.cps:
            cp.wait_recv()

    def wait_send(self):
        for cp in self.cps:
            cp.wait_send()


def depth_sums(grad, halo, hidden, depth):
    def chunk(n, carry):
        lanes = pl.ds(pl.multiple_of(n * 128, 128), 128)
        first, last = col_masks(128)
        rows = [grad[PLANE * r : PLANE * r + COLS, lanes].astype(F32) for r in range(ROWS)]
        sums = [jnp.zeros((8, 128), F32) for _ in range(9)]
        for r in range(-1, ROWS + 1):
            if r < 0:
                own = halo[0, :, lanes].astype(F32)
            elif r == ROWS:
                own = halo[1, :, lanes].astype(F32)
            else:
                own = hidden[r, :, lanes].astype(F32)
            moved = [later(own, first), own, earlier(own, last)]
            for a in range(3):
                if 0 <= r + 1 - a < ROWS:
                    for b in range(3):
                        product = moved[b] * rows[r + 1 - a]
                        for i in range(7):
                            sums[3 * a + b] = sums[3 * a + b] + product[8 * i : 8 * i + 8]
        for t in range(9):
            depth[t : t + 1, lanes] = jnp.sum(sums[t], axis=0, keepdims=True)
        return carry

    lax.fori_loop(0, E // 128, chunk, 0)


def conv_backward(grad, halo, taps, hidden_grad, begin, end):
    def chunk(n, carry):
        lanes = pl.ds(pl.multiple_of(n * 128, 128), 128)
        first, last = col_masks(128)
        rows = [halo[0, 0:COLS, lanes].astype(F32)]
        rows += [grad[PLANE * r : PLANE * r + COLS, lanes].astype(F32) for r in range(ROWS)]
        rows += [halo[1, 0:COLS, lanes].astype(F32)]
        tap = [taps[t : t + 1, lanes] for t in range(9)]
        for r in range(ROWS):
            part = [sum(tap[3 * a + b] * rows[r + 2 - a] for a in range(3)) for b in range(3)]
            total = earlier(part[0], last) + part[1] + later(part[2], first)
            hidden_grad[r, :, lanes] = total.astype(BF16)
        return carry

    lax.fori_loop(begin, end, chunk, 0)


def settle_kernel(*refs):
    count = len(refs) // 2
    for n in range(count):
        refs[count + n][...] = refs[n][...]


def tile(n, width=256):
    return pl.ds(pl.multiple_of(n * width, width), width)


def section_kernel(
    block_h, hidden_h, cot_h, proj_h, qkv_h, out_h, depth_w, gain,
    block_o, input_o, hidden_o, depth_o, gain_o, proj_o, qkv_o, out_o,
    block, hidden, cot, proj_w, qkv_w, out_w, loads,
    halo, taps, own_n, own_c, win_n, win_c, mid, act, slope,
    norm_p, cot_p, qkv, gatt, att_p, gqkv, turned, turned2, gn_p, probs,
    att_w, gn_w, att, gn, ig, gc, edges, depth,
    agrads, ar0, as0, arx, as1, arz, atot, arow, atile, arecv,
    pgrads, pr0, ps0, prx, ps1, prz, qs0, qrz, qs1, qrx, ptot, ptile, precv,
    small, srecv, ssum, sall, sfinal,
    hs, hr, ns, nr, cs, cr, ts, tr, us, ur, es, er,
    a0s, a0r, axs, axr, azs, azr, als, alr,
    p0s, p0r, pxs, pxr, pzs, pzr, qzs, qzr, qxs, qxr, pls, plr,
    d0s, d0r, d1s, d1r, d2s, d2r,
):
    dp, sp, x, zh, core = place()
    pulls = {}
    pairs = ((hidden_h, hidden), (proj_h, proj_w), (block_h, block), (cot_h, cot), (qkv_h, qkv_w), (out_h, out_w))
    for n, (src, dst) in enumerate(pairs):
        pulls[n] = pltpu.make_async_copy(src, dst, loads.at[n])
        pulls[n].start()
    pair = (dp_of(x, zh, 1 - core), sp)
    plane16 = [(dp_of(lax.rem(x + i, 4), lax.rem(zh + j, 4), core), sp) for i in range(4) for j in range(4)][1:]
    sps = [(dp, lax.rem(sp + j, 8)) for j in range(1, 8)]
    others = sps + [(dp_of(x, zh, 1 - core), lax.rem(sp + j, 8)) for j in range(8)]
    greet(plane16 + others)
    xp = {m: (dp_of(flip(x, m), zh, core), sp) for m in (1, 3)}
    zp = {m: (dp_of(x, flip(zh, m), core), sp) for m in (1, 3)}

    edge = Halo(hidden_h.at[0], hidden_h.at[ROWS - 1], halo, hs, hr, dp, sp)
    edge.start()
    cots = Rows(own_c, win_c, cs, cr, dp, sp, True)
    norms = Rows(own_n, win_n, ns, nr, dp, sp, True)
    taps[0:9] = depth_w[...].astype(F32)
    scale = gain[...].reshape(1, C)

    def norm(r):
        here = tile(r, PLANE)
        total = mid[here, :] + padded(block[r].astype(F32))
        mid[here, :] = total
        own_n[here, :] = (normal(total)[0] * scale).astype(BF16)
        norms.start(r)

    def norm_inner(r, carry):
        norm(r)
        return carry

    def norm_outer(i, carry):
        norm(lax.rem(i + 5, 7))
        return carry

    def proj_inner(n, carry):
        mid[64:320, tile(n)] = jnp.dot(act[64:320, :], proj_w[:, tile(n)], preferred_element_type=F32)
        return carry

    def proj_outer(n, carry):
        left = jnp.concatenate([act[0:64, :], act[320:448, :]], axis=0)
        part = jnp.dot(left, proj_w[:, tile(n)], preferred_element_type=F32)
        mid[0:64, tile(n)] = part[0:64]
        mid[320:448, tile(n)] = part[64:192]
        return carry

    pulls[0].wait()
    conv_forward(hidden, halo, taps, act, slope, 1, 5)
    pulls[1].wait()
    lax.fori_loop(0, C // 256, proj_inner, 0)
    pulls[2].wait()
    lax.fori_loop(1, 5, norm_inner, 0)
    edge.wait_recv()
    conv_forward(hidden, halo, taps, act, slope, 5, 7)
    conv_forward(hidden, halo, taps, act, slope, 0, 1)
    lax.fori_loop(0, C // 256, proj_outer, 0)
    lax.fori_loop(0, 3, norm_outer, 0)
    pulls[3].wait()
    for r in range(ROWS):
        own_c[PLANE * r : PLANE * (r + 1)] = padded(cot[r].astype(F32)).astype(BF16)
        cots.start(r)

    index = window_place(lax.broadcasted_iota(jnp.int32, (WIN, 1), 0))
    tokens = lax.broadcasted_iota(jnp.int32, (WIN, TOK), 1)
    perm = (index == tokens).astype(F32).astype(BF16)
    for r in range(ROWS):
        norms.wait_recv(r)
    norm_p[...] = jnp.dot(perm, win_n[...], preferred_element_type=F32).astype(BF16)
    pulls[4].wait()

    def qkv_step(n, carry):
        qkv[:, tile(n)] = jnp.dot(
            norm_p[...], qkv_w[:, tile(n)], preferred_element_type=F32
        ).astype(BF16)
        return carry

    lax.fori_loop(0, 9, qkv_step, 0)
    turned[...] = norm_p[...].T
    attend(qkv, probs, att_p)
    for r in range(ROWS):
        cots.wait_recv(r)
    cot_p[...] = jnp.dot(perm, win_c[...], preferred_element_type=F32).astype(BF16)
    pulls[5].wait()

    def gatt_step(n, carry):
        gatt[:, tile(n)] = lax.dot_general(
            cot_p[...], out_w[tile(n), :], NT, preferred_element_type=F32
        ).astype(BF16)
        return carry

    lax.fori_loop(0, 3, gatt_step, 0)

    ring = lambda q, h: (q, pl.ds(2 * h, 2))
    ring_piece = lambda q, h, i: (q, 2 * h + i)
    line = lambda q, h: (q, slice(None), slice(256 * h, 256 + 128 * h))
    line_piece = lambda q, h, i: line(q, h)

    class Chunk:
        def __init__(self, c):
            self.c = c
            self.pair = Whole(agrads.at[c], ar0.at[c], a0s.at[c], a0r.at[c], core, pair)
            six = pl.ds(6 * c, 6)
            self.first = Halve(
                as0.at[c], arx.at[c], axs.at[six], axr.at[six], x, xp, ring, ring_piece, 2
            )
            self.second = Halve(
                as1.at[c], arz.at[c], azs.at[six], azr.at[six], zh, zp, line, line_piece, 1
            )

        def put0(self, q, i, value):
            as0[self.c, q, i] = value

        def put1(self, h, i, value):
            as1[self.c, 2 * h + i] = value.astype(BF16)

        def put2(self, h, i, value):
            atot[self.c, :, 256 * h : 256 + 128 * h] = value

        def step(self, n):
            if n == 0:
                self.pair.start(0)
            elif n == 1:
                self.pair.add(self.put0)
                self.first.start()
            elif n == 2:
                self.first.forward()
            elif n == 3:
                self.first.finish(self.put1)
                self.second.start()
            elif n == 4:
                self.second.forward()
            elif n == 5:
                self.second.finish(self.put2)

        def wait_send(self):
            for one in (self.pair, self.first, self.second):
                one.wait_send()

    chunks = [Chunk(c) for c in range(4)]

    def advance(slot):
        for c in range(4):
            if 0 <= slot - c <= 5:
                chunks[c].step(slot - c)

    turned2[...] = att_p[...].T

    def out_grad_step(n, carry):
        right = jnp.concatenate([cot_p[:, tile(n, 128)], cot_p[:, tile(n + 3, 128)]], axis=1)
        agrads[0, :, :, :, :, tile(n, 128)] = half_rows(
            jnp.dot(turned2[...], right, preferred_element_type=F32)
        )
        return carry

    lax.fori_loop(0, 3, out_grad_step, 0)
    advance(0)
    index = window_place(lax.broadcasted_iota(jnp.int32, (1, WIN), 1))
    tokens = lax.broadcasted_iota(jnp.int32, (TOK, WIN), 0)
    back = (index == tokens).astype(F32).astype(BF16)
    gns = Rows(gn_w, gn, us, ur, dp, sp, False)
    atts = Rows(att_w, att, ts, tr, dp, sp, False)
    att_w[...] = jnp.dot(back, att_p[...], preferred_element_type=F32).astype(BF16)
    for g in range(ROWS):
        atts.start(g)

    def qkv_grad(c):
        def grad_step(n, carry):
            right = gqkv[:, pl.ds(pl.multiple_of(768 * n + 256 * (c - 1), 256), 256)]
            agrads[c, :, :, :, :, tile(n, 128)] = half_rows(
                jnp.dot(turned[...], right, preferred_element_type=F32)
            )
            return carry

        lax.fori_loop(0, 3, grad_step, 0)
        advance(c)

    attend_back(qkv, gatt, probs, gqkv, (0, 1))
    qkv_grad(1)
    attend_back(qkv, gatt, probs, gqkv, (2, 3))
    attend_back(qkv, gatt, probs, gqkv, (4, 5))

    def gn_step(n, carry):
        gn_p[:, tile(n)] = lax.dot_general(
            gqkv[...], qkv_w[tile(n), :], NT, preferred_element_type=F32
        ).astype(BF16)
        return carry

    lax.fori_loop(0, 3, gn_step, 0)
    gn_w[...] = jnp.dot(back, gn_p[...], preferred_element_type=F32).astype(BF16)
    for g in range(ROWS):
        gns.start(g)
    qkv_grad(2)
    qkv_grad(3)
    for r in range(ROWS):
        atts.wait_recv(r)

    def out_step(n, carry):
        part = jnp.dot(att[...], out_w[:, tile(n)], preferred_element_type=F32)
        part = (part + mid[:, tile(n)]).astype(BF16)
        for r in range(ROWS):
            block_o[r, :, tile(n)] = part[PLANE * r : PLANE * r + COLS]
        return carry

    lax.fori_loop(0, C // 256, out_step, 0)

    for r in range(ROWS):
        gns.wait_recv(r)

    def norm_step(r, carry):
        here = tile(r, PLANE)
        hat, inv = normal(mid[here, :])
        grad = gn[here, :].astype(F32)
        grad_hat = grad * scale
        carry = carry + (grad * hat).reshape(8, 8, C).sum(axis=0)
        inner = jnp.mean(grad_hat * hat, axis=1, keepdims=True)
        mean = jnp.mean(grad_hat, axis=1, keepdims=True)
        cotangent = padded(cot[r].astype(F32))
        low = (cotangent + inv * (grad_hat - mean - hat * inner)).astype(BF16)
        ig[here, :] = low
        input_o[r] = low[0:COLS]
        return carry

    gain_part = lax.fori_loop(0, ROWS, norm_step, jnp.zeros((8, C), F32))
    gain_part = jnp.sum(gain_part, axis=0, keepdims=True)
    advance(4)

    ppair = Pair(pgrads, pr0, p0s, p0r, core, pair)
    ends = lambda width: (
        lambda q, h: (q, slice(None), slice(width * h, width * (h + 1))),
        lambda q, h, i: (q, slice(None), slice(width * h, width * (h + 1))),
    )
    px = Halve(ps0, prx, pxs, pxr, x, xp, ring, ring_piece, 2)
    pz = Halve(ps1, prz, pzs, pzr, zh, zp, *ends(256), 1)
    qz = Halve(qs0, qrz, qzs, qzr, zh, zp, ring, ring_piece, 2)
    qx = Halve(qs1, qrx, qxs, qxr, x, xp, *ends(128), 1)

    def put_p0(q, i, value):
        ps0[q, i] = value[:, 0:512]
        qs0[i, q] = value[:, 512:768]

    def put_ps1(h, i, value):
        ps1[2 * h + i] = value.astype(BF16)

    def put_qs1(h, i, value):
        qs1[2 * h + i] = value.astype(BF16)

    def put_p2(h, i, value):
        ptot[:, 256 * h : 256 * (h + 1)] = value

    def put_q2(h, i, value):
        ptot[:, 512 + 128 * h : 512 + 128 * (h + 1)] = value

    for m in XORS:
        xx = flip(x, m)
        turned2[0:384, 0:TOK] = act[:, pl.ds(pl.multiple_of(xx * 384, 128), 384)].T

        def proj_step(n, carry, xx=xx):
            part = jnp.dot(turned2[0:384, 0:TOK], ig[:, tile(n)], preferred_element_type=F32)
            pgrads[xx, :, :, :, tile(n)] = part.reshape(4, 2, 48, 256).astype(BF16)
            return carry

        lax.fori_loop(0, 3, proj_step, 0)
        ppair.start(xx)

    for m in XORS:
        ppair.add(flip(x, m), put_p0)
    px.start()
    qz.start()
    advance(5)

    def act_step(n, carry):
        part = lax.dot_general(ig[...], proj_w[tile(n), :], NT, preferred_element_type=F32)
        gc[:, tile(n)] = (part * slope[:, tile(n)]).astype(BF16)
        return carry

    lax.fori_loop(0, E // 256, act_step, 0)
    edge2 = Halo(gc.at[0:PLANE], gc.at[TOK - PLANE : TOK], edges, es, er, dp, sp)
    edge2.start()
    depth_sums(gc, halo, hidden, depth)

    for n in range(12):
        small[n] = depth[0:8, 128 * n : 128 * (n + 1)]
        small[12 + n // 8, n % 8 : n % 8 + 1, :] = depth[8:9, 128 * n : 128 * (n + 1)]
    for n in range(6):
        small[13 + (4 + n) // 8, (4 + n) % 8 : (4 + n) % 8 + 1, :] = gain_part[:, 128 * n : 128 * (n + 1)]
    small[14, 2:8, :] = jnp.zeros((6, 128), F32)
    small[15] = jnp.zeros((8, 128), F32)
    shifts = [(i, j) for i in range(4) for j in range(4)][1:]

    def spot(i, j):
        return lax.rem(x + i, 4) * 4 + lax.rem(zh + j, 4)

    mine = x * 4 + zh
    scatter = Fan(lambda n: small.at[spot(*shifts[n])], lambda n: srecv.at[n], d0s, d0r, plane16)
    spread = Fan(lambda n: ssum, lambda n: sall.at[n], d1s, d1r, others)
    collect = Fan(lambda n: sfinal.at[mine], lambda n: sfinal.at[mine], d2s, d2r, plane16)
    scatter.start()
    px.forward()
    qz.forward()
    advance(6)
    edge2.wait_recv()
    conv_backward(gc, edges, taps, hidden_o, 0, 6)
    scatter.wait_recv()
    total = small[mine]
    for n in range(15):
        total = total + srecv[n]
    ssum[...] = total
    spread.start()
    px.finish(put_ps1)
    pz.start()
    qz.finish(put_qs1)
    qx.start()
    advance(7)
    conv_backward(gc, edges, taps, hidden_o, 6, 12)
    spread.wait_recv()
    total = ssum[...]
    for n in range(15):
        total = total + sall[n]
    sfinal[mine] = total
    collect.start()
    pz.forward()
    qx.forward()
    advance(8)
    for hh in range(2):
        rows = slice(24 * hh, 24 * (hh + 1))
        arow[:, 2304 + 384 * hh : 2304 + 384 * (hh + 1)] = atot[0, rows, :]
        for c in range(1, 4):
            for part in range(3):
                begin = C * part + 256 * (c - 1) + 128 * hh
                arow[:, begin : begin + 128] = atot[c, rows, 128 * part : 128 * (part + 1)]
    blank = jnp.zeros((8, 384), F32)
    for j in range(8):
        left = arow[:, 288 * j : 288 * (j + 1)]
        right = arow[:, 2304 + 96 * j : 2304 + 96 * (j + 1)]
        value = jnp.concatenate([jnp.concatenate([left, right], axis=1), blank], axis=0)
        atile[j] = value.astype(BF16)
    alast = Fan(lambda n: atile.at[lax.rem(sp + n + 1, 8)], lambda n: arecv.at[n], als, alr, sps)
    alast.start()
    qx.finish(put_q2)
    pz.finish(put_p2)
    for j in range(8):
        ptile[j, :, 0:96] = ptot[:, 96 * j : 96 * (j + 1)].astype(BF16)
    plast = Fan(lambda n: ptile.at[lax.rem(sp + n + 1, 8)], lambda n: precv.at[n], pls, plr, sps)
    plast.start()
    alast.wait_recv()
    total = atile[sp].astype(F32)
    for n in range(7):
        total = total + arecv[n].astype(F32)
    qkv_o[...] = total[0:24, 0:288]
    out_o[...] = total[0:24, 288:384]
    collect.wait_recv()
    for n in range(12):
        depth_o[0:8, 128 * n : 128 * (n + 1)] = sfinal[n]
        depth_o[8:9, 128 * n : 128 * (n + 1)] = sfinal[12 + n // 8, n % 8 : n % 8 + 1, :]
    gains = [sfinal[13 + (4 + n) // 8, (4 + n) % 8 : (4 + n) % 8 + 1, :] for n in range(6)]
    gain_o[...] = jnp.concatenate(gains, axis=1).reshape(C)
    plast.wait_recv()
    total = ptile[sp].astype(F32)
    for n in range(7):
        total = total + precv[n].astype(F32)
    proj_o[...] = total[:, 0:96]
    for g in range(ROWS):
        for rows in (cots, norms, gns, atts):
            rows.wait_send(g)
    for one in [edge, edge2, ppair, px, pz, qx, qz, scatter, spread, collect, plast, alast] + chunks:
        one.wait_send()


VM = pl.BlockSpec(memory_space=pltpu.VMEM)
ANY = pl.BlockSpec(memory_space=pl.ANY)
DMA = pltpu.SemaphoreType.DMA
MIB = 1024 * 1024


def shape(dims, dtype=BF16):
    return jax.ShapeDtypeStruct(dims, dtype)


def low(*dims):
    return pltpu.VMEM(dims, BF16)


def full(*dims):
    return pltpu.VMEM(dims, F32)


def local(block, hidden, cot, depth_w, proj_w, gain, qkv_w, out_w):
    scratch = [low(ROWS, COLS, C), low(ROWS, COLS, E), low(ROWS, COLS, C), low(E, C), low(C, 3 * C), low(C, C), DMA((6,))]
    scratch += [low(2, COLS, E), full(16, E)] + [low(TOK, C)] * 4 + [full(TOK, C), low(TOK, E), full(TOK, E)]
    scratch += [low(WIN, C), low(WIN, C), low(WIN, 3 * C), low(WIN, C), low(WIN, C), low(WIN, 3 * C), low(C, WIN), low(C, WIN), low(WIN, C)]
    scratch += [full(6, WIN, 256)]
    scratch += [low(TOK, C)] * 5 + [low(TOK, E), low(2, PLANE, E), full(16, E)]
    scratch += [
        low(4, 4, 4, 2, 48, 384), low(4, 4, 4, 48, 384), low(4, 4, 4, 48, 384), low(4, 3, 4, 48, 384),
        low(4, 4, 48, 384), low(4, 3, 48, 384), full(4, 48, 384), full(24, 4 * C), low(8, 32, 384), low(7, 32, 384),
    ]
    scratch += [
        low(4, 4, 2, 48, C), low(4, 4, 48, C), low(4, 4, 48, 512), low(3, 4, 48, 512), low(4, 48, 512), low(3, 48, 512),
        low(4, 4, 48, 256), low(3, 4, 48, 256), low(4, 48, 256), low(3, 48, 256),
        full(48, C), low(8, 48, 128), low(7, 48, 128),
    ]
    scratch += [full(16, 8, 128), full(15, 8, 128), full(8, 128), full(15, 8, 128), full(16, 8, 128)]
    counts = [2, 2, 7, 7, 7, 7, 7, 7, 7, 7, 2, 2]
    counts += [4, 4, 24, 24, 24, 24, 7, 7]
    counts += [4, 4, 6, 6, 6, 6, 6, 6, 6, 6, 7, 7]
    counts += [15] * 6
    scratch += [DMA((n,)) for n in counts]
    shapes = (
        shape((ROWS, COLS, C)), shape((ROWS, COLS, C)), shape((ROWS, COLS, E)),
        shape((9, E), F32), shape((C,), F32),
        shape((48, 96), F32), shape((24, 288), F32), shape((24, 96), F32),
    )
    outs = pl.pallas_call(
        section_kernel,
        out_shape=shapes,
        in_specs=[ANY] * 6 + [VM] * 2,
        out_specs=(VM,) * 8,
        scratch_shapes=scratch,
        compiler_params=pltpu.CompilerParams(
            collective_id=1, has_side_effects=True, vmem_limit_bytes=63 * MIB
        ),
        name="section",
    )(block[0], hidden[0], cot[0], proj_w, qkv_w, out_w, depth_w, gain)
    outs = pl.pallas_call(
        settle_kernel,
        out_shape=shapes,
        in_specs=[VM] * 8,
        out_specs=(VM,) * 8,
        name="settle",
    )(*outs)
    return tuple(one[None] for one in outs[:3]) + tuple(outs[3:])


def solution(mesh):
    slab = P("dp", "space", None, None)
    part = P("dp", "space")
    return jax.shard_map(
        local,
        mesh=mesh,
        in_specs=(slab, slab, slab, P(), P(), P(), P(), P()),
        out_specs=(slab, slab, slab, P(), P(), part, part, part),
        check_vma=False,
    )
```

```python
import jax
import jax.numpy as jnp
from jax import lax
from jax.experimental import pallas as pl
from jax.experimental.pallas import tpu as pltpu
from jax.sharding import PartitionSpec as P

MESH = pl.DeviceIdType.MESH
F32, BF16 = jnp.float32, jnp.bfloat16
EPS = 1e-05
C, E, HEADS, HD = 768, 1536, 24, 32
ROWS, COLS, PLANE = 7, 56, 64
TOK = ROWS * PLANE
WIN = 512
SCALE = HD ** (-0.5)
XORS = (2, 1, 3, 0)
NT = (((1,), (1,)), ((), ()))
TN = (((0,), (0,)), ((), ()))


def place():
    dp, sp = lax.axis_index("dp"), lax.axis_index("space")
    return dp, sp, lax.div(dp, 8), lax.rem(lax.div(dp, 2), 4), lax.rem(dp, 2)


def dp_of(x, zh, core):
    return (x * 4 + zh) * 2 + core


def greet(ids):
    barrier = pltpu.get_barrier_semaphore()
    for one in ids:
        pl.semaphore_signal(barrier, inc=1, device_id=one, device_id_type=MESH)
    pl.semaphore_wait(barrier, len(ids))


def remote(src, dst, send, recv, to):
    return pltpu.make_async_remote_copy(
        src_ref=src, dst_ref=dst, send_sem=send, recv_sem=recv, device_id=to, device_id_type=MESH
    )


def planes(ref, n):
    return ref.at[pl.ds(pl.multiple_of(n * PLANE, PLANE), PLANE)]


class Rows:
    def __init__(self, src, dst, ssem, rsem, dp, sp, out):
        self.src, self.dst, self.ssem, self.rsem = src, dst, ssem, rsem
        self.dp, self.sp, self.out = dp, sp, out

    def target(self, n):
        if self.out:
            row = self.sp * 7 + n
            return lax.rem(row, 8), lax.div(row, 8)
        row = n * 8 + self.sp
        return lax.div(row, 7), lax.rem(row, 7)

    def copies(self, n):
        to, slot = self.target(n)
        src, dst = planes(self.src, n), planes(self.dst, slot)
        far = remote(src, dst, self.ssem.at[n], self.rsem.at[slot], (self.dp, to))
        near = pltpu.make_async_copy(src, dst, self.rsem.at[slot])
        return to, far, near

    def start(self, n):
        to, far, near = self.copies(n)

        @pl.when(to != self.sp)
        def _():
            far.start()

        @pl.when(to == self.sp)
        def _():
            near.start()

    def wait_recv(self, n):
        one = planes(self.dst, n)
        pltpu.make_async_copy(one, one, self.rsem.at[n]).wait()

    def wait_send(self, n):
        to, far, _ = self.copies(n)

        @pl.when(to != self.sp)
        def _():
            far.wait_send()


class Halo:
    def __init__(self, top, bottom, halo, ssem, rsem, dp, sp):
        self.sp = sp
        self.up = remote(top, halo.at[1], ssem.at[0], rsem.at[1], (dp, jnp.maximum(sp - 1, 0)))
        self.down = remote(bottom, halo.at[0], ssem.at[1], rsem.at[0], (dp, jnp.minimum(sp + 1, 7)))
        self.halo = halo

    def start(self):
        @pl.when(self.sp > 0)
        def _():
            self.up.start()

        @pl.when(self.sp < 7)
        def _():
            self.down.start()

        zero = jnp.zeros(self.halo.shape[1:], self.halo.dtype)

        @pl.when(self.sp == 0)
        def _():
            self.halo[0] = zero

        @pl.when(self.sp == 7)
        def _():
            self.halo[1] = zero

    def wait_recv(self):
        @pl.when(self.sp > 0)
        def _():
            self.down.wait_recv()

        @pl.when(self.sp < 7)
        def _():
            self.up.wait_recv()

    def wait_send(self):
        @pl.when(self.sp > 0)
        def _():
            self.up.wait_send()

        @pl.when(self.sp < 7)
        def _():
            self.down.wait_send()


def col_masks(lanes):
    index = lax.broadcasted_iota(jnp.int32, (COLS, lanes), 0)
    return index == 0, index == COLS - 1


def later(value, first):
    return jnp.where(first, 0.0, pltpu.roll(value, 1, 0))


def earlier(value, last):
    return jnp.where(last, 0.0, pltpu.roll(value, COLS - 1, 0))


def padded(value):
    return jnp.concatenate([value, jnp.zeros((PLANE - COLS, value.shape[1]), F32)], axis=0)


def gelu_and_slope(value):
    k0, k1 = 0.7978845608028654, 0.044715
    square = value * value
    tanh = jnp.tanh(k0 * value * (1.0 + k1 * square))
    half = 0.5 * (1.0 + tanh)
    slope = half + 0.5 * value * (1.0 - tanh * tanh) * (k0 * (1.0 + 3.0 * k1 * square))
    return value * half, slope


def conv_forward(hidden, halo, taps, act, slope, begin, end):
    def chunk(n, carry):
        lanes = pl.ds(pl.multiple_of(n * 128, 128), 128)
        first, last = col_masks(128)
        rows = {}
        for r in range(begin - 1, end + 1):
            if r < 0:
                rows[r] = halo[0, :, lanes].astype(F32)
            elif r == ROWS:
                rows[r] = halo[1, :, lanes].astype(F32)
            else:
                rows[r] = hidden[r, :, lanes].astype(F32)
        tap = [taps[t : t + 1, lanes] for t in range(9)]
        for r in range(begin, end):
            part = [sum(tap[3 * a + b] * rows[r + a - 1] for a in range(3)) for b in range(3)]
            conv = later(part[0], first) + part[1] + earlier(part[2], last)
            low, grad = gelu_and_slope(conv)
            act[PLANE * r : PLANE * (r + 1), lanes] = padded(low).astype(BF16)
            slope[PLANE * r : PLANE * (r + 1), lanes] = padded(grad)
        return carry

    lax.fori_loop(0, E // 128, chunk, 0)


def normal(mid):
    mean = jnp.mean(mid, axis=1, keepdims=True)
    centred = mid - mean
    inv = lax.rsqrt(jnp.mean(centred * centred, axis=1, keepdims=True) + EPS)
    return centred * inv, inv


def window_place(index):
    win, n = index >> 6, index & 63
    g = (n * 37) >> 8
    return jnp.where(n < 49, g * PLANE + (n - 7 * g) * 8 + win, -1)


def head_tools():
    lane = lax.broadcasted_iota(jnp.int32, (64, 128), 1) >> 5
    big = lax.broadcasted_iota(jnp.int32, (256, 128), 0) >> 6
    own = (big == (lax.broadcasted_iota(jnp.int32, (256, 128), 1) >> 5)).astype(F32).astype(BF16)

    def spread(value):
        return jnp.concatenate([value] * 4, axis=0) * own

    def gather(value):
        return jnp.where(
            lane < 2,
            jnp.where(lane == 0, value[0:64], value[64:128]),
            jnp.where(lane == 2, value[128:192], value[192:256]),
        )

    return spread, gather


def heads(part, g):
    return slice(part * C + 128 * g, part * C + 128 * (g + 1))


def attend(qkv, probs, att):
    spread, gather = head_tools()
    valid = lax.broadcasted_iota(jnp.int32, (64, 256), 0) < 49

    def window(w, carry):
        rows = pl.ds(pl.multiple_of(w * 64, 64), 64)
        for g in range(6):
            query, key, value = (qkv[rows, heads(part, g)] for part in range(3))
            score = lax.dot_general(key, spread(query), NT, preferred_element_type=F32) * SCALE
            score = jnp.where(valid, score, -1e30)
            power = jnp.exp(score - jnp.max(score, axis=0, keepdims=True))
            prob = power * (1.0 / jnp.sum(power, axis=0, keepdims=True))
            probs[g, rows] = prob
            att[rows, heads(0, g)] = gather(
                lax.dot_general(prob.astype(BF16), value, TN, preferred_element_type=F32)
            ).astype(BF16)
        return carry

    lax.fori_loop(0, 8, window, 0)


def attend_back(qkv, gatt, probs, gqkv, groups):
    spread, gather = head_tools()

    def window(pair, carry):
        for w in range(4):
            rows = pl.ds(pl.multiple_of(pair * 256 + 64 * w, 64), 64)
            for g in groups:
                query, key, value = (qkv[rows, heads(part, g)] for part in range(3))
                query = spread(query)
                grad = spread(gatt[rows, heads(0, g)])
                prob = probs[g, rows]
                low = prob.astype(BF16)
                grad_prob = lax.dot_general(value, grad, NT, preferred_element_type=F32)
                inner = jnp.sum(grad_prob * prob, axis=0, keepdims=True)
                grad_low = (prob * (grad_prob - inner) * SCALE).astype(BF16)
                gqkv[rows, heads(0, g)] = gather(
                    lax.dot_general(grad_low, key, TN, preferred_element_type=F32)
                ).astype(BF16)
                gqkv[rows, heads(1, g)] = jnp.dot(
                    grad_low, query, preferred_element_type=F32
                ).astype(BF16)
                gqkv[rows, heads(2, g)] = jnp.dot(low, grad, preferred_element_type=F32).astype(BF16)
        return carry

    lax.fori_loop(0, 2, window, 0)


def half_rows(value):
    left, right = (value[:, 128 * h : 128 * (h + 1)].reshape(32, 24, 128) for h in range(2))
    return jnp.concatenate([left, right], axis=1).reshape(4, 4, 2, 48, 128).astype(BF16)


def flip(q, mask):
    if mask == 0:
        return q
    if mask == 1:
        return q + 1 - 2 * lax.rem(q, 2)
    if mask == 3:
        return 3 - q
    return lax.rem(q + 2, 4)


class Pair:
    def __init__(self, grads, recv, ssem, rsem, core, peer):
        self.grads, self.recv, self.core = grads, recv, core
        self.ssem, self.rsem, self.peer = ssem, rsem, peer
        self.begun = []

    def copy(self, q):
        return remote(
            self.grads.at[q, :, 1 - self.core], self.recv.at[q], self.ssem.at[q], self.rsem.at[q], self.peer
        )

    def start(self, q):
        self.copy(q).start()

    def add(self, q, put):
        self.copy(q).wait_recv()

        def body(i, carry):
            mine = self.grads[q, i, self.core].astype(F32)
            put(q, i, (mine + self.recv[q, i].astype(F32)).astype(BF16))
            return carry

        lax.fori_loop(0, 4, body, 0)

    def wait_send(self):
        for q in range(4):
            self.copy(q).wait_send()


class Whole(Pair):
    def copy(self, q=0):
        return remote(self.grads.at[:, :, 1 - self.core], self.recv, self.ssem, self.rsem, self.peer)

    def add(self, put):
        self.copy().wait_recv()

        def body(i, carry):
            q, j = lax.div(i, 4), lax.rem(i, 4)
            mine = self.grads[q, j, self.core].astype(F32)
            put(q, j, (mine + self.recv[q, j].astype(F32)).astype(BF16))
            return carry

        lax.fori_loop(0, 16, body, 0)

    def wait_send(self):
        self.copy().wait_send()


class Halve:
    def __init__(self, src, recv, ssem, rsem, q, peers, view, piece, count):
        self.src, self.recv, self.q, self.view, self.piece, self.count = src, recv, q, view, piece, count
        self.cps = {}
        for h in range(2):
            near, far = (1, 3) if h == 0 else (3, 1)
            for slot, (block, to) in enumerate(((near, near), (2, near), (far, far))):
                n = 3 * h + slot
                self.cps[h, slot] = remote(
                    src.at[view(flip(q, block), h)], recv.at[view(slot, h)], ssem.at[n], rsem.at[n], peers[to]
                )

    def start(self):
        for slot in (1, 0):
            for h in range(2):
                self.cps[h, slot].start()

    def forward(self):
        for h in range(2):
            self.cps[h, 1].wait_recv()
            block = flip(self.q, 3 if h == 0 else 1)

            def body(i, carry, h=h, block=block):
                mine = self.src[self.piece(block, h, i)].astype(F32)
                mine = mine + self.recv[self.piece(1, h, i)].astype(F32)
                self.src[self.piece(block, h, i)] = mine.astype(BF16)
                return carry

            lax.fori_loop(0, self.count, body, 0)
            self.cps[h, 2].start()

    def finish(self, put):
        for h in range(2):
            self.cps[h, 0].wait_recv()
            self.cps[h, 2].wait_recv()

            def body(i, carry, h=h):
                mine = self.src[self.piece(self.q, h, i)].astype(F32)
                mine = mine + self.recv[self.piece(0, h, i)].astype(F32)
                put(h, i, mine + self.recv[self.piece(2, h, i)].astype(F32))
                return carry

            lax.fori_loop(0, self.count, body, 0)

    def wait_send(self):
        for cp in self.cps.values():
            cp.wait_send()


class Fan:
    def __init__(self, pieces, recvs, ssem, rsem, peers):
        self.cps = [
            remote(pieces(n), recvs(n), ssem.at[n], rsem.at[n], peer) for n, peer in enumerate(peers)
        ]

    def start(self):
        for cp in self.cps:
            cp.start()

    def wait_recv(self):
        for cp in self.cps:
            cp.wait_recv()

    def wait_send(self):
        for cp in self.cps:
            cp.wait_send()


def depth_sums(grad, halo, hidden, depth):
    def chunk(n, carry):
        lanes = pl.ds(pl.multiple_of(n * 128, 128), 128)
        first, last = col_masks(128)
        rows = [grad[PLANE * r : PLANE * r + COLS, lanes].astype(F32) for r in range(ROWS)]
        sums = [jnp.zeros((8, 128), F32) for _ in range(9)]
        for r in range(-1, ROWS + 1):
            if r < 0:
                own = halo[0, :, lanes].astype(F32)
            elif r == ROWS:
                own = halo[1, :, lanes].astype(F32)
            else:
                own = hidden[r, :, lanes].astype(F32)
            moved = [later(own, first), own, earlier(own, last)]
            for a in range(3):
                if 0 <= r + 1 - a < ROWS:
                    for b in range(3):
                        product = moved[b] * rows[r + 1 - a]
                        for i in range(7):
                            sums[3 * a + b] = sums[3 * a + b] + product[8 * i : 8 * i + 8]
        for t in range(9):
            depth[t : t + 1, lanes] = jnp.sum(sums[t], axis=0, keepdims=True)
        return carry

    lax.fori_loop(0, E // 128, chunk, 0)


def conv_backward(grad, halo, taps, hidden_grad, begin, end):
    def chunk(n, carry):
        lanes = pl.ds(pl.multiple_of(n * 128, 128), 128)
        first, last = col_masks(128)
        rows = [halo[0, 0:COLS, lanes].astype(F32)]
        rows += [grad[PLANE * r : PLANE * r + COLS, lanes].astype(F32) for r in range(ROWS)]
        rows += [halo[1, 0:COLS, lanes].astype(F32)]
        tap = [taps[t : t + 1, lanes] for t in range(9)]
        for r in range(ROWS):
            part = [sum(tap[3 * a + b] * rows[r + 2 - a] for a in range(3)) for b in range(3)]
            total = earlier(part[0], last) + part[1] + later(part[2], first)
            hidden_grad[r, :, lanes] = total.astype(BF16)
        return carry

    lax.fori_loop(begin, end, chunk, 0)


def settle_kernel(*refs):
    count = len(refs) // 2
    for n in range(count):
        refs[count + n][...] = refs[n][...]


def tile(n, width=256):
    return pl.ds(pl.multiple_of(n * width, width), width)


def section_kernel(
    block_h, hidden_h, cot_h, proj_h, qkv_h, out_h, depth_w, gain,
    block_o, input_o, hidden_o, depth_o, gain_o, proj_o, qkv_o, out_o,
    block, hidden, cot, proj_w, qkv_w, out_w, loads,
    halo, taps, own_n, own_c, win_n, win_c, mid, act, slope,
    norm_p, cot_p, qkv, gatt, att_p, gqkv, turned, turned2, gn_p, probs,
    att_w, gn_w, att, gn, ig, gc, edges, depth,
    agrads, ar0, as0, arx, as1, arz, atot, arow, atile, arecv,
    pgrads, pr0, ps0, prx, ps1, prz, qs0, qrz, qs1, qrx, ptot, ptile, precv,
    small, srecv, ssum, sall, sfinal,
    hs, hr, ns, nr, cs, cr, ts, tr, us, ur, es, er,
    a0s, a0r, axs, axr, azs, azr, als, alr,
    p0s, p0r, pxs, pxr, pzs, pzr, qzs, qzr, qxs, qxr, pls, plr,
    d0s, d0r, d1s, d1r, d2s, d2r,
):
    dp, sp, x, zh, core = place()
    pulls = {}
    pairs = ((hidden_h, hidden), (proj_h, proj_w), (block_h, block), (cot_h, cot), (qkv_h, qkv_w), (out_h, out_w))
    for n, (src, dst) in enumerate(pairs):
        pulls[n] = pltpu.make_async_copy(src, dst, loads.at[n])
        pulls[n].start()
    pair = (dp_of(x, zh, 1 - core), sp)
    plane16 = [(dp_of(lax.rem(x + i, 4), lax.rem(zh + j, 4), core), sp) for i in range(4) for j in range(4)][1:]
    sps = [(dp, lax.rem(sp + j, 8)) for j in range(1, 8)]
    others = sps + [(dp_of(x, zh, 1 - core), lax.rem(sp + j, 8)) for j in range(8)]
    greet(plane16 + others)
    xp = {m: (dp_of(flip(x, m), zh, core), sp) for m in (1, 3)}
    zp = {m: (dp_of(x, flip(zh, m), core), sp) for m in (1, 3)}

    edge = Halo(hidden_h.at[0], hidden_h.at[ROWS - 1], halo, hs, hr, dp, sp)
    edge.start()
    cots = Rows(own_c, win_c, cs, cr, dp, sp, True)
    norms = Rows(own_n, win_n, ns, nr, dp, sp, True)
    taps[0:9] = depth_w[...].astype(F32)
    scale = gain[...].reshape(1, C)

    def norm(r):
        here = tile(r, PLANE)
        total = mid[here, :] + padded(block[r].astype(F32))
        mid[here, :] = total
        own_n[here, :] = (normal(total)[0] * scale).astype(BF16)
        norms.start(r)

    def norm_inner(r, carry):
        norm(r)
        return carry

    def norm_outer(i, carry):
        norm(lax.rem(i + 5, 7))
        return carry

    def proj_inner(n, carry):
        mid[64:320, tile(n)] = jnp.dot(act[64:320, :], proj_w[:, tile(n)], preferred_element_type=F32)
        return carry

    def proj_outer(n, carry):
        left = jnp.concatenate([act[0:64, :], act[320:448, :]], axis=0)
        part = jnp.dot(left, proj_w[:, tile(n)], preferred_element_type=F32)
        mid[0:64, tile(n)] = part[0:64]
        mid[320:448, tile(n)] = part[64:192]
        return carry

    pulls[0].wait()
    conv_forward(hidden, halo, taps, act, slope, 1, 5)
    pulls[1].wait()
    lax.fori_loop(0, C // 256, proj_inner, 0)
    pulls[2].wait()
    lax.fori_loop(1, 5, norm_inner, 0)
    edge.wait_recv()
    conv_forward(hidden, halo, taps, act, slope, 5, 7)
    conv_forward(hidden, halo, taps, act, slope, 0, 1)
    lax.fori_loop(0, C // 256, proj_outer, 0)
    lax.fori_loop(0, 3, norm_outer, 0)
    pulls[3].wait()
    for r in range(ROWS):
        own_c[PLANE * r : PLANE * (r + 1)] = padded(cot[r].astype(F32)).astype(BF16)
        cots.start(r)

    index = window_place(lax.broadcasted_iota(jnp.int32, (WIN, 1), 0))
    tokens = lax.broadcasted_iota(jnp.int32, (WIN, TOK), 1)
    perm = (index == tokens).astype(F32).astype(BF16)
    for r in range(ROWS):
        norms.wait_recv(r)
    norm_p[...] = jnp.dot(perm, win_n[...], preferred_element_type=F32).astype(BF16)
    pulls[4].wait()

    def qkv_step(n, carry):
        qkv[:, tile(n)] = jnp.dot(
            norm_p[...], qkv_w[:, tile(n)], preferred_element_type=F32
        ).astype(BF16)
        return carry

    lax.fori_loop(0, 9, qkv_step, 0)
    turned[...] = norm_p[...].T
    attend(qkv, probs, att_p)
    for r in range(ROWS):
        cots.wait_recv(r)
    cot_p[...] = jnp.dot(perm, win_c[...], preferred_element_type=F32).astype(BF16)
    pulls[5].wait()

    def gatt_step(n, carry):
        gatt[:, tile(n)] = lax.dot_general(
            cot_p[...], out_w[tile(n), :], NT, preferred_element_type=F32
        ).astype(BF16)
        return carry

    lax.fori_loop(0, 3, gatt_step, 0)

    ring = lambda q, h: (q, pl.ds(2 * h, 2))
    ring_piece = lambda q, h, i: (q, 2 * h + i)
    line = lambda q, h: (q, slice(None), slice(256 * h, 256 + 128 * h))
    line_piece = lambda q, h, i: line(q, h)

    class Chunk:
        def __init__(self, c):
            self.c = c
            self.pair = Whole(agrads.at[c], ar0.at[c], a0s.at[c], a0r.at[c], core, pair)
            six = pl.ds(6 * c, 6)
            self.first = Halve(
                as0.at[c], arx.at[c], axs.at[six], axr.at[six], x, xp, ring, ring_piece, 2
            )
            self.second = Halve(
                as1.at[c], arz.at[c], azs.at[six], azr.at[six], zh, zp, line, line_piece, 1
            )

        def put0(self, q, i, value):
            as0[self.c, q, i] = value

        def put1(self, h, i, value):
            as1[self.c, 2 * h + i] = value.astype(BF16)

        def put2(self, h, i, value):
            atot[self.c, :, 256 * h : 256 + 128 * h] = value

        def step(self, n):
            if n == 0:
                self.pair.start(0)
            elif n == 1:
                self.pair.add(self.put0)
                self.first.start()
            elif n == 2:
                self.first.forward()
            elif n == 3:
                self.first.finish(self.put1)
                self.second.start()
            elif n == 4:
                self.second.forward()
            elif n == 5:
                self.second.finish(self.put2)

        def wait_send(self):
            for one in (self.pair, self.first, self.second):
                one.wait_send()

    chunks = [Chunk(c) for c in range(4)]

    def advance(slot):
        for c in range(4):
            if 0 <= slot - c <= 5:
                chunks[c].step(slot - c)

    turned2[...] = att_p[...].T

    def out_grad_step(n, carry):
        right = jnp.concatenate([cot_p[:, tile(n, 128)], cot_p[:, tile(n + 3, 128)]], axis=1)
        agrads[0, :, :, :, :, tile(n, 128)] = half_rows(
            jnp.dot(turned2[...], right, preferred_element_type=F32)
        )
        return carry

    lax.fori_loop(0, 3, out_grad_step, 0)
    advance(0)
    index = window_place(lax.broadcasted_iota(jnp.int32, (1, WIN), 1))
    tokens = lax.broadcasted_iota(jnp.int32, (TOK, WIN), 0)
    back = (index == tokens).astype(F32).astype(BF16)
    gns = Rows(gn_w, gn, us, ur, dp, sp, False)
    atts = Rows(att_w, att, ts, tr, dp, sp, False)
    att_w[...] = jnp.dot(back, att_p[...], preferred_element_type=F32).astype(BF16)
    for g in range(ROWS):
        atts.start(g)

    def qkv_grad(c):
        def grad_step(n, carry):
            right = gqkv[:, pl.ds(pl.multiple_of(768 * n + 256 * (c - 1), 256), 256)]
            agrads[c, :, :, :, :, tile(n, 128)] = half_rows(
                jnp.dot(turned[...], right, preferred_element_type=F32)
            )
            return carry

        lax.fori_loop(0, 3, grad_step, 0)
        advance(c)

    attend_back(qkv, gatt, probs, gqkv, (0, 1))
    qkv_grad(1)
    attend_back(qkv, gatt, probs, gqkv, (2, 3))
    attend_back(qkv, gatt, probs, gqkv, (4, 5))

    def gn_step(n, carry):
        gn_p[:, tile(n)] = lax.dot_general(
            gqkv[...], qkv_w[tile(n), :], NT, preferred_element_type=F32
        ).astype(BF16)
        return carry

    lax.fori_loop(0, 3, gn_step, 0)
    gn_w[...] = jnp.dot(back, gn_p[...], preferred_element_type=F32).astype(BF16)
    for g in range(ROWS):
        gns.start(g)
    qkv_grad(2)
    qkv_grad(3)
    for r in range(ROWS):
        atts.wait_recv(r)

    def out_step(n, carry):
        part = jnp.dot(att[...], out_w[:, tile(n)], preferred_element_type=F32)
        part = (part + mid[:, tile(n)]).astype(BF16)
        for r in range(ROWS):
            block_o[r, :, tile(n)] = part[PLANE * r : PLANE * r + COLS]
        return carry

    lax.fori_loop(0, C // 256, out_step, 0)

    for r in range(ROWS):
        gns.wait_recv(r)

    def norm_step(r, carry):
        here = tile(r, PLANE)
        hat, inv = normal(mid[here, :])
        grad = gn[here, :].astype(F32)
        grad_hat = grad * scale
        carry = carry + (grad * hat).reshape(8, 8, C).sum(axis=0)
        inner = jnp.mean(grad_hat * hat, axis=1, keepdims=True)
        mean = jnp.mean(grad_hat, axis=1, keepdims=True)
        cotangent = padded(cot[r].astype(F32))
        low = (cotangent + inv * (grad_hat - mean - hat * inner)).astype(BF16)
        ig[here, :] = low
        input_o[r] = low[0:COLS]
        return carry

    gain_part = lax.fori_loop(0, ROWS, norm_step, jnp.zeros((8, C), F32))
    gain_part = jnp.sum(gain_part, axis=0, keepdims=True)
    advance(4)

    ppair = Pair(pgrads, pr0, p0s, p0r, core, pair)
    ends = lambda width: (
        lambda q, h: (q, slice(None), slice(width * h, width * (h + 1))),
        lambda q, h, i: (q, slice(None), slice(width * h, width * (h + 1))),
    )
    px = Halve(ps0, prx, pxs, pxr, x, xp, ring, ring_piece, 2)
    pz = Halve(ps1, prz, pzs, pzr, zh, zp, *ends(256), 1)
    qz = Halve(qs0, qrz, qzs, qzr, zh, zp, ring, ring_piece, 2)
    qx = Halve(qs1, qrx, qxs, qxr, x, xp, *ends(128), 1)

    def put_p0(q, i, value):
        ps0[q, i] = value[:, 0:512]
        qs0[i, q] = value[:, 512:768]

    def put_ps1(h, i, value):
        ps1[2 * h + i] = value.astype(BF16)

    def put_qs1(h, i, value):
        qs1[2 * h + i] = value.astype(BF16)

    def put_p2(h, i, value):
        ptot[:, 256 * h : 256 * (h + 1)] = value

    def put_q2(h, i, value):
        ptot[:, 512 + 128 * h : 512 + 128 * (h + 1)] = value

    for m in XORS:
        xx = flip(x, m)
        turned2[0:384, 0:TOK] = act[:, pl.ds(pl.multiple_of(xx * 384, 128), 384)].T

        def proj_step(n, carry, xx=xx):
            part = jnp.dot(turned2[0:384, 0:TOK], ig[:, tile(n)], preferred_element_type=F32)
            pgrads[xx, :, :, :, tile(n)] = part.reshape(4, 2, 48, 256).astype(BF16)
            return carry

        lax.fori_loop(0, 3, proj_step, 0)
        ppair.start(xx)

    for m in XORS:
        ppair.add(flip(x, m), put_p0)
    px.start()
    qz.start()
    advance(5)

    def act_step(n, carry):
        part = lax.dot_general(ig[...], proj_w[tile(n), :], NT, preferred_element_type=F32)
        gc[:, tile(n)] = (part * slope[:, tile(n)]).astype(BF16)
        return carry

    lax.fori_loop(0, E // 256, act_step, 0)
    edge2 = Halo(gc.at[0:PLANE], gc.at[TOK - PLANE : TOK], edges, es, er, dp, sp)
    edge2.start()
    depth_sums(gc, halo, hidden, depth)

    for n in range(12):
        small[n] = depth[0:8, 128 * n : 128 * (n + 1)]
        small[12 + n // 8, n % 8 : n % 8 + 1, :] = depth[8:9, 128 * n : 128 * (n + 1)]
    for n in range(6):
        small[13 + (4 + n) // 8, (4 + n) % 8 : (4 + n) % 8 + 1, :] = gain_part[:, 128 * n : 128 * (n + 1)]
    small[14, 2:8, :] = jnp.zeros((6, 128), F32)
    small[15] = jnp.zeros((8, 128), F32)
    shifts = [(i, j) for i in range(4) for j in range(4)][1:]

    def spot(i, j):
        return lax.rem(x + i, 4) * 4 + lax.rem(zh + j, 4)

    mine = x * 4 + zh
    scatter = Fan(lambda n: small.at[spot(*shifts[n])], lambda n: srecv.at[n], d0s, d0r, plane16)
    spread = Fan(lambda n: ssum, lambda n: sall.at[n], d1s, d1r, others)
    collect = Fan(lambda n: sfinal.at[mine], lambda n: sfinal.at[mine], d2s, d2r, plane16)
    scatter.start()
    px.forward()
    qz.forward()
    advance(6)
    edge2.wait_recv()
    conv_backward(gc, edges, taps, hidden_o, 0, 6)
    scatter.wait_recv()
    total = small[mine]
    for n in range(15):
        total = total + srecv[n]
    ssum[...] = total
    spread.start()
    px.finish(put_ps1)
    pz.start()
    qz.finish(put_qs1)
    qx.start()
    advance(7)
    conv_backward(gc, edges, taps, hidden_o, 6, 12)
    spread.wait_recv()
    total = ssum[...]
    for n in range(15):
        total = total + sall[n]
    sfinal[mine] = total
    collect.start()
    pz.forward()
    qx.forward()
    advance(8)
    for hh in range(2):
        rows = slice(24 * hh, 24 * (hh + 1))
        arow[:, 2304 + 384 * hh : 2304 + 384 * (hh + 1)] = atot[0, rows, :]
        for c in range(1, 4):
            for part in range(3):
                begin = C * part + 256 * (c - 1) + 128 * hh
                arow[:, begin : begin + 128] = atot[c, rows, 128 * part : 128 * (part + 1)]
    blank = jnp.zeros((8, 384), F32)
    for j in range(8):
        left = arow[:, 288 * j : 288 * (j + 1)]
        right = arow[:, 2304 + 96 * j : 2304 + 96 * (j + 1)]
        value = jnp.concatenate([jnp.concatenate([left, right], axis=1), blank], axis=0)
        atile[j] = value.astype(BF16)
    alast = Fan(lambda n: atile.at[lax.rem(sp + n + 1, 8)], lambda n: arecv.at[n], als, alr, sps)
    alast.start()
    qx.finish(put_q2)
    pz.finish(put_p2)
    for j in range(8):
        ptile[j, :, 0:96] = ptot[:, 96 * j : 96 * (j + 1)].astype(BF16)
    plast = Fan(lambda n: ptile.at[lax.rem(sp + n + 1, 8)], lambda n: precv.at[n], pls, plr, sps)
    plast.start()
    alast.wait_recv()
    total = atile[sp].astype(F32)
    for n in range(7):
        total = total + arecv[n].astype(F32)
    qkv_o[...] = total[0:24, 0:288]
    out_o[...] = total[0:24, 288:384]
    collect.wait_recv()
    for n in range(12):
        depth_o[0:8, 128 * n : 128 * (n + 1)] = sfinal[n]
        depth_o[8:9, 128 * n : 128 * (n + 1)] = sfinal[12 + n // 8, n % 8 : n % 8 + 1, :]
    gains = [sfinal[13 + (4 + n) // 8, (4 + n) % 8 : (4 + n) % 8 + 1, :] for n in range(6)]
    gain_o[...] = jnp.concatenate(gains, axis=1).reshape(C)
    plast.wait_recv()
    total = ptile[sp].astype(F32)
    for n in range(7):
        total = total + precv[n].astype(F32)
    proj_o[...] = total[:, 0:96]
    for g in range(ROWS):
        for rows in (cots, norms, gns, atts):
            rows.wait_send(g)
    for one in [edge, edge2, ppair, px, pz, qx, qz, scatter, spread, collect, plast, alast] + chunks:
        one.wait_send()


VM = pl.BlockSpec(memory_space=pltpu.VMEM)
ANY = pl.BlockSpec(memory_space=pl.ANY)
DMA = pltpu.SemaphoreType.DMA
MIB = 1024 * 1024


def shape(dims, dtype=BF16):
    return jax.ShapeDtypeStruct(dims, dtype)


def low(*dims):
    return pltpu.VMEM(dims, BF16)


def full(*dims):
    return pltpu.VMEM(dims, F32)


def local(block, hidden, cot, depth_w, proj_w, gain, qkv_w, out_w):
    scratch = [low(ROWS, COLS, C), low(ROWS, COLS, E), low(ROWS, COLS, C), low(E, C), low(C, 3 * C), low(C, C), DMA((6,))]
    scratch += [low(2, COLS, E), full(16, E)] + [low(TOK, C)] * 4 + [full(TOK, C), low(TOK, E), full(TOK, E)]
    scratch += [low(WIN, C), low(WIN, C), low(WIN, 3 * C), low(WIN, C), low(WIN, C), low(WIN, 3 * C), low(C, WIN), low(C, WIN), low(WIN, C)]
    scratch += [full(6, WIN, 256)]
    scratch += [low(TOK, C)] * 5 + [low(TOK, E), low(2, PLANE, E), full(16, E)]
    scratch += [
        low(4, 4, 4, 2, 48, 384), low(4, 4, 4, 48, 384), low(4, 4, 4, 48, 384), low(4, 3, 4, 48, 384),
        low(4, 4, 48, 384), low(4, 3, 48, 384), full(4, 48, 384), full(24, 4 * C), low(8, 32, 384), low(7, 32, 384),
    ]
    scratch += [
        low(4, 4, 2, 48, C), low(4, 4, 48, C), low(4, 4, 48, 512), low(3, 4, 48, 512), low(4, 48, 512), low(3, 48, 512),
        low(4, 4, 48, 256), low(3, 4, 48, 256), low(4, 48, 256), low(3, 48, 256),
        full(48, C), low(8, 48, 128), low(7, 48, 128),
    ]
    scratch += [full(16, 8, 128), full(15, 8, 128), full(8, 128), full(15, 8, 128), full(16, 8, 128)]
    counts = [2, 2, 7, 7, 7, 7, 7, 7, 7, 7, 2, 2]
    counts += [4, 4, 24, 24, 24, 24, 7, 7]
    counts += [4, 4, 6, 6, 6, 6, 6, 6, 6, 6, 7, 7]
    counts += [15] * 6
    scratch += [DMA((n,)) for n in counts]
    shapes = (
        shape((ROWS, COLS, C)), shape((ROWS, COLS, C)), shape((ROWS, COLS, E)),
        shape((9, E), F32), shape((C,), F32),
        shape((48, 96), F32), shape((24, 288), F32), shape((24, 96), F32),
    )
    outs = pl.pallas_call(
        section_kernel,
        out_shape=shapes,
        in_specs=[ANY] * 6 + [VM] * 2,
        out_specs=(VM,) * 8,
        scratch_shapes=scratch,
        compiler_params=pltpu.CompilerParams(
            collective_id=1, has_side_effects=True, vmem_limit_bytes=63 * MIB
        ),
        name="section",
    )(block[0], hidden[0], cot[0], proj_w, qkv_w, out_w, depth_w, gain)
    outs = pl.pallas_call(
        settle_kernel,
        out_shape=shapes,
        in_specs=[VM] * 8,
        out_specs=(VM,) * 8,
        name="settle",
    )(*outs)
    return tuple(one[None] for one in outs[:3]) + tuple(outs[3:])


def solution(mesh):
    slab = P("dp", "space", None, None)
    part = P("dp", "space")
    return jax.shard_map(
        local,
        mesh=mesh,
        in_specs=(slab, slab, slab, P(), P(), P(), P(), P()),
        out_specs=(slab, slab, slab, P(), P(), part, part, part),
        check_vma=False,
    )
```
